32 devices in a mesh: dp: 8 (over z, x), mp: 4 (over y, core).
Axes of the slice: x: 2, y: 2, z: 4, core: 2. Of those that a mesh axis runs over, the one named last changes fastest.
Arguments:
- states: bfloat16 [65536, 2048], P(('dp', 'mp')), may hold values from -6 to 6
- dest_device: int32 [65536, 1], P(('dp', 'mp')), may hold values from 0 to 7; in each aligned block of 2048 rows (0 to 2047, 2048 to 4095, ...) at most 320 rows name the same one
- goals: bfloat16 [81920, 1024], P(('dp', 'mp')), may hold values from -6 to 6
- returns: bfloat16 [81920], P(('dp', 'mp')), may hold values from -9 to 9
- weight_in: bfloat16 [3072, 512], P('mp'), may hold values from -0.109375 to 0.109375
- weight_hidden: bfloat16 [3, 512, 512], P(None, 'mp'), may hold values from -0.25 to 0.25
- norm_gain: bfloat16 [4, 512], P(None, 'mp'), may hold values from 0.5 to 1.5
- norm_shift: bfloat16 [4, 512], P(None, 'mp'), may hold values from -1.5 to 1.5
- weight_out: bfloat16 [512], P('mp'), may hold values from -0.25 to 0.25
Outputs:
- total_loss: float32 [], replicated
- grad_states: bfloat16 [65536, 2048], P(('dp', 'mp'))
- grad_goals: bfloat16 [81920, 1024], P(('dp', 'mp'))
- grad_weight_in: float32 [3072, 512], P(None, ('dp', 'mp'))
- grad_weight_hidden: float32 [3, 512, 512], P(None, None, ('dp', 'mp'))
- grad_norm_gain: float32 [4, 512], P(None, ('dp', 'mp'))
- grad_norm_shift: float32 [4, 512], P(None, ('dp', 'mp'))
- grad_weight_out: float32 [512], P(('dp', 'mp'))
The draws below stay inside these ranges and needn't reach their ends.
Inputs may be any that keep to these rules, and one draw needn't show every extreme that they name: `dest_device`: the 2048 rows of one device name each destination at most 320 times, a bound that some block reaches.
All inputs are finite; a program needn't handle non-finite values.
Results may differ from the reference program's by a relative error of at most 0.019.
Values may be sent and summed in bfloat16 or wider, within the bound.
No kernel may reach another device: no remote copies, remote signals or barrier semaphores. Data moves between devices by JAX's collectives and lax.ppermute only.
A program may use at most 192 MiB of HBM per device.

```python
import math
import jax
import jax.numpy as jnp
import numpy as np
from jax import lax

FEAT = 2048
GOAL = 1024
H = 512
LAYERS = 4
TOK_DEV = 2048
IN = 3072
CAP = 320
ROWS = 65536
SLOTS = 81920
N_DP = 8
N_MP = 4


def draw_returns(key, part):
    ramp = 1.0 + 2.0 * jnp.arange(SLOTS, dtype=jnp.float32) / SLOTS
    normal_part = jnp.clip(jax.random.normal(key, (SLOTS,), jnp.float32), -2.9, 2.9)
    return (normal_part * ramp).astype(jnp.bfloat16)


def level_of(key, extent, pieces, least, top_value):
    factor_of, own = 1.0, jax.random.fold_in(key, 6)
    for dim, parts in pieces:
        draws = jnp.exp(jax.random.uniform(jax.random.fold_in(own, dim), (parts,), jnp.float32, least / len(pieces), top_value / len(pieces)))
        factor_of = factor_of * jnp.repeat(draws, extent[dim] // parts).reshape([-1 if axis == dim else 1 for axis in range(len(extent))])
    return factor_of


def deal_out(own_key, own, number, rows, count, top, bound, lean):
    ranking = jax.random.permutation(own_key, count)
    packed, ordinary = load_shares(count, rows * top, bound, lean, True), load_shares(count, rows * top, bound, lean, False)
    places = jnp.arange(count)

    def named(tallies, rotation):
        used = int((tallies > 0).sum())
        fixed = max(1, used // 4)
        shifted = fixed + (places - fixed + rotation * (used - fixed)) % max(1, count - fixed)
        return jnp.zeros((count,), jnp.int32).at[ranking[jnp.where(places < fixed, places, shifted)]].set(jnp.asarray(tallies, jnp.int32))

    tallies = jnp.where(number % 4 == 0, named(packed, number // 4), named(ordinary, number - number // 4 - 1))
    mixed = jax.random.permutation(jax.random.fold_in(own, 3), count)
    source_of, taker = mixed[0:count // 2 * 2:2], mixed[1:count // 2 * 2:2]
    slack = jnp.minimum(tallies[source_of] - 1, bound - tallies[taker]) // 2
    slack = jnp.where((source_of == ranking[0]) | (taker == ranking[0]) | (tallies[taker] == 0), 0, jnp.maximum(slack, 0))
    shifted = jax.random.randint(jax.random.fold_in(own, 4), (count // 2,), 0, 1 << 20) % (slack + 1)
    tallies = tallies.at[source_of].add(-shifted).at[taker].add(shifted)
    members = jnp.searchsorted(jnp.cumsum(tallies), jnp.arange(rows * top), side="right").astype(jnp.int32)
    table = members.reshape(top, rows).T
    table = table[jax.random.permutation(jax.random.fold_in(own, 1), rows)]
    rotation = jax.random.randint(jax.random.fold_in(own, 2), (rows, 1), 0, top)
    return jnp.take_along_axis(table, (jnp.arange(top)[None, :] + rotation) % top, axis=1)


def load_shares(count, total, limit, slope, full):
    loads = [(1 << 20) // math.isqrt(rank ** slope) + 1 for rank in range(1, count + 1)]
    largest = limit if full else min(limit, max(-(-total // count), total * loads[0] // sum(loads)))
    least = 1 if total - largest >= count - 1 else 0
    given, surplus = [largest] + [least] * (count - 1), total - largest - least * (count - 1)
    while surplus > 0:
        movable = [i for i in range(1, count) if given[i] < largest] or [i for i in range(1, count) if given[i] < limit]
        mass, remaining = sum([loads[i] for i in movable]), surplus
        for i in movable:
            addition = min(limit - given[i], max(1, remaining * loads[i] // mass), surplus)
            given[i] = given[i] + addition
            surplus = surplus - addition
    return np.array(given)


def scatter_about(rng, dims, scale, most, cuts=(), kind=jnp.bfloat16):
    level = level_of(rng, dims, cuts, -0.22, 0.18) if cuts else 1.0
    entries = jax.random.normal(rng, dims, jnp.float32) * scale * level
    return jnp.minimum(jnp.maximum(entries, -most), most).astype(kind)


def setup_inputs(seed: int = 0) -> dict:
    key_of = jax.random.split(jax.random.key(seed), 10)
    states = scatter_about(key_of[0], (ROWS, FEAT), 1.0, 6.0, ((0, 32),))
    dest_device_keys = jax.random.split(jax.random.fold_in(key_of[1], 1), ROWS // TOK_DEV)
    dest_device_turns = jax.random.permutation(jax.random.fold_in(key_of[1], 3), ROWS // TOK_DEV)
    dest_device = jax.vmap(lambda own, number: deal_out(jax.random.fold_in(key_of[1], 2), own, number, TOK_DEV, N_DP, 1, CAP, 1))(dest_device_keys, dest_device_turns).reshape((ROWS, 1))
    goals = scatter_about(key_of[2], (SLOTS, GOAL), 1.0, 6.0, ((0, 32),))
    returns = draw_returns(jax.random.fold_in(key_of[9], 71), 0)
    weight_in = scatter_about(key_of[4], (IN, H), IN ** -0.5, 0.109375, ((0, 4),))
    weight_hidden = scatter_about(key_of[5], (LAYERS - 1, H, H), H ** -0.5, 0.25, ((1, 4),))
    norm_gain = jnp.clip(1.0 + 0.1 * jax.random.normal(key_of[6], (LAYERS, H), jnp.float32), 0.5, 1.5).astype(jnp.bfloat16)
    norm_shift = scatter_about(key_of[7], (LAYERS, H), 0.3, 1.5, ((1, 4),))
    weight_out = scatter_about(key_of[8], (H,), H ** -0.5, 0.25, ((0, 4),))
    return dict(states=states, dest_device=dest_device, goals=goals, returns=returns, weight_in=weight_in, weight_hidden=weight_hidden, norm_gain=norm_gain, norm_shift=norm_shift, weight_out=weight_out)


@jax.custom_vjp
def low(v):
    return lax.optimization_barrier(v.astype(jnp.bfloat16)).astype(jnp.float32)

@jax.custom_vjp
def low_back(v):
    return v

def low_keep(v):
    return (low(v), None)

def low_pass(kept, grad):
    return (grad,)

def back_keep(v):
    return (v, None)

def back_low(kept, grad):
    return (low(grad),)
low.defvjp(low_keep, low_pass)
low_back.defvjp(back_keep, back_low)

def norm_act(values, gain, shift):
    center = values - lax.optimization_barrier(jnp.mean(values, axis=-1, keepdims=True))
    spread = lax.optimization_barrier(jnp.mean(center * center, axis=-1, keepdims=True))
    return jax.nn.elu(center * lax.rsqrt(spread + 1e-05) * gain + shift)

def block_loss(params, state_block, goal_block, target_block):
    weight_in, weight_hidden, norm_gain, norm_shift, weight_out = params
    highest = lax.Precision.HIGHEST
    inputs = jnp.concatenate([low_back(state_block), low_back(goal_block)], axis=1)
    hidden = inputs
    for layer_number in range(LAYERS):
        matrix = weight_in if layer_number == 0 else weight_hidden[layer_number - 1]
        projected = low_back(jnp.dot(hidden, matrix, precision=highest))
        hidden = low(norm_act(projected, norm_gain[layer_number], norm_shift[layer_number]))
    value_pred = low_back(jnp.dot(hidden, weight_out, precision=highest))
    row_error = value_pred - target_block
    return 0.5 * jnp.sum(row_error * row_error) / ROWS

def reference(states, dest_device, goals, returns, weight_in, weight_hidden, norm_gain, norm_shift, weight_out):
    device_total = N_DP * N_MP
    dest_rows = dest_device[:, 0].reshape(device_total, TOK_DEV)
    dest_onehot = (dest_rows[:, :, None] == jnp.arange(N_DP, dtype=jnp.int32)[None, None, :]).astype(jnp.int32)
    rank_within = lax.optimization_barrier(jnp.sum((jnp.cumsum(dest_onehot, axis=1) - dest_onehot) * dest_onehot, axis=2))
    device_ids = jnp.arange(device_total, dtype=jnp.int32)[:, None]
    slot_index = ((dest_rows * N_MP + device_ids % N_MP) * N_DP + device_ids // N_MP) * CAP + rank_within
    slot_index = slot_index.astype(jnp.int32)
    slot_flat = slot_index.reshape(-1)
    row_returns = returns[slot_flat].astype(jnp.float32)
    scale_value = jnp.sqrt(jnp.sum(row_returns * row_returns) / ROWS + 1e-06)
    targets = (row_returns / scale_value).reshape(device_total, TOK_DEV)
    params = tuple((weight.astype(jnp.float32) for weight in (weight_in, weight_hidden, norm_gain, norm_shift, weight_out)))
    state_blocks = states.reshape(device_total, TOK_DEV, FEAT)

    def scan_step(running, block):
        state_block, slot_block, target_block = block
        goal_block = goals[slot_block].astype(jnp.float32)

        def local_loss(param_set, state_set, goal_set):
            return block_loss(param_set, state_set, goal_set, target_block)
        loss_block, pullback = jax.vjp(local_loss, params, state_block.astype(jnp.float32), goal_block)
        grad_params, grad_block, grad_goal_block = pullback(jnp.ones_like(loss_block))
        updated = (running[0] + loss_block, jax.tree.map(lambda first, second: first + second, running[1], grad_params))
        return (updated, (grad_block.astype(jnp.bfloat16), grad_goal_block.astype(jnp.bfloat16)))
    start = (jnp.zeros((), jnp.float32), jax.tree.map(jnp.zeros_like, params))
    (total_loss, grads), (grad_blocks, goal_blocks) = lax.scan(scan_step, start, (state_blocks, slot_index, targets))
    grad_goals = jnp.zeros((SLOTS, GOAL), jnp.bfloat16).at[slot_flat].set(goal_blocks.reshape(ROWS, GOAL))
    return (total_loss, grad_blocks.reshape(ROWS, FEAT), grad_goals, grads[0], grads[1], grads[2], grads[3], grads[4])
```

```python
import functools

import jax
import jax.numpy as jnp
from jax import lax
from jax.experimental import pallas as pl
from jax.experimental.pallas import tpu as pltpu
from jax.sharding import PartitionSpec as P

BF = jnp.bfloat16
F32 = jnp.float32
TILES = 8
STEP = 32
VMEM = 48 * 1024 * 1024


def dot(first, second, dims):
    return lax.dot_general(first, second, (dims, ((), ())), preferred_element_type=F32)


def xor_pairs(count, bits):
    return [(i, i ^ bits) for i in range(count)]


def goal_forward_kernel(order, _, goals_ref, weight_ref, *out_refs):
    step = pl.program_id(0)
    product = dot(goals_ref[...], weight_ref[...], ((1,), (0,))).astype(BF)
    for place, out_ref in enumerate(out_refs):

        @pl.when(step == place)
        def _():
            out_ref[...] = product


def goal_forward(own, goals, weight, tiles):
    rows, width, units = goals.shape[0] // TILES, goals.shape[1], weight.shape[1]
    places = jnp.array(tiles, jnp.int32) ^ own
    return pl.pallas_call(
        functools.partial(goal_forward_kernel, tiles),
        out_shape=[jax.ShapeDtypeStruct((rows, units), BF)] * len(tiles),
        grid_spec=pltpu.PrefetchScalarGridSpec(
            num_scalar_prefetch=1,
            grid=(len(tiles),),
            in_specs=[
                pl.BlockSpec((rows, width), lambda i, places: (places[i], 0)),
                pl.BlockSpec((width, units), lambda i, places: (0, 0)),
            ],
            out_specs=[pl.BlockSpec((rows, units), lambda i, places: (0, 0))] * len(tiles),
        ),
        compiler_params=pltpu.CompilerParams(vmem_limit_bytes=VMEM),
        cost_estimate=pl.CostEstimate(
            flops=2 * len(tiles) * rows * width * units,
            bytes_accessed=len(tiles) * rows * (width + units) * 2 + width * units * 2,
            transcendentals=0,
        ),
        name="goal_forward",
    )(places, goals, weight)


def goal_backward_kernel(count, has_before, places_ref, *refs):
    grad_refs, refs = refs[:count], refs[count:]
    goals_ref, weight_ref = refs[:2]
    refs = refs[2:]
    if has_before:
        sum_before_ref = refs[1]
        refs = refs[2:]
    out_ref, sum_ref, grad_scratch = refs
    step = pl.program_id(0)
    for place in range(count):

        @pl.when(step == place)
        def _():
            grad_scratch[...] = grad_refs[place][...]

    grad = grad_scratch[...]
    out_ref[...] = dot(grad, weight_ref[...], ((1,), (1,))).astype(BF)
    share = dot(grad, goals_ref[...], ((0,), (0,)))

    @pl.when(step == 0)
    def _():
        if has_before:
            sum_ref[...] = sum_before_ref[...] + share
        else:
            sum_ref[...] = share

    @pl.when(step > 0)
    def _():
        sum_ref[...] += share


def goal_backward(own, grads, goals, weight, tiles, before):
    rows, width, units = goals.shape[0] // TILES, goals.shape[1], weight.shape[1]
    places = jnp.array(tiles, jnp.int32) ^ own
    count = len(tiles)
    whole = pl.BlockSpec((rows, units), lambda i, places: (0, 0))
    in_specs = [whole] * count + [
        pl.BlockSpec((rows, width), lambda i, places: (places[i], 0)),
        pl.BlockSpec((width, units), lambda i, places: (0, 0)),
    ]
    operands = [*grads, goals, weight]
    aliases = {}
    if before is not None:
        in_specs += [
            pl.BlockSpec(memory_space=pl.ANY),
            pl.BlockSpec((units, width), lambda i, places: (0, 0)),
        ]
        operands += list(before)
        aliases = {count + 3: 0}
    return pl.pallas_call(
        functools.partial(goal_backward_kernel, count, before is not None),
        out_shape=[
            jax.ShapeDtypeStruct(goals.shape, BF),
            jax.ShapeDtypeStruct((units, width), F32),
        ],
        grid_spec=pltpu.PrefetchScalarGridSpec(
            num_scalar_prefetch=1,
            grid=(count,),
            in_specs=in_specs,
            out_specs=[
                pl.BlockSpec((rows, width), lambda i, places: (places[i], 0)),
                pl.BlockSpec((units, width), lambda i, places: (0, 0)),
            ],
            scratch_shapes=[pltpu.VMEM((rows, units), BF)],
        ),
        input_output_aliases=aliases,
        compiler_params=pltpu.CompilerParams(vmem_limit_bytes=VMEM),
        cost_estimate=pl.CostEstimate(
            flops=4 * count * rows * width * units,
            bytes_accessed=count * rows * (2 * width + units) * 2 + width * units * 6,
            transcendentals=0,
        ),
        name="goal_backward",
    )(places, *operands)


def critic_kernel(
    count, first_tile, layers, key_ref, target_ref, states_ref, hidden_ref, vectors_ref, out_weight_ref, *refs
):
    goal_refs, refs = refs[:count], refs[count:]
    first_refs, refs = refs[:count], refs[count:]
    acts_ref, grads_ref, sums_ref, work, nhat, slope, spread, top_act, low_grad, sums = refs
    step = pl.program_id(0)
    rows, units = work.shape
    tokens = key_ref.shape[1]
    steps = rows // STEP

    @pl.when(step == 0)
    def _():
        sums[...] = jnp.zeros_like(sums)

    for place in range(count):

        @pl.when(step == place)
        def _():
            low_grad[...] = goal_refs[place][...]

    base = (first_tile + step) * rows
    slot = base + lax.broadcasted_iota(jnp.int32, (rows, tokens), 0)
    pick = (slot == key_ref[...]).astype(F32).astype(BF)
    work[...] = dot(pick, states_ref[...], ((1,), (0,))) + low_grad[...].astype(F32)

    for layer in range(layers):
        gain = vectors_ref[pl.ds(layer, 1), :]
        shift = vectors_ref[pl.ds(layers + layer, 1), :]

        @pl.loop(0, steps)
        def _(i):
            here = pl.ds(pl.multiple_of(i * STEP, STEP), STEP)
            values = work[here, :]
            center = values - jnp.mean(values, axis=1, keepdims=True)
            inverse = lax.rsqrt(jnp.mean(center * center, axis=1, keepdims=True) + 1e-05)
            scaled = center * inverse
            shifted = scaled * gain + shift
            slopes = jnp.exp(jnp.minimum(shifted, 0.0))
            nhat[layer, here, :] = scaled
            slope[layer, here, :] = slopes
            spread[layer, here, :] = inverse
            act = (jnp.maximum(shifted, 0.0) + (slopes - 1.0)).astype(BF)
            if layer < layers - 1:
                acts_ref[layer, here, :] = act
            else:
                top_act[here, :] = act

        if layer < layers - 1:
            work[...] = dot(acts_ref[layer], hidden_ref[layer], ((1,), (0,)))

    out_weight = out_weight_ref[...]
    last = top_act[...]
    value = dot(out_weight, last, ((1,), (1,)))
    target = target_ref[0]
    error = (value[0:1, :] - target[0:1, :]) * target[1:2, :]
    grad_value = (error * target[2:3, :]).astype(BF)
    grad_rows = jnp.concatenate([grad_value.astype(F32), jnp.zeros((7, rows), F32)], axis=0).astype(BF)
    sums[2 * layers] += dot(grad_rows, last, ((1,), (0,)))
    sums[2 * layers + 1] += jnp.broadcast_to(jnp.sum(error * error, axis=1, keepdims=True), (8, units))
    work[...] = dot(grad_rows, out_weight, ((0,), (0,)))

    for layer in reversed(range(layers)):
        gain = vectors_ref[pl.ds(layer, 1), :]

        @pl.loop(0, steps)
        def _(i):
            here = pl.ds(pl.multiple_of(i * STEP, STEP), STEP)
            scaled = nhat[layer, here, :]
            grad_norm = work[here, :] * slope[layer, here, :]
            by_scaled = grad_norm * scaled
            sums[layer] += jnp.sum(by_scaled.reshape(STEP // 8, 8, units), axis=0)
            sums[layers + layer] += jnp.sum(grad_norm.reshape(STEP // 8, 8, units), axis=0)
            grad_scaled = grad_norm * gain
            first_mean = jnp.mean(grad_scaled, axis=1, keepdims=True)
            second_mean = jnp.mean(by_scaled * gain, axis=1, keepdims=True)
            grad = spread[layer, here, :] * (grad_scaled - first_mean - scaled * second_mean)
            if layer > 0:
                grads_ref[layer - 1, here, :] = grad.astype(BF)
            else:
                low_grad[here, :] = grad.astype(BF)

        if layer > 0:
            work[...] = dot(grads_ref[layer - 1], hidden_ref[layer - 1], ((1,), (1,)))

    for place in range(count):

        @pl.when(step == place)
        def _():
            first_refs[place][...] = low_grad[...]

    @pl.when(step == count - 1)
    def _():
        sums_ref[...] = sums[...]


def critic(key_row, targets, state_part, hidden, vectors, out_weight, goal_parts, tiles):
    count, first_tile = len(tiles), tiles[0]
    rows, units = goal_parts[0].shape
    layers = hidden.shape[0] + 1
    whole = lambda shape: pl.BlockSpec(shape, lambda i: (0,) * len(shape))
    sums_shape = (2 * layers + 2, 8, units)
    return pl.pallas_call(
        functools.partial(critic_kernel, count, first_tile, layers),
        grid=(count,),
        out_shape=[jax.ShapeDtypeStruct((rows, units), BF)] * count
        + [jax.ShapeDtypeStruct((layers - 1, count * rows, units), BF)] * 2
        + [jax.ShapeDtypeStruct(sums_shape, F32)],
        in_specs=[
            whole(key_row.shape),
            pl.BlockSpec((1,) + targets.shape[1:], lambda i: (first_tile + i, 0, 0)),
            whole(state_part.shape),
            whole(hidden.shape),
            whole(vectors.shape),
            whole(out_weight.shape),
        ]
        + [whole((rows, units))] * count,
        out_specs=[whole((rows, units))] * count
        + [pl.BlockSpec((layers - 1, rows, units), lambda i: (0, i, 0))] * 2
        + [whole(sums_shape)],
        scratch_shapes=[
            pltpu.VMEM((rows, units), F32),
            pltpu.VMEM((layers, rows, units), F32),
            pltpu.VMEM((layers, rows, units), F32),
            pltpu.VMEM((layers, rows, 1), F32),
            pltpu.VMEM((rows, units), BF),
            pltpu.VMEM((rows, units), BF),
            pltpu.VMEM(sums_shape, F32),
        ],
        compiler_params=pltpu.CompilerParams(vmem_limit_bytes=VMEM),
        cost_estimate=pl.CostEstimate(
            flops=2 * count * rows * units * (key_row.shape[1] + 6 * units + 200),
            bytes_accessed=count * rows * units * 16 + state_part.size * 2 + hidden.size * 2,
            transcendentals=count * rows * units * layers,
        ),
        name="critic",
    )(key_row, targets, state_part, hidden, vectors, out_weight, *goal_parts)


def across(block, tile, dp_count):
    per = dp_count // TILES
    moved = block if tile == 0 else lax.ppermute(block, "dp", xor_pairs(dp_count, tile * per))
    if per == 1:
        return moved
    groups = [[group * per + low for low in range(per)] for group in range(TILES)]
    parts = moved.reshape((per, block.shape[0] // per) + block.shape[1:])
    parts = lax.all_to_all(parts, "dp", 0, 0, axis_index_groups=groups, tiled=True)
    return parts.reshape(block.shape)


def gather_pieces(piece, mp_count):
    upper = mp_count // 2
    pieces = [piece] + [None] * (mp_count - 1)
    bit = upper
    filled = [0]
    while bit:
        for j in list(filled):
            pieces[j ^ bit] = lax.ppermute(pieces[j], "mp", xor_pairs(mp_count, bit))
        filled += [j ^ bit for j in filled]
        bit //= 2
    return pieces


def piece_of(pieces, shard, own):
    return lax.select_n(own, *[pieces[shard ^ i] for i in range(len(pieces))])


def scatter_sum(partial, dp_count, mp_count):
    own_dp, own_mp = lax.axis_index("dp"), lax.axis_index("mp")
    units, width = partial.shape
    share = units // (dp_count * mp_count)
    bits = mp_count.bit_length() - 1
    held = partial.reshape((dp_count,) + (2,) * bits + (share, width))
    for level in range(bits):
        axis = bits - level
        mine = (own_mp >> level) & 1
        sent = lax.dynamic_index_in_dim(held, 1 - mine, axis, keepdims=False).astype(BF)
        kept = lax.dynamic_index_in_dim(held, mine, axis, keepdims=False)
        held = kept + lax.ppermute(sent, "mp", xor_pairs(mp_count, 1 << level)).astype(F32)
    if dp_count > TILES:
        held = held.reshape(dp_count * share, width)
        return lax.psum_scatter(held, "dp", scatter_dimension=0, tiled=True)
    total = lax.dynamic_index_in_dim(held, own_dp, 0, keepdims=False)
    sent = [lax.dynamic_index_in_dim(held, own_dp ^ o, 0, keepdims=False).astype(BF) for o in range(1, dp_count)]
    for offset, block in enumerate(sent, 1):
        total = total + lax.ppermute(block, "dp", xor_pairs(dp_count, offset)).astype(F32)
    return total


def sum_over_all(value, dp_count, mp_count):
    for name, count in (("mp", mp_count), ("dp", dp_count)):
        if count > TILES:
            value = lax.psum(value, name)
            continue
        got = [lax.ppermute(value, name, xor_pairs(count, offset)) for offset in range(1, count)]
        for other in got:
            value = value + other
    return value


def shards(
    states, dest_device, goals, returns, weight_in, weight_hidden, norm_gain, norm_shift, weight_out
):
    dp_count, mp_count = lax.axis_size("dp"), lax.axis_size("mp")
    own_dp, own_mp = lax.axis_index("dp"), lax.axis_index("mp")
    tokens, feat_width = states.shape
    all_rows = tokens * dp_count * mp_count
    slot_count, goal_width = goals.shape
    capacity = slot_count // dp_count
    shard_in, units = weight_in.shape
    layers = norm_gain.shape[0]
    shard_units = norm_gain.shape[1]
    per = dp_count // TILES
    rows = slot_count // TILES
    own_tile = own_dp // per

    cut = feat_width % shard_in
    first_goal_shard = feat_width // shard_in
    tail_pieces = gather_pieces(weight_in[cut:], mp_count)
    head_pieces = gather_pieces(weight_in[:cut], mp_count) if cut else None
    small = jnp.concatenate([norm_gain, norm_shift, weight_out[None, :]], axis=0)
    small = jnp.pad(small, ((0, 16 - small.shape[0]), (0, 0)))
    layer_pieces = gather_pieces(weight_hidden.reshape((layers - 1) * shard_units, units), mp_count)
    small_pieces = gather_pieces(small, mp_count)

    state_weight, goal_weight = [], []
    for shard in range(mp_count):
        tail = piece_of(tail_pieces, shard, own_mp)
        head = piece_of(head_pieces, shard, own_mp) if cut else None
        if shard < first_goal_shard:
            state_weight += [head, tail] if cut else [tail]
        elif shard == first_goal_shard and cut:
            state_weight.append(head)
            goal_weight.append(tail)
        else:
            goal_weight += [head, tail] if cut else [tail]
    state_weight = jnp.concatenate(state_weight, axis=0)
    goal_weight = jnp.concatenate(goal_weight, axis=0)
    hidden = jnp.concatenate(
        [
            piece_of(layer_pieces, shard, own_mp).reshape(layers - 1, shard_units, units)
            for shard in range(mp_count)
        ],
        axis=1,
    )
    vectors_bf = jnp.concatenate([piece_of(small_pieces, shard, own_mp) for shard in range(mp_count)], axis=1)
    vectors = vectors_bf.astype(F32)
    out_weight = jnp.pad(vectors_bf[2 * layers : 2 * layers + 1], ((0, 7), (0, 0)))

    dest = dest_device[:, 0]
    offset = ((dest // per) ^ own_tile) * per + dest % per
    blocks = tokens // 128
    marks = (offset[None, :] == jnp.arange(dp_count, dtype=jnp.int32)[:, None]).astype(F32)
    marks = marks.reshape(dp_count, blocks, 128)
    upper = jnp.arange(128)[:, None] < jnp.arange(128)[None, :]
    within = dot(marks.astype(BF), upper.astype(BF), ((2,), (0,)))
    block_sums = jnp.sum(marks, axis=2)
    earlier = jnp.arange(blocks)[None, :] < jnp.arange(blocks)[:, None]
    ahead = jnp.sum(jnp.where(earlier[None], block_sums[:, None, :], 0.0), axis=2)
    rank = jnp.sum(marks * (within + ahead[:, :, None]), axis=0).reshape(tokens)
    key = offset * capacity + rank.astype(jnp.int32)
    filled = jnp.sum(block_sums, axis=1)

    tile_returns = returns.reshape(TILES, rows)
    got_returns = [
        across(lax.dynamic_index_in_dim(tile_returns, own_tile ^ t, 0, keepdims=False), t, dp_count)
        for t in range(TILES)
    ]
    got_returns = jnp.stack(got_returns).reshape(dp_count, capacity).astype(F32)
    valid = (jnp.arange(capacity, dtype=F32)[None, :] < filled[:, None]).astype(F32)
    local_square = jnp.sum(valid * got_returns * got_returns)
    square_total = sum_over_all(jnp.full((8, 128), local_square), dp_count, mp_count)[0, 0]
    scale_value = jnp.sqrt(square_total / all_rows + 1e-06)
    targets = jnp.stack(
        [got_returns / scale_value, valid, jnp.full_like(valid, 1.0 / all_rows)]
        + [jnp.zeros_like(valid)] * 5
    )
    targets = targets.reshape(8, TILES, rows).transpose(1, 0, 2)

    far, near = tuple(range(TILES // 2, TILES)), tuple(range(TILES // 2))
    sent_far = goal_forward(own_tile, goals, goal_weight, far)
    got_far = [across(block, tile, dp_count) for block, tile in zip(sent_far, far)]
    sent_near = goal_forward(own_tile, goals, goal_weight, near)
    got_near = [across(block, tile, dp_count) for block, tile in zip(sent_near, near)]

    state_part = dot(states, state_weight, ((1,), (0,))).astype(BF)
    key_row = key[None, :]
    half = len(far) // 2
    groups = ((near, got_near), (far[:half], got_far[:half]), (far[half:], got_far[half:]))
    first_grads, acts, grads, sums = [], [], [], []
    for tiles, got in groups:
        made = critic(key_row, targets, state_part, hidden, vectors, out_weight, got, tiles)
        first_grads.append(made[: len(tiles)])
        acts.append(made[-3])
        grads.append(made[-2])
        sums.append(made[-1])
    back = [
        [across(block, tile, dp_count) for block, tile in zip(blocks_of, tiles)]
        for blocks_of, (tiles, _) in zip(first_grads, groups)
    ]

    all_first = jnp.concatenate([block for blocks_of in first_grads for block in blocks_of], axis=0)
    pick = (key[:, None] == jnp.arange(slot_count, dtype=jnp.int32)[None, :]).astype(BF)
    first_grad = dot(pick, all_first, ((1,), (0,))).astype(BF)
    grad_states = dot(first_grad, state_weight, ((1,), (1,))).astype(BF)
    grad_state_weight = dot(first_grad, states, ((0,), (0,)))
    grad_hidden = [
        sum(dot(grad[layer], act[layer], ((0,), (0,))) for grad, act in zip(grads, acts))
        for layer in range(layers - 1)
    ]
    sums = sum(sums)
    vector_sums = jnp.sum(sums[: 2 * layers + 1], axis=1)
    local_loss = 0.5 * sums[2 * layers + 1, 0, 0] / all_rows
    vector_sums = jnp.concatenate([vector_sums, jnp.full((1, units), local_loss)], axis=0)
    high = vector_sums.astype(BF).astype(F32)
    count = 2 * layers + 2
    columns = jnp.concatenate(
        [high, vector_sums - high, jnp.zeros((128 - 2 * count, units), F32)], axis=0
    ).T
    share = scatter_sum(
        jnp.concatenate([grad_state_weight] + grad_hidden + [columns], axis=1), dp_count, mp_count
    )
    vector_share = share[:, -128:]
    vector_share = (vector_share[:, :count] + vector_share[:, count : 2 * count]).T

    running = None
    for (tiles, _), got in zip(groups, back):
        running = goal_backward(own_tile, got, goals, goal_weight, tiles, running)
    grad_goals, grad_goal_weight = running
    goal_share = scatter_sum(grad_goal_weight, dp_count, mp_count)

    state_share = share[:, :feat_width]
    hidden_share = share[:, feat_width : feat_width + (layers - 1) * units]
    return (
        vector_share[count - 1, 0],
        grad_states,
        grad_goals,
        jnp.concatenate([state_share, goal_share], axis=1).T,
        hidden_share.reshape(-1, layers - 1, units).transpose(1, 2, 0),
        vector_share[:layers],
        vector_share[layers : 2 * layers],
        vector_share[2 * layers],
    )


def solution(mesh):
    placed = (
        P(("dp", "mp"), None),
        P(("dp", "mp"), None),
        P(("dp", "mp"), None),
        P(("dp", "mp")),
        P("mp", None),
        P(None, "mp", None),
        P(None, "mp"),
        P(None, "mp"),
        P("mp"),
    )
    return jax.shard_map(
        shards,
        mesh=mesh,
        in_specs=placed,
        out_specs=(
            P(),
            P(("dp", "mp"), None),
            P(("dp", "mp"), None),
            P(None, ("dp", "mp")),
            P(None, None, ("dp", "mp")),
            P(None, ("dp", "mp")),
            P(None, ("dp", "mp")),
            P(("dp", "mp")),
        ),
        check_vma=False,
    )
```

```python
import functools

import jax
import jax.numpy as jnp
from jax import lax
from jax.experimental import pallas as pl
from jax.experimental.pallas import tpu as pltpu
from jax.sharding import PartitionSpec as P

BF = jnp.bfloat16
F32 = jnp.float32
I32 = jnp.int32
TILES = 8
STEP = 64
VMEM = 58 * 1024 * 1024
NEAR, FAR_ONE, FAR_TWO = (0, 1, 2, 3), (4, 5), (6, 7)
BRIEF = pl.CostEstimate(flops=1, bytes_accessed=1, transcendentals=0)
LONG = pl.CostEstimate(flops=6_000_000_000, bytes_accessed=10_000_000, transcendentals=0)
CORE, Y, X, Z_LOW, Z_HIGH = range(5)
FIRST_ORDER = (CORE, Y, Z_HIGH, Z_LOW, X)


def dot(first, second, dims):
    return lax.dot_general(first, second, (dims, ((), ())), preferred_element_type=F32)


ROWS_BY_COLUMNS, BY_ROWS, OVER_ROWS = ((1,), (0,)), ((1,), (1,)), ((0,), (0,))


def after(value, *others):
    return lax.optimization_barrier((value, *others))[0]


def xor_pairs(count, bits):
    return [(i, i ^ bits) for i in range(count)]


def like(*shape_and_type):
    *shape, dtype = shape_and_type
    return jax.ShapeDtypeStruct(tuple(shape), dtype)


def whole(shape):
    return pl.BlockSpec(tuple(shape), lambda *_: (0,) * len(shape))


ANYWHERE = pl.BlockSpec(memory_space=pl.ANY)


def call(kernel, name, grid, scalars, in_specs, out_specs, out_shape, operands, scratch=(), aliases=None, cost=BRIEF):
    return pl.pallas_call(
        kernel,
        out_shape=out_shape,
        grid_spec=pltpu.PrefetchScalarGridSpec(
            num_scalar_prefetch=1,
            grid=grid,
            in_specs=in_specs,
            out_specs=out_specs,
            scratch_shapes=list(scratch),
        ),
        input_output_aliases=aliases or {},
        compiler_params=pltpu.CompilerParams(vmem_limit_bytes=VMEM),
        cost_estimate=cost,
        name=name,
    )(scalars, *operands)


def route_kernel(capacity, own_ref, dest_ref, returns_ref, row_ref, column_ref, message_ref, wide, text):
    own = own_ref[0]
    tokens = dest_ref.shape[1]
    count = returns_ref.shape[0]
    blocks = tokens // 128
    offsets = dest_ref[...] ^ own
    marks = (lax.broadcasted_iota(I32, (count, tokens), 0) == offsets).astype(F32)
    stacked = jnp.concatenate([marks[:, 128 * b : 128 * b + 128] for b in range(blocks)], axis=0)
    upper = lax.broadcasted_iota(I32, (128, 128), 0) < lax.broadcasted_iota(I32, (128, 128), 1)
    within = dot(stacked.astype(BF), upper.astype(F32).astype(BF), ROWS_BY_COLUMNS)
    totals = jnp.sum(stacked, axis=1, keepdims=True)
    ahead = jnp.zeros((count, 1), F32)
    for b in range(blocks):
        part = slice(count * b, count * b + count)
        lanes = slice(128 * b, 128 * b + 128)
        rank = jnp.sum(stacked[part] * (within[part] + ahead), axis=0, keepdims=True)
        key = offsets[:, lanes].astype(F32) * capacity + rank
        row_ref[:, lanes] = key.astype(I32)
        column_ref[lanes, :] = jnp.broadcast_to(key, (128, 128)).T[:, 0:1].astype(I32)
        ahead = ahead + totals[part]
    wide[...] = returns_ref[...].astype(F32)
    lane = lax.broadcasted_iota(I32, text.shape, 1) - (text.shape[1] - 128)
    high = jnp.floor(ahead * 0.0625)
    text[...] = jnp.where(lane == 0, high, jnp.where(lane == 1, ahead - 16.0 * high, 0.0))
    for offset in range(count):
        text[offset : offset + 1, 0:capacity] = wide[pl.ds(own ^ offset, 1), :]
    message_ref[...] = text[...].astype(BF)


def route(own, dest_row, returns, units):
    tokens, (count, capacity) = dest_row.shape[1], returns.shape
    return call(
        functools.partial(route_kernel, capacity),
        "route",
        (1,),
        own[None],
        [whole(dest_row.shape), whole(returns.shape)],
        [whole((1, tokens)), whole((tokens, 1)), whole((count, units))],
        [like(1, tokens, I32), like(tokens, 1, I32), like(count, units, BF)],
        [dest_row, returns],
        [pltpu.VMEM(returns.shape, F32), pltpu.VMEM((count, units), F32)],
    )


def prepare_kernel(layers, rows, capacity, total_rows, own_ref, *refs):
    pieces, refs = refs[:4], refs[4:]
    hidden_ref, vectors_ref, out_weight_ref = refs[:3]
    own = own_ref[0]
    width = hidden_ref.shape[2] // 4
    for shard in range(4):
        columns = slice(shard * width, (shard + 1) * width)
        for value in range(4):

            @pl.when(own == value)
            def _():
                piece = pieces[shard ^ value]
                for layer in range(layers - 1):
                    hidden_ref[layer, columns, :] = piece[layer * width : (layer + 1) * width, :]
                start = (layers - 1) * width
                small = piece[start : start + 16, :].astype(F32)
                for row in range(2 * layers + 1):
                    vectors_ref[row : row + 1, columns] = small[
                        row // 4 : row // 4 + 1, (row % 4) * width : (row % 4 + 1) * width
                    ]

    vectors_ref[2 * layers + 1 :, :] = jnp.zeros((16 - 2 * layers - 1, vectors_ref.shape[1]), F32)
    out_weight_ref[...] = jnp.concatenate(
        [vectors_ref[2 * layers : 2 * layers + 1, :], jnp.zeros((7, vectors_ref.shape[1]), F32)], axis=0
    ).astype(BF)
    if len(refs) == 3:
        return
    targets_ref = refs[3]
    targets_ref[...] = jnp.zeros_like(targets_ref)
    index = lax.broadcasted_iota(I32, (64, 64), 0)
    partner = ((index // 8) ^ (index % 8)) * 8 + index % 8
    swap = (lax.broadcasted_iota(I32, (64, 64), 1) == partner).astype(F32).astype(BF)
    lane = lax.broadcasted_iota(I32, (64, 128 * 3), 1).astype(F32)
    total = jnp.zeros((1, 1), F32)
    for piece in pieces:
        message = piece[rows : rows + 64, :]
        counts = dot(swap, message[:, 384:512], ROWS_BY_COLUMNS)
        counts = counts[:, 0:1] * 16.0 + counts[:, 1:2]
        values = message[:, 0:384].astype(F32)
        squares = jnp.sum(jnp.where(lane < counts, values * values, 0.0), axis=1, keepdims=True)
        total = total + jnp.sum(squares, axis=0, keepdims=True)
    scale = jnp.sqrt(total / total_rows + 1e-06)
    message = pieces[0][rows : rows + 64, :].astype(F32)
    counts = message[0:8, 384:385] * 16.0 + message[0:8, 385:386]
    for tile in range(TILES):
        lanes = slice((tile % 2) * capacity, (tile % 2) * capacity + capacity)
        target = message[9 * tile : 9 * tile + 1, 0:384] / scale
        filled = (lane[0:1] < counts[tile : tile + 1]).astype(F32)
        targets_ref[tile // 2, 0:1, lanes] = target[:, 0:capacity]
        targets_ref[tile // 2, 1:2, lanes] = filled[:, 0:capacity]
        targets_ref[tile // 2, 2:3, lanes] = jnp.full((1, capacity), 1.0 / total_rows, F32)


def prepare(own, pieces, layers, rows, capacity, total_rows):
    units = pieces[0].shape[1]
    shapes = [like(layers - 1, units, units, BF), like(16, units, F32), like(8, units, BF)]
    if pieces[0].shape[0] > rows:
        shapes.append(like(TILES // 2, 8, 2 * capacity, F32))
    return call(
        functools.partial(prepare_kernel, layers, rows, capacity, total_rows),
        "prepare",
        (1,),
        own[None],
        [whole(piece.shape) for piece in pieces],
        [whole(shape.shape) for shape in shapes],
        shapes,
        pieces,
    )


def fetch(own, parts, target_ref, sems, later=()):
    place = 0
    for number, (shard, candidates) in enumerate(parts):
        size = candidates[0].shape[0]
        there = target_ref.at[place : place + size]
        for value in range(4):

            @pl.when(own == value)
            def _():
                pltpu.make_async_copy(candidates[shard ^ value], there, sems.at[number]).start()

        place += size
    for copy in later:
        copy.start()
    place = 0
    for number, (shard, candidates) in enumerate(parts):
        size = candidates[0].shape[0]
        there = target_ref.at[place : place + size]
        pltpu.make_async_copy(candidates[0], there, sems.at[number]).wait()
        place += size


def first_weight_parts(refs, cut, shards, first, last):
    own, one, tail_two, tail_three, odd_two, odd_three, even_two, even_three = refs
    head = lambda shard: (
        own.at[:cut],
        one.at[:cut],
        odd_two if shard % 2 else even_two,
        odd_three if shard % 2 else even_three,
    )
    tail = (own.at[cut:], one.at[cut:], tail_two, tail_three)
    parts = []
    for shard in shards:
        if not (shard == first and last is None):
            parts.append((shard, head(shard)))
        if not (shard == last):
            parts.append((shard, tail))
    return parts


def goal_forward_kernel(count, fetched, cut, first_shard, scalars_ref, goals_ref, *refs):
    rows = goals_ref.shape[0] // TILES
    if fetched:
        pieces, refs = refs[:6], refs[6:]
        out_refs, weight_ref, refs = refs[:count], refs[count], refs[count + 1 :]
    else:
        weight_ref, out_refs, refs = refs[0], refs[1 : count + 1], refs[count + 1 :]
    goals, made, sems, out_sems, fetch_sems = refs
    copies = []
    for place in range(count):
        there = goals_ref.at[pl.ds(pl.multiple_of(scalars_ref[place] * rows, rows), rows)]
        copies.append(pltpu.make_async_copy(there, goals.at[place], sems.at[place]))
        if place == 0:
            copies[0].start()
    if fetched:
        own, one, tail_two, tail_three, odd_two, odd_three = pieces
        refs8 = (own, one, tail_two, tail_three, odd_two, odd_three, None, None)
        parts = first_weight_parts(refs8, cut, range(first_shard, 4), first_shard, None)
        fetch(scalars_ref[count], parts, weight_ref, fetch_sems, copies[1:])
    else:
        for copy in copies[1:]:
            copy.start()
    sent = []
    for place in range(count):
        copies[place].wait()
        made[place] = dot(goals[place], weight_ref[...], ROWS_BY_COLUMNS).astype(BF)
        sent.append(pltpu.make_async_copy(made.at[place], out_refs[place], out_sems.at[place]))
        sent[-1].start()
    for copy in sent:
        copy.wait()


def goal_forward(own_tile, own_mp, goals, weight, tiles, cut=0, first_shard=0):
    rows, width = goals.shape[0] // TILES, goals.shape[1]
    fetched = isinstance(weight, tuple)
    units = weight[0].shape[1] if fetched else weight.shape[1]
    scalars = jnp.concatenate([jnp.array(tiles, I32) ^ own_tile, own_mp[None]])
    count = len(tiles)
    return call(
        functools.partial(goal_forward_kernel, count, fetched, cut, first_shard),
        "goal_forward",
        (1,),
        scalars,
        [ANYWHERE] * 7 if fetched else [ANYWHERE, whole(weight.shape)],
        [ANYWHERE] * count + ([whole((width, units))] if fetched else []),
        [like(rows, units, BF)] * count + ([like(width, units, BF)] if fetched else []),
        [goals] + (list(weight) if fetched else [weight]),
        [
            pltpu.VMEM((count, rows, width), BF),
            pltpu.VMEM((count, rows, units), BF),
            pltpu.SemaphoreType.DMA((count,)),
            pltpu.SemaphoreType.DMA((count,)),
            pltpu.SemaphoreType.DMA((8,)),
        ],
    )


def state_forward_kernel(cut, last_shard, own_ref, states_ref, *refs):
    pieces, (out_ref, weight_ref, sems) = refs[:8], refs[8:]

    @pl.when(pl.program_id(0) == 0)
    def _():
        parts = first_weight_parts(pieces, cut, range(last_shard + 1), None, last_shard)
        fetch(own_ref[0], parts, weight_ref, sems)

    out_ref[...] = dot(states_ref[...], weight_ref[...], ROWS_BY_COLUMNS).astype(BF)


def state_forward(own, states, pieces, cut, last_shard):
    tokens, width = states.shape
    units = pieces[0].shape[1]
    steps = 4
    return call(
        functools.partial(state_forward_kernel, cut, last_shard),
        "state_forward",
        (steps,),
        own[None],
        [pl.BlockSpec((tokens // steps, width), lambda i, _: (i, 0))] + [ANYWHERE] * 8,
        [pl.BlockSpec((tokens // steps, units), lambda i, _: (i, 0)), whole((width, units))],
        [like(tokens, units, BF), like(width, units, BF)],
        [states, *pieces],
        [pltpu.SemaphoreType.DMA((8,))],
        cost=BRIEF,
    )


def split_rows(total_ref, kept_ref, sent_ref, bit_value, order):
    parts = 1 << len(order)
    size = total_ref.shape[0] // parts
    for place in range(parts // 2):
        number = 0
        for depth, bit in enumerate(order[1:]):
            number += ((place >> (len(order) - 2 - depth)) & 1) << bit
        here = slice(place * size, (place + 1) * size)
        mine = pl.multiple_of((number + (bit_value << order[0])) * size, size)
        other = pl.multiple_of((number + ((1 - bit_value) << order[0])) * size, size)
        kept_ref[here, :] = total_ref[pl.ds(mine, size), :]
        sent_ref[here, :] = total_ref[pl.ds(other, size), :].astype(BF)


def critic_kernel(pairs, first_pair, layers, first_call, last_call, _, *refs):
    key_ref, target_ref, states_ref, hidden_ref, vectors_ref, out_weight_ref = refs[:6]
    refs = refs[6:]
    goal_refs, refs = refs[: 2 * pairs], refs[2 * pairs :]
    if not first_call:
        shares_before_ref, sums_before_ref = refs[:2]
        refs = refs[3:]
    first_refs, refs = refs[: 2 * pairs], refs[2 * pairs :]
    all_first_ref, refs = refs[0], refs[1:]
    if last_call:
        total_ref, refs = refs[0], refs[1:]
    else:
        shares_ref, sums_ref = refs[:2]
        refs = refs[2:]
    work, nhat, slope, spread, acts, low_grad = refs[:6]
    if last_call:
        sums_ref = refs[6]
        share_at = lambda layer: total_ref.at[:, layer * work.shape[1] : (layer + 1) * work.shape[1]]
    else:
        share_at = lambda layer: shares_ref.at[layer]
    step = pl.program_id(0)
    rows, units = work.shape
    half = rows // 2
    tokens = key_ref.shape[1]
    steps = rows // STEP

    @pl.when(step == 0)
    def _():
        for layer in range(layers - 1):
            if first_call:
                share_at(layer)[...] = jnp.zeros((units, units), F32)
            else:
                share_at(layer)[...] = shares_before_ref[layer]
        sums_ref[...] = jnp.zeros_like(sums_ref) if first_call else sums_before_ref[...]

    for pair in range(pairs):

        @pl.when(step == pair)
        def _():
            low_grad[0:half, :] = goal_refs[2 * pair][...]
            low_grad[half:rows, :] = goal_refs[2 * pair + 1][...]

    base = (first_pair + step) * rows
    slot = base + lax.broadcasted_iota(I32, (rows, tokens), 0)
    pick = (slot == key_ref[...]).astype(F32).astype(BF)
    work[...] = dot(pick, states_ref[...], ROWS_BY_COLUMNS) + low_grad[...].astype(F32)

    for layer in range(layers):
        gain = vectors_ref[layer : layer + 1, :]
        shift = vectors_ref[layers + layer : layers + layer + 1, :]
        for i in range(steps):
            here = slice(i * STEP, (i + 1) * STEP)
            values = work[here, :]
            center = values - jnp.mean(values, axis=1, keepdims=True)
            inverse = lax.rsqrt(jnp.mean(center * center, axis=1, keepdims=True) + 1e-05)
            scaled = center * inverse
            shifted = scaled * gain + shift
            slopes = jnp.exp(jnp.minimum(shifted, 0.0))
            nhat[layer, here, :] = scaled
            slope[layer, here, :] = slopes
            spread[layer, here, :] = inverse
            acts[layer, here, :] = (jnp.maximum(shifted, 0.0) + (slopes - 1.0)).astype(BF)
        if layer < layers - 1:
            work[...] = dot(acts[layer], hidden_ref[layer], ROWS_BY_COLUMNS)

    out_weight = out_weight_ref[...]
    last = acts[layers - 1]
    value = dot(out_weight, last, BY_ROWS)
    target = target_ref[0]
    error = (value[0:1, :] - target[0:1, :]) * target[1:2, :]
    grad_value = (error * target[2:3, :]).astype(BF)
    grad_rows = jnp.concatenate([grad_value.astype(F32), jnp.zeros((7, rows), F32)], axis=0).astype(BF)
    sums_ref[2 * layers] += dot(grad_rows, last, ROWS_BY_COLUMNS)
    sums_ref[2 * layers + 1] += jnp.broadcast_to(jnp.sum(error * error, axis=1, keepdims=True), (8, units))
    work[...] = dot(grad_rows, out_weight, OVER_ROWS)

    for layer in reversed(range(layers)):
        gain = vectors_ref[layer : layer + 1, :]
        for i in range(steps):
            here = slice(i * STEP, (i + 1) * STEP)
            scaled = nhat[layer, here, :]
            grad_norm = work[here, :] * slope[layer, here, :]
            by_scaled = grad_norm * scaled
            sums_ref[layer] += jnp.sum(by_scaled.reshape(STEP // 8, 8, units), axis=0)
            sums_ref[layers + layer] += jnp.sum(grad_norm.reshape(STEP // 8, 8, units), axis=0)
            grad_scaled = grad_norm * gain
            first_mean = jnp.mean(grad_scaled, axis=1, keepdims=True)
            second_mean = jnp.mean(by_scaled * gain, axis=1, keepdims=True)
            grad = spread[layer, here, :] * (grad_scaled - first_mean - scaled * second_mean)
            low_grad[here, :] = grad.astype(BF)
        if layer > 0:
            grads = low_grad[...]
            work[...] = dot(grads, hidden_ref[layer - 1], BY_ROWS)
            share_at(layer - 1)[...] += dot(grads, acts[layer - 1], OVER_ROWS)

    all_first_ref[...] = low_grad[...]
    for pair in range(pairs):

        @pl.when(step == pair)
        def _():
            first_refs[2 * pair][...] = low_grad[0:half, :]
            first_refs[2 * pair + 1][...] = low_grad[half:rows, :]

    if last_call:

        @pl.when(step == pairs - 1)
        def _():
            count = 2 * layers + 2
            sums = jnp.concatenate(
                [jnp.sum(sums_ref[row], axis=0, keepdims=True) for row in range(count - 1)]
                + [sums_ref[count - 1][0:1, :]],
                axis=0,
            )
            high = sums.astype(BF).astype(F32)
            columns = jnp.concatenate([high, sums - high, jnp.zeros((128 - 2 * count, units), F32)], axis=0)
            total_ref[:, (layers - 1) * units :] = columns.T


def critic(own, key_row, targets, state_part, hidden, vectors, out_weight, goal_parts, tiles, before, last_call):
    pairs, first_pair = len(tiles) // 2, tiles[0] // 2
    half, units = goal_parts[0].shape
    rows = 2 * half
    layers = hidden.shape[0] + 1
    width = (layers - 1) * units + 128
    sums_shape, shares_shape = (2 * layers + 2, 8, units), (layers - 1, units, units)
    operands = [key_row, targets, state_part, hidden, vectors, out_weight, *goal_parts]
    in_specs = [
        whole(key_row.shape),
        pl.BlockSpec((1,) + targets.shape[1:], lambda i, _: (first_pair + i, 0, 0)),
        whole(state_part.shape),
        whole(hidden.shape),
        whole(vectors.shape),
        whole(out_weight.shape),
    ] + [whole((half, units))] * (2 * pairs)
    aliases = {}
    if before is not None:
        in_specs += [whole(shares_shape), whole(sums_shape), ANYWHERE]
        operands += list(before)
        aliases = {len(operands): 2 * pairs}
    out_shape = [like(half, units, BF)] * (2 * pairs) + [like(TILES * half, units, BF)]
    out_specs = [whole((half, units))] * (2 * pairs) + [
        pl.BlockSpec((rows, units), lambda i, _: (first_pair + i, 0))
    ]
    scratch = [
        pltpu.VMEM((rows, units), F32),
        pltpu.VMEM((layers, rows, units), F32),
        pltpu.VMEM((layers, rows, units), F32),
        pltpu.VMEM((layers, rows, 1), F32),
        pltpu.VMEM((layers, rows, units), BF),
        pltpu.VMEM((rows, units), BF),
    ]
    if last_call:
        shapes = [like(units, width, F32)]
        scratch += [pltpu.VMEM(sums_shape, F32)]
    else:
        shapes = [like(*shares_shape, F32), like(*sums_shape, F32)]
    return call(
        functools.partial(critic_kernel, pairs, first_pair, layers, before is None, last_call),
        "critic",
        (pairs,),
        own[None],
        in_specs,
        out_specs + [whole(shape.shape) for shape in shapes],
        out_shape + shapes,
        operands,
        scratch,
        aliases,
    )


def state_weight_kernel(split, core_ref, key_ref, first_ref, states_ref, rest_ref, grad_ref, *refs):
    step = pl.program_id(0)
    slots = first_ref.shape[0]
    width = states_ref.shape[1]
    slot = lax.broadcasted_iota(I32, (key_ref.shape[0], slots), 1)
    pick = (slot == key_ref[...]).astype(F32).astype(BF)
    grad = dot(pick, first_ref[...], ROWS_BY_COLUMNS).astype(BF)
    grad_ref[...] = grad
    total_ref = refs[-1]
    share = dot(grad, states_ref[...], OVER_ROWS)

    @pl.when(step == 0)
    def _():
        total_ref[...] = share

    @pl.when(step > 0)
    def _():
        total_ref[...] += share

    @pl.when(step == pl.num_programs(0) - 1)
    def _():
        if split:
            for start, source in ((0, total_ref), (width, rest_ref)):
                here = slice(start, start + source.shape[1])
                split_rows(source, refs[0].at[:, here], refs[1].at[:, here], core_ref[0], FIRST_ORDER)
        else:
            refs[0][:, 0:width] = total_ref[...]
            refs[0][:, width:] = rest_ref[...]


def state_weight_grad(core_bit, key_column, first, states, rest, split):
    tokens, width = states.shape
    units = first.shape[1]
    steps = 4
    columns = width + rest.shape[1]
    shapes = [like(units // 2, columns, F32), like(units // 2, columns, BF)] if split else [like(units, columns, F32)]
    return call(
        functools.partial(state_weight_kernel, split),
        "state_weight_grad",
        (steps,),
        core_bit[None],
        [
            pl.BlockSpec((tokens // steps, 1), lambda i, _: (i, 0)),
            whole(first.shape),
            pl.BlockSpec((tokens // steps, width), lambda i, _: (i, 0)),
            whole(rest.shape),
        ],
        [pl.BlockSpec((tokens // steps, units), lambda i, _: (i, 0))] + [whole(shape.shape) for shape in shapes],
        [like(tokens, units, BF)] + shapes,
        [key_column, first, states, rest],
        [pltpu.VMEM((units, width), F32)],
    )


def state_grad_kernel(_, grad_ref, weight_ref, out_ref):
    out_ref[...] = dot(grad_ref[...], weight_ref[...], BY_ROWS).astype(BF)


def state_grad(own, grad, weight):
    tokens, units = grad.shape
    width = weight.shape[0]
    steps = 4
    return call(
        state_grad_kernel,
        "state_grad",
        (steps,),
        own[None],
        [pl.BlockSpec((tokens // steps, units), lambda i, _: (i, 0)), whole(weight.shape)],
        [pl.BlockSpec((tokens // steps, width), lambda i, _: (i, 0))],
        [like(tokens, width, BF)],
        [grad, weight],
    )[0]


def goal_backward_kernel(count, with_grad, with_sum, has_before, last_call, scalars_ref, *refs):
    grad_refs, refs = refs[:count], refs[count:]
    if with_sum:
        goals_ref, refs = refs[0], refs[1:]
    if with_grad:
        weight_ref, refs = refs[0], refs[1:]
    if has_before:
        before_ref, refs = refs[0], refs[1:]
    if with_grad:
        out_ref, refs = refs[0], refs[1:]
    step = pl.program_id(0)
    grad_scratch, refs = refs[-1], refs[:-1]
    for place in range(count):

        @pl.when(step == place)
        def _():
            grad_scratch[...] = grad_refs[place][...]

    grad = grad_scratch[...]
    if with_sum:
        share = dot(grad, goals_ref[...], OVER_ROWS)
        sum_ref = refs[-1]

        @pl.when(step == 0)
        def _():
            if has_before:
                sum_ref[...] = before_ref[...] + share
            else:
                sum_ref[...] = share

        @pl.when(step > 0)
        def _():
            sum_ref[...] += share

    if with_grad:
        out_ref[...] = dot(grad, weight_ref[...], BY_ROWS).astype(BF)
    if last_call:

        @pl.when(step == count - 1)
        def _():
            split_rows(sum_ref, refs[0], refs[1], scalars_ref[count], FIRST_ORDER)


def goal_backward(own_tile, core_bit, grads, goals, weight, tiles, with_grad, with_sum, before=None, split=False):
    rows, width, units = goals.shape[0] // TILES, goals.shape[1], weight.shape[1]
    scalars = jnp.concatenate([jnp.array(tiles, I32) ^ own_tile, core_bit[None]])
    count = len(tiles)
    by_tile = pl.BlockSpec((rows, width), lambda i, scalars: (scalars[i], 0))
    in_specs, operands = [whole((rows, units))] * count, [*grads]
    out_specs, shapes, aliases, scratch = [], [], {}, []
    if with_sum:
        in_specs.append(by_tile)
        operands.append(goals)
    if with_grad:
        in_specs.append(whole(weight.shape))
        operands.append(weight)
        out_specs.append(by_tile)
        shapes.append(like(*goals.shape, BF))
    if before is not None:
        in_specs.append(whole((units, width)) if with_sum else ANYWHERE)
        operands.append(before)
        if not with_sum:
            aliases = {len(operands): 0}
    if with_sum and split:
        shapes += [like(units // 2, width, F32), like(units // 2, width, BF)]
        out_specs += [whole(shape.shape) for shape in shapes[-2:]]
        scratch.append(pltpu.VMEM((units, width), F32))
    elif with_sum:
        shapes.append(like(units, width, F32))
        out_specs.append(whole((units, width)))
    return call(
        functools.partial(goal_backward_kernel, count, with_grad, with_sum, before is not None, split),
        "goal_backward",
        (count,),
        scalars,
        in_specs,
        out_specs,
        shapes,
        operands,
        scratch + [pltpu.VMEM((rows, units), BF)],
        aliases,
    )


def fold_kernel(_, kept_mine_ref, got_mine_ref, kept_other_ref, got_other_ref, kept_ref, sent_ref):
    kept_ref[...] = kept_mine_ref[...] + got_mine_ref[...].astype(F32)
    sent_ref[...] = (kept_other_ref[...] + got_other_ref[...].astype(F32)).astype(BF)


def fold(kept, got, bit_value):
    rows, width = kept.shape[0] // 2, kept.shape[1]
    block = min(rows, 64)
    steps = rows // block
    mine = pl.BlockSpec((block, width), lambda i, bit: (bit[0] * steps + i, 0))
    other = pl.BlockSpec((block, width), lambda i, bit: ((1 - bit[0]) * steps + i, 0))
    straight = pl.BlockSpec((block, width), lambda i, bit: (i, 0))
    return call(
        fold_kernel,
        "fold",
        (steps,),
        bit_value[None],
        [mine, mine, other, other],
        [straight, straight],
        [like(rows, width, F32), like(rows, width, BF)],
        [kept, got, kept, got],
    )


def spread_kernel(count, own_ref, *refs):
    kept_refs, got_refs, out_refs = refs[:2], refs[2:4], refs[4:]
    own = own_ref[0]
    size = kept_refs[0].shape[0] // count
    for offset in range(count):
        here = pl.ds(pl.multiple_of((own ^ offset) * size, size), size)
        start = 0
        for kept_ref, got_ref in zip(kept_refs, got_refs):
            total = kept_ref[here, :] + got_ref[here, :].astype(F32)
            out_refs[offset][:, start : start + total.shape[1]] = total.astype(out_refs[offset].dtype)
            start += total.shape[1]


def finish_kernel(widths, count, _, own_ref, *refs):
    total = own_ref[...]
    for got_ref in refs[: count - 1]:
        total = total + got_ref[...].astype(F32)
    first_ref, hidden_ref, rest_ref = refs[count - 1 :]
    layers, _, units = hidden_ref.shape
    feat_width, goal_width = widths
    first_ref[:, 0:feat_width] = total[:, 0:feat_width]
    first_ref[:, feat_width:] = total[:, total.shape[1] - goal_width :]
    for layer in range(layers):
        start = feat_width + layer * units
        hidden_ref[layer] = total[:, start : start + units]
    rest_ref[...] = total[:, feat_width + layers * units : total.shape[1] - goal_width]


def swap_bit(block, bit, dp_count, mp_count):
    if bit < 2:
        return lax.ppermute(block, "mp", xor_pairs(mp_count, 1 << bit))
    return lax.ppermute(block, "dp", xor_pairs(dp_count, 1 << (bit - 2)))


def sum_plain(partial, dp_count):
    return lax.psum_scatter(partial, ("dp", "mp"), scatter_dimension=0, tiled=True)


def across(block, tile, dp_count):
    per = dp_count // TILES
    moved = block if tile == 0 else lax.ppermute(block, "dp", xor_pairs(dp_count, tile * per))
    if per == 1:
        return moved
    groups = [[group * per + low for low in range(per)] for group in range(TILES)]
    parts = moved.reshape((per, block.shape[0] // per) + block.shape[1:])
    parts = lax.all_to_all(parts, "dp", 0, 0, axis_index_groups=groups, tiled=True)
    return parts.reshape(block.shape)


def shards(
    states, dest_device, goals, returns, weight_in, weight_hidden, norm_gain, norm_shift, weight_out
):
    dp_count, mp_count = lax.axis_size("dp"), lax.axis_size("mp")
    own_dp, own_mp = lax.axis_index("dp"), lax.axis_index("mp")
    number = own_dp * mp_count + own_mp
    core_bit = number & 1
    tokens, feat_width = states.shape
    all_rows = tokens * dp_count * mp_count
    slot_count, goal_width = goals.shape
    capacity = slot_count // dp_count
    shard_in, units = weight_in.shape
    layers = norm_gain.shape[0]
    shard_units = norm_gain.shape[1]
    per = dp_count // TILES
    rows = slot_count // TILES
    own_tile = own_dp // per
    single = per == 1
    swap, cross = xor_pairs(4, 1), xor_pairs(4, 2)

    small = jnp.concatenate([norm_gain, norm_shift, weight_out[None, :]], axis=0)
    small = jnp.pad(small.reshape(-1), (0, 16 * units - small.size)).reshape(16, units)
    others = jnp.concatenate([weight_hidden.reshape((layers - 1) * shard_units, units), small], axis=0)
    other_rows = others.shape[0]
    if single:
        key_row, key_column, message = route(
            own_dp, dest_device.reshape(1, tokens), returns.reshape(dp_count, capacity), units
        )
    else:
        dest = dest_device[:, 0]
        offset = ((dest // per) ^ own_tile) * per + dest % per
        blocks = tokens // 128
        marks = (offset[None, :] == jnp.arange(dp_count, dtype=I32)[:, None]).astype(F32)
        marks = marks.reshape(dp_count, blocks, 128)
        upper = jnp.arange(128)[:, None] < jnp.arange(128)[None, :]
        within = dot(marks.astype(BF), upper.astype(BF), ((2,), (0,)))
        block_sums = jnp.sum(marks, axis=2)
        earlier = jnp.arange(blocks)[None, :] < jnp.arange(blocks)[:, None]
        ahead = jnp.sum(jnp.where(earlier[None], block_sums[:, None, :], 0.0), axis=2)
        rank = jnp.sum(marks * (within + ahead[:, :, None]), axis=0).reshape(tokens)
        key = offset * capacity + rank.astype(I32)
        key_row, key_column = key[None, :], key[:, None]
        valid = jnp.arange(capacity, dtype=F32)[None, :] < jnp.sum(block_sums, axis=1)[:, None]
        tile_returns = returns.reshape(TILES, rows)
        got_returns = [
            across(lax.dynamic_index_in_dim(tile_returns, own_tile ^ t, 0, keepdims=False), t, dp_count)
            for t in range(TILES)
        ]
        got_returns = jnp.stack(got_returns).reshape(dp_count, capacity).astype(F32)
        square_total = lax.psum(jnp.sum(jnp.where(valid, got_returns * got_returns, 0.0)), ("dp", "mp"))
        scale_value = jnp.sqrt(square_total / all_rows + 1e-06)
        targets = jnp.stack(
            [got_returns / scale_value, valid.astype(F32), jnp.full(valid.shape, 1.0 / all_rows, F32)]
            + [jnp.zeros(valid.shape, F32)] * 5
        )
        targets = targets.reshape(8, TILES // 2, 2 * rows).transpose(1, 0, 2)

    cut = feat_width % shard_in
    first_goal_shard = feat_width // shard_in
    head, tail = weight_in[:cut], weight_in[cut:]
    tail_two = lax.ppermute(tail, "mp", cross)
    one = lax.ppermute(weight_in, "mp", swap)
    odd_two = lax.ppermute(head, "mp", [(1, 3), (3, 1)])
    if single:
        messages = message
        for bit, ready in ((1, ()), (2, (tail_two, one)), (4, (odd_two,))):
            messages = after(messages, *ready)
            messages = jnp.concatenate([messages, lax.ppermute(messages, "dp", xor_pairs(dp_count, bit))], axis=0)
        others = jnp.concatenate([others, messages], axis=0)
    first_three = lax.ppermute(jnp.concatenate([tail_two, odd_two], axis=0), "mp", swap)
    tail_three, odd_three = first_three[: shard_in - cut], first_three[shard_in - cut :]
    even_two = lax.ppermute(head, "mp", [(0, 2), (2, 0)])
    even_three = lax.ppermute(even_two, "mp", [(0, 1), (2, 3)])
    others_two = lax.ppermute(others, "mp", cross)

    parts = {}
    tiles = (1, 2, 3, 4, 5)
    pieces = (weight_in, one, tail_two, tail_three, odd_two, odd_three)
    *made, goal_weight = goal_forward(own_tile, own_mp, goals, pieces, tiles, cut, first_goal_shard)
    parts.update(zip(tiles, made))
    others_two = after(others_two, goal_weight)
    others_pair = lax.ppermute(jnp.concatenate([others, others_two], axis=0), "mp", swap)
    size = others.shape[0]
    others_one, others_three = others_pair[:size], others_pair[size:]
    tiles = (6, 7, 0)
    parts.update(zip(tiles, goal_forward(own_tile, own_mp, goals, goal_weight, tiles)))
    parts = {tile: across(parts[tile], tile, dp_count) for tile in NEAR + FAR_ONE + FAR_TWO}

    pieces = pieces + (even_two, even_three)
    state_part, state_weight = state_forward(own_mp, states, pieces, cut, first_goal_shard)
    prepared = prepare(
        own_mp, [others, others_one, others_two, others_three], layers, other_rows, rows, float(all_rows)
    )
    hidden, vectors, out_weight = prepared[:3]
    if single:
        targets = prepared[3]

    running, back, made_of = None, {}, {}
    for tiles in (NEAR, FAR_ONE, FAR_TWO):
        made = critic(
            own_dp, key_row, targets, state_part, hidden, vectors, out_weight,
            [parts[t] for t in tiles], tiles, running, tiles == FAR_TWO,
        )
        running = (made[-2], made[-1], made[len(tiles)])
        made_of.update(zip(tiles, made))
        if tiles == FAR_ONE:
            for tile in NEAR + FAR_ONE:
                back[tile] = across(after(made_of[tile], made_of[FAR_ONE[0]], *[parts[u] for u in FAR_TWO]), tile, dp_count)
    for tile in FAR_TWO:
        back[tile] = across(after(made_of[tile], *[back[u] for u in NEAR + FAR_ONE]), tile, dp_count)
    first, rest = made[-2], made[-1]

    state_made = state_weight_grad(core_bit, key_column, first, states, rest, single)

    early = NEAR + FAR_ONE
    grad_goals, running_sum = goal_backward(
        own_tile, core_bit, [back[t] for t in early], goals, goal_weight, early, True, True
    )
    grad_states = state_grad(own_dp, after(state_made[0], running_sum), state_weight)
    goal_made = goal_backward(
        own_tile, core_bit, [back[t] for t in FAR_TWO], goals, goal_weight, FAR_TWO, False, True,
        after(running_sum, grad_states), single,
    )
    grad_goals = goal_backward(
        own_tile, core_bit, [after(back[t], goal_made[0]) for t in FAR_TWO], goals, goal_weight, FAR_TWO, True, False,
        grad_goals,
    )[0]

    share = units // (dp_count * mp_count)
    if single:
        folded = []
        kept, sent = state_made[1:]
        sent = after(sent, *[back[t] for t in NEAR + FAR_ONE])
        for kept, sent in ((kept, sent), goal_made):
            kept, sent = fold(kept, swap_bit(sent, CORE, dp_count, mp_count), (number >> Y) & 1)
            folded.append((kept, swap_bit(sent, Y, dp_count, mp_count)))
        (states_kept, states_got), (goals_kept, goals_got) = folded
        columns = states_kept.shape[1] + goals_kept.shape[1]
        operands = [states_kept, goals_kept, states_got, goals_got]
        blocks = call(
            functools.partial(spread_kernel, dp_count), "spread", (1,), own_dp[None],
            [whole(operand.shape) for operand in operands],
            [whole((share, columns))] * dp_count,
            [like(share, columns, F32)] + [like(share, columns, BF)] * (dp_count - 1),
            operands,
        )
        arrived = [lax.ppermute(blocks[o], "dp", xor_pairs(dp_count, o)) for o in range(1, dp_count)]
        shapes = [
            like(share, feat_width + goal_width, F32), like(layers - 1, share, units, F32), like(share, 128, F32),
        ]
        first_share, hidden_share, rest = call(
            functools.partial(finish_kernel, (feat_width, goal_width), dp_count), "finish", (1,), core_bit[None],
            [whole((share, columns))] * dp_count,
            [whole(shape.shape) for shape in shapes],
            shapes,
            [blocks[0], *arrived],
        )
    else:
        total = sum_plain(state_made[1], dp_count)
        hidden_share = total[:, feat_width : feat_width + (layers - 1) * units]
        hidden_share = hidden_share.reshape(share, layers - 1, units).transpose(1, 0, 2)
        rest = total[:, feat_width + (layers - 1) * units :]
        first_share = jnp.concatenate([total[:, :feat_width], sum_plain(goal_made[0], dp_count)], axis=1)

    count = 2 * layers + 2
    rest = (rest[:, :count] + rest[:, count : 2 * count]).T
    return (
        0.5 * rest[count - 1, 0] / all_rows,
        grad_states,
        grad_goals,
        first_share.T,
        hidden_share.transpose(0, 2, 1),
        rest[:layers],
        rest[layers : 2 * layers],
        rest[2 * layers],
    )


def solution(mesh):
    placed = (
        P(("dp", "mp"), None),
        P(("dp", "mp"), None),
        P(("dp", "mp"), None),
        P(("dp", "mp")),
        P("mp", None),
        P(None, "mp", None),
        P(None, "mp"),
        P(None, "mp"),
        P("mp"),
    )
    return jax.shard_map(
        shards,
        mesh=mesh,
        in_specs=placed,
        out_specs=(
            P(),
            P(("dp", "mp"), None),
            P(("dp", "mp"), None),
            P(None, ("dp", "mp")),
            P(None, None, ("dp", "mp")),
            P(None, ("dp", "mp")),
            P(None, ("dp", "mp")),
            P(("dp", "mp")),
        ),
        check_vma=False,
    )
```

```python
import functools

import jax
import jax.numpy as jnp
from jax import lax
from jax.experimental import pallas as pl
from jax.experimental.pallas import tpu as pltpu
from jax.sharding import PartitionSpec as P

BF = jnp.bfloat16
F32 = jnp.float32
I32 = jnp.int32
TILES = 8
STEP = 64
VMEM = 63 * 1024 * 1024
NEAR, FAR_ONE, FAR_TWO = (0, 1, 2, 3), (4, 5), (6, 7)
BRIEF = pl.CostEstimate(flops=1, bytes_accessed=1, transcendentals=0)
LONG = pl.CostEstimate(flops=20_000_000_000, bytes_accessed=10_000_000, transcendentals=0)
CORE, Y, X, Z_LOW, Z_HIGH = range(5)
FIRST_ORDER = (CORE, Y, Z_HIGH, Z_LOW, X)


def dot(first, second, dims):
    return lax.dot_general(first, second, (dims, ((), ())), preferred_element_type=F32)


ROWS_BY_COLUMNS, BY_ROWS, OVER_ROWS = ((1,), (0,)), ((1,), (1,)), ((0,), (0,))


def after(value, *others):
    return lax.optimization_barrier((value, *others))[0]


def xor_pairs(count, bits):
    return [(i, i ^ bits) for i in range(count)]


def like(*shape_and_type):
    *shape, dtype = shape_and_type
    return jax.ShapeDtypeStruct(tuple(shape), dtype)


def whole(shape):
    return pl.BlockSpec(tuple(shape), lambda *_: (0,) * len(shape))


ANYWHERE = pl.BlockSpec(memory_space=pl.ANY)


def call(kernel, name, grid, scalars, in_specs, out_specs, out_shape, operands, scratch=(), aliases=None, cost=BRIEF):
    return pl.pallas_call(
        kernel,
        out_shape=out_shape,
        grid_spec=pltpu.PrefetchScalarGridSpec(
            num_scalar_prefetch=1,
            grid=grid,
            in_specs=in_specs,
            out_specs=out_specs,
            scratch_shapes=list(scratch),
        ),
        input_output_aliases=aliases or {},
        compiler_params=pltpu.CompilerParams(vmem_limit_bytes=VMEM),
        cost_estimate=cost,
        name=name,
    )(scalars, *operands)


def route_kernel(capacity, own_ref, dest_ref, returns_ref, row_ref, column_ref, message_ref, wide, text):
    own = own_ref[0]
    tokens = dest_ref.shape[1]
    count = returns_ref.shape[0]
    blocks = tokens // 128
    offsets = dest_ref[...] ^ own
    marks = (lax.broadcasted_iota(I32, (count, tokens), 0) == offsets).astype(F32)
    stacked = jnp.concatenate([marks[:, 128 * b : 128 * b + 128] for b in range(blocks)], axis=0)
    upper = lax.broadcasted_iota(I32, (128, 128), 0) < lax.broadcasted_iota(I32, (128, 128), 1)
    within = dot(stacked.astype(BF), upper.astype(F32).astype(BF), ROWS_BY_COLUMNS)
    totals = jnp.sum(stacked, axis=1, keepdims=True)
    ahead = jnp.zeros((count, 1), F32)
    for b in range(blocks):
        part = slice(count * b, count * b + count)
        lanes = slice(128 * b, 128 * b + 128)
        rank = jnp.sum(stacked[part] * (within[part] + ahead), axis=0, keepdims=True)
        key = offsets[:, lanes].astype(F32) * capacity + rank
        row_ref[:, lanes] = key.astype(I32)
        column_ref[lanes, :] = jnp.broadcast_to(key, (128, 128)).T[:, 0:1].astype(I32)
        ahead = ahead + totals[part]
    wide[...] = returns_ref[...].astype(F32)
    lane = lax.broadcasted_iota(I32, text.shape, 1) - (text.shape[1] - 128)
    high = jnp.floor(ahead * 0.0625)
    text[...] = jnp.where(lane == 0, high, jnp.where(lane == 1, ahead - 16.0 * high, 0.0))
    for offset in range(count):
        text[offset : offset + 1, 0:capacity] = wide[pl.ds(own ^ offset, 1), :]
    message_ref[...] = text[...].astype(BF)


def route(own, dest_row, returns, units):
    tokens, (count, capacity) = dest_row.shape[1], returns.shape
    return call(
        functools.partial(route_kernel, capacity),
        "route",
        (1,),
        own[None],
        [whole(dest_row.shape), whole(returns.shape)],
        [whole((1, tokens)), whole((tokens, 1)), whole((count, units))],
        [like(1, tokens, I32), like(tokens, 1, I32), like(count, units, BF)],
        [dest_row, returns],
        [pltpu.VMEM(returns.shape, F32), pltpu.VMEM((count, units), F32)],
    )


def reverse(bits):
    return (bits % 2) * 4 + (bits // 2 % 2) * 2 + bits // 4


def prepare_kernel(layers, rows, capacity, total_rows, own_ref, *refs):
    pieces, refs = refs[:4], refs[4:]
    hidden_ref, vectors_ref, out_weight_ref = refs[:3]
    own = own_ref[0]
    width = hidden_ref.shape[2] // 4
    for shard in range(4):
        columns = slice(shard * width, (shard + 1) * width)
        for value in range(4):

            @pl.when(own == value)
            def _():
                piece = pieces[shard ^ value]
                for layer in range(layers - 1):
                    hidden_ref[layer, columns, :] = piece[layer * width : (layer + 1) * width, :]
                start = (layers - 1) * width
                small = piece[start : start + 16, :].astype(F32)
                for row in range(2 * layers + 1):
                    vectors_ref[row : row + 1, columns] = small[
                        row // 4 : row // 4 + 1, (row % 4) * width : (row % 4 + 1) * width
                    ]

    vectors_ref[2 * layers + 1 :, :] = jnp.zeros((16 - 2 * layers - 1, vectors_ref.shape[1]), F32)
    out_weight_ref[...] = jnp.concatenate(
        [vectors_ref[2 * layers : 2 * layers + 1, :], jnp.zeros((7, vectors_ref.shape[1]), F32)], axis=0
    ).astype(BF)
    if len(refs) == 3:
        return
    targets_ref = refs[3]
    targets_ref[...] = jnp.zeros_like(targets_ref)
    index = lax.broadcasted_iota(I32, (64, 64), 0)
    partner = (reverse(reverse(index // 8) ^ (index % 8))) * 8 + index % 8
    swap = (lax.broadcasted_iota(I32, (64, 64), 1) == partner).astype(F32).astype(BF)
    lane = lax.broadcasted_iota(I32, (64, 128 * 3), 1).astype(F32)
    total = jnp.zeros((1, 1), F32)
    for piece in pieces:
        message = piece[rows : rows + 64, :]
        counts = dot(swap, message[:, 384:512], ROWS_BY_COLUMNS)
        counts = counts[:, 0:1] * 16.0 + counts[:, 1:2]
        values = message[:, 0:384].astype(F32)
        squares = jnp.sum(jnp.where(lane < counts, values * values, 0.0), axis=1, keepdims=True)
        total = total + jnp.sum(squares, axis=0, keepdims=True)
    scale = jnp.sqrt(total / total_rows + 1e-06)
    message = pieces[0][rows : rows + 64, :].astype(F32)
    counts = message[0:8, 384:385] * 16.0 + message[0:8, 385:386]
    for tile in range(TILES):
        lanes = slice((tile % 2) * capacity, (tile % 2) * capacity + capacity)
        row = reverse(tile) * 8 + tile
        target = message[row : row + 1, 0:384] / scale
        filled = (lane[0:1] < counts[tile : tile + 1]).astype(F32)
        targets_ref[tile // 2, 0:1, lanes] = target[:, 0:capacity]
        targets_ref[tile // 2, 1:2, lanes] = filled[:, 0:capacity]
        targets_ref[tile // 2, 2:3, lanes] = jnp.full((1, capacity), 1.0 / total_rows, F32)


def prepare(own, pieces, layers, rows, capacity, total_rows):
    units = pieces[0].shape[1]
    shapes = [like(layers - 1, units, units, BF), like(16, units, F32), like(8, units, BF)]
    if pieces[0].shape[0] > rows:
        shapes.append(like(TILES // 2, 8, 2 * capacity, F32))
    return call(
        functools.partial(prepare_kernel, layers, rows, capacity, total_rows),
        "prepare",
        (1,),
        own[None],
        [whole(piece.shape) for piece in pieces],
        [whole(shape.shape) for shape in shapes],
        shapes,
        pieces,
    )


def fetch(own, parts, target_ref, sems, later=()):
    place = 0
    for number, (shard, candidates) in enumerate(parts):
        size = candidates[0].shape[0]
        there = target_ref.at[place : place + size]
        for value in range(4):

            @pl.when(own == value)
            def _():
                pltpu.make_async_copy(candidates[shard ^ value], there, sems.at[number]).start()

        place += size
    for copy in later:
        copy.start()
    place = 0
    for number, (shard, candidates) in enumerate(parts):
        size = candidates[0].shape[0]
        there = target_ref.at[place : place + size]
        pltpu.make_async_copy(candidates[0], there, sems.at[number]).wait()
        place += size


def first_weight_parts(pieces, cut, shards, first, last):
    parts = []
    for shard in shards:
        here = slice(cut if shard == first else 0, cut if shard == last else pieces[0].shape[0])
        parts.append((shard, [piece.at[here] for piece in pieces]))
    return parts


def goal_forward_kernel(cut, first_shard, scalars_ref, goals_ref, *refs):
    pieces, refs = refs[:4], refs[4:]
    out_refs, weight_ref, refs = refs[:TILES], refs[TILES], refs[TILES + 1 :]
    goals, made, sems, out_sems, fetch_sems = refs
    rows = goals_ref.shape[0] // TILES
    copies = []
    for place in range(TILES):
        there = goals_ref.at[pl.ds(pl.multiple_of((scalars_ref[0] ^ place) * rows, rows), rows)]
        copies.append(pltpu.make_async_copy(there, goals.at[place], sems.at[place]))
    order = [*NEAR[1:], *FAR_ONE, *FAR_TWO, 0]
    copies[order[0]].start()
    parts = first_weight_parts(pieces, cut, range(first_shard, 4), first_shard, None)
    fetch(scalars_ref[1], parts, weight_ref, fetch_sems, [copies[place] for place in order[1:]])
    sent = []
    for place in order:
        copies[place].wait()
        made[place] = dot(goals[place], weight_ref[...], ROWS_BY_COLUMNS).astype(BF)
        sent.append(pltpu.make_async_copy(made.at[place], out_refs[place], out_sems.at[place]))
        sent[-1].start()
    for copy in sent:
        copy.wait()


def goal_forward(own_tile, own_mp, goals, pieces, cut, first_shard):
    rows, width = goals.shape[0] // TILES, goals.shape[1]
    units = pieces[0].shape[1]
    return call(
        functools.partial(goal_forward_kernel, cut, first_shard),
        "goal_forward",
        (1,),
        jnp.stack([own_tile, own_mp]),
        [ANYWHERE] * 5,
        [ANYWHERE] * TILES + [whole((width, units))],
        [like(rows, units, BF)] * TILES + [like(width, units, BF)],
        [goals, *pieces],
        [
            pltpu.VMEM((TILES, rows, width), BF),
            pltpu.VMEM((TILES, rows, units), BF),
            pltpu.SemaphoreType.DMA((TILES,)),
            pltpu.SemaphoreType.DMA((TILES,)),
            pltpu.SemaphoreType.DMA((4,)),
        ],
    )


def state_forward_kernel(steps, cut, last_shard, own_ref, states_ref, *refs):
    pieces, (out_ref, weight_ref, states, sems, fetch_sems) = refs[:4], refs[4:]
    rows = states.shape[1]
    copies = [
        pltpu.make_async_copy(states_ref.at[step * rows : (step + 1) * rows], states.at[step], sems.at[step])
        for step in range(steps)
    ]
    copies[0].start()
    parts = first_weight_parts(pieces, cut, range(last_shard + 1), None, last_shard)
    fetch(own_ref[0], parts, weight_ref, fetch_sems, copies[1:])
    for step in range(steps):
        copies[step].wait()
        here = slice(step * rows, (step + 1) * rows)
        out_ref[here, :] = dot(states[step], weight_ref[...], ROWS_BY_COLUMNS).astype(BF)


def state_forward(own, states, pieces, cut, last_shard):
    tokens, width = states.shape
    units = pieces[0].shape[1]
    steps = 4
    return call(
        functools.partial(state_forward_kernel, steps, cut, last_shard),
        "state_forward",
        (1,),
        own[None],
        [ANYWHERE] * 5,
        [whole((tokens, units)), whole((width, units))],
        [like(tokens, units, BF), like(width, units, BF)],
        [states, *pieces],
        [
            pltpu.VMEM((steps, tokens // steps, width), BF),
            pltpu.SemaphoreType.DMA((steps,)),
            pltpu.SemaphoreType.DMA((4,)),
        ],
    )


def split_rows(total_ref, kept_ref, sent_ref, bit_value, order):
    parts = 1 << len(order)
    size = total_ref.shape[0] // parts
    for place in range(parts // 2):
        number = 0
        for depth, bit in enumerate(order[1:]):
            number += ((place >> (len(order) - 2 - depth)) & 1) << bit
        here = slice(place * size, (place + 1) * size)
        mine = pl.multiple_of((number + (bit_value << order[0])) * size, size)
        other = pl.multiple_of((number + ((1 - bit_value) << order[0])) * size, size)
        kept_ref[here, :] = total_ref[pl.ds(mine, size), :]
        sent_ref[here, :] = total_ref[pl.ds(other, size), :].astype(BF)


def critic_kernel(pairs, first_pair, layers, first_call, last_call, _, *refs):
    key_ref, target_ref, states_ref, hidden_ref, vectors_ref, out_weight_ref = refs[:6]
    refs = refs[6:]
    goal_refs, refs = refs[: 2 * pairs], refs[2 * pairs :]
    if not first_call:
        shares_before_ref, sums_before_ref = refs[:2]
        refs = refs[3:]
    first_refs, refs = refs[: 2 * pairs], refs[2 * pairs :]
    all_first_ref, refs = refs[0], refs[1:]
    if last_call:
        total_ref, refs = refs[0], refs[1:]
    else:
        shares_ref, sums_ref = refs[:2]
        refs = refs[2:]
    work, nhat, slope, spread, acts, low_grad = refs[:6]
    if last_call:
        sums_ref = refs[6]
        share_at = lambda layer: total_ref.at[:, layer * work.shape[1] : (layer + 1) * work.shape[1]]
    else:
        share_at = lambda layer: shares_ref.at[layer]
    step = pl.program_id(0)
    rows, units = work.shape
    half = rows // 2
    tokens = key_ref.shape[1]
    steps = rows // STEP

    @pl.when(step == 0)
    def _():
        for layer in range(layers - 1):
            if first_call:
                share_at(layer)[...] = jnp.zeros((units, units), F32)
            else:
                share_at(layer)[...] = shares_before_ref[layer]
        sums_ref[...] = jnp.zeros_like(sums_ref) if first_call else sums_before_ref[...]

    for pair in range(pairs):

        @pl.when(step == pair)
        def _():
            low_grad[0:half, :] = goal_refs[2 * pair][...]
            low_grad[half:rows, :] = goal_refs[2 * pair + 1][...]

    base = (first_pair + step) * rows
    slot = base + lax.broadcasted_iota(I32, (rows, tokens), 0)
    pick = (slot == key_ref[...]).astype(F32).astype(BF)
    work[...] = dot(pick, states_ref[...], ROWS_BY_COLUMNS) + low_grad[...].astype(F32)

    for layer in range(layers):
        gain = vectors_ref[layer : layer + 1, :]
        shift = vectors_ref[layers + layer : layers + layer + 1, :]
        for i in range(steps):
            here = slice(i * STEP, (i + 1) * STEP)
            values = work[here, :]
            center = values - jnp.mean(values, axis=1, keepdims=True)
            inverse = lax.rsqrt(jnp.mean(center * center, axis=1, keepdims=True) + 1e-05)
            scaled = center * inverse
            shifted = scaled * gain + shift
            slopes = jnp.exp(jnp.minimum(shifted, 0.0))
            nhat[layer, here, :] = scaled
            slope[layer, here, :] = slopes
            spread[layer, here, :] = inverse
            acts[layer, here, :] = (jnp.maximum(shifted, 0.0) + (slopes - 1.0)).astype(BF)
        if layer < layers - 1:
            work[...] = dot(acts[layer], hidden_ref[layer], ROWS_BY_COLUMNS)

    out_weight = out_weight_ref[...]
    last = acts[layers - 1]
    value = dot(out_weight, last, BY_ROWS)
    target = target_ref[0]
    error = (value[0:1, :] - target[0:1, :]) * target[1:2, :]
    grad_value = (error * target[2:3, :]).astype(BF)
    grad_rows = jnp.concatenate([grad_value.astype(F32), jnp.zeros((7, rows), F32)], axis=0).astype(BF)
    sums_ref[2 * layers] += dot(grad_rows, last, ROWS_BY_COLUMNS)
    sums_ref[2 * layers + 1] += jnp.broadcast_to(jnp.sum(error * error, axis=1, keepdims=True), (8, units))
    work[...] = dot(grad_rows, out_weight, OVER_ROWS)

    for layer in reversed(range(layers)):
        gain = vectors_ref[layer : layer + 1, :]
        for i in range(steps):
            here = slice(i * STEP, (i + 1) * STEP)
            scaled = nhat[layer, here, :]
            grad_norm = work[here, :] * slope[layer, here, :]
            by_scaled = grad_norm * scaled
            sums_ref[layer] += jnp.sum(by_scaled.reshape(STEP // 8, 8, units), axis=0)
            sums_ref[layers + layer] += jnp.sum(grad_norm.reshape(STEP // 8, 8, units), axis=0)
            grad_scaled = grad_norm * gain
            first_mean = jnp.mean(grad_scaled, axis=1, keepdims=True)
            second_mean = jnp.mean(by_scaled * gain, axis=1, keepdims=True)
            grad = spread[layer, here, :] * (grad_scaled - first_mean - scaled * second_mean)
            low_grad[here, :] = grad.astype(BF)
        if layer > 0:
            grads = low_grad[...]
            work[...] = dot(grads, hidden_ref[layer - 1], BY_ROWS)
            share_at(layer - 1)[...] += dot(grads, acts[layer - 1], OVER_ROWS)

    all_first_ref[...] = low_grad[...]
    for pair in range(pairs):

        @pl.when(step == pair)
        def _():
            first_refs[2 * pair][...] = low_grad[0:half, :]
            first_refs[2 * pair + 1][...] = low_grad[half:rows, :]

    if last_call:

        @pl.when(step == pairs - 1)
        def _():
            count = 2 * layers + 2
            sums = jnp.concatenate(
                [jnp.sum(sums_ref[row], axis=0, keepdims=True) for row in range(count - 1)]
                + [sums_ref[count - 1][0:1, :]],
                axis=0,
            )
            high = sums.astype(BF).astype(F32)
            columns = jnp.concatenate([high, sums - high, jnp.zeros((128 - 2 * count, units), F32)], axis=0)
            total_ref[:, (layers - 1) * units :] = columns.T


def critic(own, key_row, targets, state_part, hidden, vectors, out_weight, goal_parts, tiles, before, last_call):
    pairs, first_pair = len(tiles) // 2, tiles[0] // 2
    half, units = goal_parts[0].shape
    rows = 2 * half
    layers = hidden.shape[0] + 1
    width = (layers - 1) * units + 128
    sums_shape, shares_shape = (2 * layers + 2, 8, units), (layers - 1, units, units)
    operands = [key_row, targets, state_part, hidden, vectors, out_weight, *goal_parts]
    in_specs = [
        whole(key_row.shape),
        pl.BlockSpec((1,) + targets.shape[1:], lambda i, _: (first_pair + i, 0, 0)),
        whole(state_part.shape),
        whole(hidden.shape),
        whole(vectors.shape),
        whole(out_weight.shape),
    ] + [whole((half, units))] * (2 * pairs)
    aliases = {}
    if before is not None:
        in_specs += [whole(shares_shape), whole(sums_shape), ANYWHERE]
        operands += list(before)
        aliases = {len(operands): 2 * pairs}
    out_shape = [like(half, units, BF)] * (2 * pairs) + [like(TILES * half, units, BF)]
    out_specs = [whole((half, units))] * (2 * pairs) + [
        pl.BlockSpec((rows, units), lambda i, _: (first_pair + i, 0))
    ]
    scratch = [
        pltpu.VMEM((rows, units), F32),
        pltpu.VMEM((layers, rows, units), F32),
        pltpu.VMEM((layers, rows, units), F32),
        pltpu.VMEM((layers, rows, 1), F32),
        pltpu.VMEM((layers, rows, units), BF),
        pltpu.VMEM((rows, units), BF),
    ]
    if last_call:
        shapes = [like(units, width, F32)]
        scratch += [pltpu.VMEM(sums_shape, F32)]
    else:
        shapes = [like(*shares_shape, F32), like(*sums_shape, F32)]
    return call(
        functools.partial(critic_kernel, pairs, first_pair, layers, before is None, last_call),
        "critic",
        (pairs,),
        own[None],
        in_specs,
        out_specs + [whole(shape.shape) for shape in shapes],
        out_shape + shapes,
        operands,
        scratch,
        aliases,
    )


def state_weight_kernel(steps, split, core_ref, key_ref, first_hbm, states_hbm, rest_hbm, grad_hbm, *refs):
    outs, refs = refs[: 2 if split else 1], refs[2 if split else 1 :]
    first, states, rest, grad, total, first_sem, states_sems, rest_sem, grad_sems, out_sems = refs[:10]
    pieces = refs[10:]
    slots, units = first.shape
    tokens, width = states.shape
    rows, part = tokens // steps, width // steps
    load_first = pltpu.make_async_copy(first_hbm, first, first_sem)
    load_first.start()
    load_rest = pltpu.make_async_copy(rest_hbm, rest, rest_sem)
    load_rest.start()
    loads = [
        pltpu.make_async_copy(
            states_hbm.at[:, step * part : (step + 1) * part], states.at[:, step * part : (step + 1) * part],
            states_sems.at[step],
        )
        for step in range(steps)
    ]
    for load in loads:
        load.start()
    stores = []

    def give(source, start, number):
        there = slice(start, start + source.shape[1])
        if split:
            split_rows(source, pieces[0].at[:, there], pieces[1].at[:, there], core_ref[0], FIRST_ORDER)
            for which in range(2):
                copy = pltpu.make_async_copy(
                    pieces[which].at[:, there], outs[which].at[:, there], out_sems.at[which, number]
                )
                copy.start()
                stores.append(copy)
        else:
            outs[0][:, there] = source[...]

    load_first.wait()
    for step in range(steps):
        here = slice(step * rows, (step + 1) * rows)
        slot = lax.broadcasted_iota(I32, (rows, slots), 1)
        pick = (slot == key_ref[here, :]).astype(F32).astype(BF)
        grad[here, :] = dot(pick, first[...], ROWS_BY_COLUMNS).astype(BF)
    load_rest.wait()
    give(rest, width, steps)
    store_grad = pltpu.make_async_copy(grad, grad_hbm, grad_sems)
    store_grad.start()
    for step in range(steps):
        loads[step].wait()
        here = slice(step * part, (step + 1) * part)
        total[:, here] = dot(grad[...], states[:, here], OVER_ROWS)
        give(total.at[:, here], step * part, step)
    store_grad.wait()
    for store in stores:
        store.wait()


def state_weight_grad(core_bit, key_column, first, states, rest, split):
    tokens, width = states.shape
    slots, units = first.shape
    steps = 4
    columns = width + rest.shape[1]
    shapes = [like(units // 2, columns, F32), like(units // 2, columns, BF)] if split else [like(units, columns, F32)]
    dma = pltpu.SemaphoreType.DMA
    return call(
        functools.partial(state_weight_kernel, steps, split),
        "state_weight_grad",
        (1,),
        core_bit[None],
        [whole(key_column.shape), ANYWHERE, ANYWHERE, ANYWHERE],
        [ANYWHERE] * 3 if split else [ANYWHERE, whole(shapes[0].shape)],
        [like(tokens, units, BF)] + shapes,
        [key_column, first, states, rest],
        [
            pltpu.VMEM(first.shape, BF),
            pltpu.VMEM(states.shape, BF),
            pltpu.VMEM(rest.shape, F32),
            pltpu.VMEM((tokens, units), BF),
            pltpu.VMEM((units, width), F32),
            dma,
            dma((steps,)),
            dma,
            dma,
            dma((2, steps + 1)),
        ]
        + ([pltpu.VMEM(shape.shape, shape.dtype) for shape in shapes] if split else []),
    )


def state_grad_kernel(steps, _, grad_hbm, weight_hbm, out_hbm, grad, weight, out, grad_sem, weight_sem, sems):
    rows = out.shape[1]
    load_weight = pltpu.make_async_copy(weight_hbm, weight, weight_sem)
    load_weight.start()
    load_grad = pltpu.make_async_copy(grad_hbm, grad, grad_sem)
    load_grad.start()
    load_weight.wait()
    load_grad.wait()
    stores = []
    for step in range(steps):
        here = slice(step * rows, (step + 1) * rows)
        out[step] = dot(grad[here, :], weight[...], BY_ROWS).astype(BF)
        stores.append(pltpu.make_async_copy(out.at[step], out_hbm.at[here], sems.at[step]))
        stores[-1].start()
    for store in stores:
        store.wait()


def state_grad(own, grad, weight):
    tokens, units = grad.shape
    width = weight.shape[0]
    steps = 4
    dma = pltpu.SemaphoreType.DMA
    return call(
        functools.partial(state_grad_kernel, steps),
        "state_grad",
        (1,),
        own[None],
        [ANYWHERE] * 2,
        [ANYWHERE],
        [like(tokens, width, BF)],
        [grad, weight],
        [
            pltpu.VMEM(grad.shape, BF),
            pltpu.VMEM(weight.shape, BF),
            pltpu.VMEM((steps, tokens // steps, width), BF),
            dma,
            dma,
            dma((steps,)),
        ],
    )[0]


def goal_backward_kernel(count, with_grad, with_sum, has_before, split, scalars_ref, *refs):
    grad_hbm, refs = refs[:count], refs[count:]
    goals_hbm, weight_hbm, refs = refs[0], refs[1], refs[2:]
    if has_before:
        before_hbm, refs = refs[0], refs[1:]
    if with_grad:
        out_hbm, refs = refs[0], refs[1:]
    if with_sum:
        sum_outs, refs = refs[: 2 if split else 1], refs[2 if split else 1 :]
    grads, goals, weight, out, total, grad_sems, goal_sems, weight_sem, before_sem, out_sems = refs
    rows, width = goals_hbm.shape[0] // TILES, goals_hbm.shape[1]
    at = [pl.ds(pl.multiple_of(scalars_ref[n] * rows, rows), rows) for n in range(count)]
    loads = []
    for n in range(count):
        here = slice(n * rows, (n + 1) * rows)
        load = [pltpu.make_async_copy(grad_hbm[n], grads.at[here], grad_sems.at[n])]
        if with_sum:
            load.append(pltpu.make_async_copy(goals_hbm.at[at[n]], goals.at[here], goal_sems.at[n]))
        loads.append(load)
    for load in loads:
        load[0].start()
    if with_grad:
        load_weight = pltpu.make_async_copy(weight_hbm, weight, weight_sem)
        load_weight.start()
    if with_sum:
        for load in loads:
            load[1].start()
        if has_before:
            load_before = pltpu.make_async_copy(before_hbm, total, before_sem)
            load_before.start()
    stores = []
    for load in loads:
        load[0].wait()
    if with_grad:
        load_weight.wait()
        for n in range(count):
            here = slice(n * rows, (n + 1) * rows)
            out[here, :] = dot(grads[here, :], weight[...], BY_ROWS).astype(BF)
            stores.append(pltpu.make_async_copy(out.at[here], out_hbm.at[at[n]], out_sems.at[n]))
            stores[-1].start()
    if with_sum:
        for load in loads:
            load[1].wait()
        share = dot(grads[...], goals[...], OVER_ROWS)
        if has_before:
            load_before.wait()
            total[...] += share
        else:
            total[...] = share
        if split:
            split_rows(total, sum_outs[0], sum_outs[1], scalars_ref[count], FIRST_ORDER)
        else:
            sum_outs[0][...] = total[...]
    for store in stores:
        store.wait()


def goal_backward(own_tile, core_bit, grads, goals, weight, tiles, with_grad, with_sum, before=None, split=False):
    rows, width, units = goals.shape[0] // TILES, goals.shape[1], weight.shape[1]
    scalars = jnp.concatenate([jnp.array(tiles, I32) ^ own_tile, core_bit[None]])
    count = len(tiles)
    operands = [*grads, goals, weight]
    out_specs, shapes, aliases = [], [], {}
    if with_grad:
        out_specs.append(ANYWHERE)
        shapes.append(like(*goals.shape, BF))
    if before is not None:
        operands.append(before)
        if not with_sum:
            aliases = {len(operands): 0}
    if with_sum and split:
        shapes += [like(units // 2, width, F32), like(units // 2, width, BF)]
        out_specs += [whole(shape.shape) for shape in shapes[-2:]]
    elif with_sum:
        shapes.append(like(units, width, F32))
        out_specs.append(whole((units, width)))
    dma = pltpu.SemaphoreType.DMA
    return call(
        functools.partial(goal_backward_kernel, count, with_grad, with_sum, before is not None, split),
        "goal_backward",
        (1,),
        scalars,
        [ANYWHERE] * len(operands),
        out_specs,
        shapes,
        operands,
        [
            pltpu.VMEM((count * rows, units), BF),
            pltpu.VMEM((count * rows, width), BF),
            pltpu.VMEM(weight.shape, BF),
            pltpu.VMEM((count * rows, width), BF),
            pltpu.VMEM((units, width), F32),
            dma((count,)),
            dma((count,)),
            dma,
            dma,
            dma((count,)),
        ],
        aliases,
        BRIEF,
    )


def fold_kernel(_, kept_mine_ref, got_mine_ref, kept_other_ref, got_other_ref, kept_ref, sent_ref):
    kept_ref[...] = kept_mine_ref[...] + got_mine_ref[...].astype(F32)
    sent_ref[...] = (kept_other_ref[...] + got_other_ref[...].astype(F32)).astype(BF)


def fold(kept, got, bit_value):
    rows, width = kept.shape[0] // 2, kept.shape[1]
    block = min(rows, 64)
    steps = rows // block
    mine = pl.BlockSpec((block, width), lambda i, bit: (bit[0] * steps + i, 0))
    other = pl.BlockSpec((block, width), lambda i, bit: ((1 - bit[0]) * steps + i, 0))
    straight = pl.BlockSpec((block, width), lambda i, bit: (i, 0))
    return call(
        fold_kernel,
        "fold",
        (steps,),
        bit_value[None],
        [mine, mine, other, other],
        [straight, straight],
        [like(rows, width, F32), like(rows, width, BF)],
        [kept, got, kept, got],
    )


def spread_kernel(count, own_ref, kept_ref, got_ref, *out_refs):
    own = own_ref[0]
    size = kept_ref.shape[0] // count
    for offset in range(count):
        here = pl.ds(pl.multiple_of((own ^ offset) * size, size), size)
        total = kept_ref[here, :] + got_ref[here, :].astype(F32)
        out_refs[offset][...] = total.astype(out_refs[offset].dtype)


def round_kernel(_, kept_ref, got_ref, out_ref):
    out_ref[...] = (kept_ref[...] + got_ref[...].astype(F32)).astype(BF)


def finish_kernel(loss_factor, _, states_ref, *refs):
    goal_refs, refs = refs[:-6], refs[-6:]
    first_ref, hidden_ref, gain_ref, shift_ref, out_ref, loss_ref = refs
    layers, share, units = hidden_ref.shape
    total = sum(states_ref[n * share : (n + 1) * share, :].astype(F32) for n in range(states_ref.shape[0] // share))
    goal_total = sum(ref[...].astype(F32) for ref in goal_refs)
    feat_width = first_ref.shape[1] - goal_total.shape[1]
    first_ref[:, 0:feat_width] = total[:, 0:feat_width]
    first_ref[:, feat_width:] = goal_total
    for layer in range(layers):
        start = feat_width + layer * units
        hidden_ref[layer] = total[:, start : start + units]
    rest = total[:, feat_width + layers * units :].T
    parts = 2 * layers + 4
    rest = rest[:parts] + rest[parts : 2 * parts]
    gain_ref[...] = rest[: layers + 1]
    shift_ref[...] = rest[layers + 1 : 2 * layers + 2]
    out_ref[...] = rest[2 * layers + 2 : 2 * layers + 3]
    loss_ref[...] = rest[2 * layers + 3 :, 0:1] * loss_factor


def swap_bit(block, bit, dp_count, mp_count):
    if bit < 2:
        return lax.ppermute(block, "mp", xor_pairs(mp_count, 1 << bit))
    return lax.ppermute(block, "dp", xor_pairs(dp_count, 1 << (bit - 2)))


def sum_plain(partial, dp_count):
    return lax.psum_scatter(partial, ("dp", "mp"), scatter_dimension=0, tiled=True)


def across(block, tile, dp_count):
    per = dp_count // TILES
    moved = block if tile == 0 else lax.ppermute(block, "dp", xor_pairs(dp_count, tile * per))
    if per == 1:
        return moved
    groups = [[group * per + low for low in range(per)] for group in range(TILES)]
    parts = moved.reshape((per, block.shape[0] // per) + block.shape[1:])
    parts = lax.all_to_all(parts, "dp", 0, 0, axis_index_groups=groups, tiled=True)
    return parts.reshape(block.shape)


def shards(
    states, dest_device, goals, returns, weight_in, weight_hidden, norm_gain, norm_shift, weight_out
):
    dp_count, mp_count = lax.axis_size("dp"), lax.axis_size("mp")
    own_dp, own_mp = lax.axis_index("dp"), lax.axis_index("mp")
    number = own_dp * mp_count + own_mp
    core_bit = number & 1
    tokens, feat_width = states.shape
    all_rows = tokens * dp_count * mp_count
    slot_count, goal_width = goals.shape
    capacity = slot_count // dp_count
    shard_in, units = weight_in.shape
    layers = norm_gain.shape[0]
    shard_units = norm_gain.shape[1]
    per = dp_count // TILES
    rows = slot_count // TILES
    own_tile = own_dp // per
    single = per == 1
    swap, cross = xor_pairs(4, 1), xor_pairs(4, 2)

    small = jnp.concatenate([norm_gain, norm_shift, weight_out[None, :]], axis=0)
    small = jnp.pad(small.reshape(-1), (0, 16 * units - small.size)).reshape(16, units)
    others = jnp.concatenate([weight_hidden.reshape((layers - 1) * shard_units, units), small], axis=0)
    other_rows = others.shape[0]
    if single:
        key_row, key_column, message = route(
            own_dp, dest_device.reshape(1, tokens), returns.reshape(dp_count, capacity), units
        )
    else:
        dest = dest_device[:, 0]
        offset = ((dest // per) ^ own_tile) * per + dest % per
        blocks = tokens // 128
        marks = (offset[None, :] == jnp.arange(dp_count, dtype=I32)[:, None]).astype(F32)
        marks = marks.reshape(dp_count, blocks, 128)
        upper = jnp.arange(128)[:, None] < jnp.arange(128)[None, :]
        within = dot(marks.astype(BF), upper.astype(BF), ((2,), (0,)))
        block_sums = jnp.sum(marks, axis=2)
        earlier = jnp.arange(blocks)[None, :] < jnp.arange(blocks)[:, None]
        ahead = jnp.sum(jnp.where(earlier[None], block_sums[:, None, :], 0.0), axis=2)
        rank = jnp.sum(marks * (within + ahead[:, :, None]), axis=0).reshape(tokens)
        key = offset * capacity + rank.astype(I32)
        key_row, key_column = key[None, :], key[:, None]
        valid = jnp.arange(capacity, dtype=F32)[None, :] < jnp.sum(block_sums, axis=1)[:, None]
        tile_returns = returns.reshape(TILES, rows)
        got_returns = [
            across(lax.dynamic_index_in_dim(tile_returns, own_tile ^ t, 0, keepdims=False), t, dp_count)
            for t in range(TILES)
        ]
        got_returns = jnp.stack(got_returns).reshape(dp_count, capacity).astype(F32)
        square_total = lax.psum(jnp.sum(jnp.where(valid, got_returns * got_returns, 0.0)), ("dp", "mp"))
        scale_value = jnp.sqrt(square_total / all_rows + 1e-06)
        targets = jnp.stack(
            [got_returns / scale_value, valid.astype(F32), jnp.full(valid.shape, 1.0 / all_rows, F32)]
            + [jnp.zeros(valid.shape, F32)] * 5
        )
        targets = targets.reshape(8, TILES // 2, 2 * rows).transpose(1, 0, 2)

    cut = feat_width % shard_in
    first_goal_shard = feat_width // shard_in
    one = lax.ppermute(weight_in, "mp", swap)
    two = lax.ppermute(weight_in, "mp", cross)
    if single:
        messages = message
        for bit in (4, 2, 1):
            messages = jnp.concatenate([messages, lax.ppermute(messages, "dp", xor_pairs(dp_count, bit))], axis=0)
        two = after(two, messages)
    pieces = (weight_in, one, two, lax.ppermute(two, "mp", swap))

    *parts, goal_weight = goal_forward(own_tile, own_mp, goals, pieces, cut, first_goal_shard)
    if single:
        others = jnp.concatenate([others, after(messages, goal_weight)], axis=0)
    others_one = lax.ppermute(others, "mp", swap)
    others_two = lax.ppermute(others, "mp", cross)
    others_three = lax.ppermute(others_two, "mp", swap)

    state_part, state_weight = state_forward(after(own_mp, goal_weight), states, pieces, cut, first_goal_shard)
    parts = [across(after(part, state_part) if tile > 4 else part, tile, dp_count) for tile, part in enumerate(parts)]
    prepared = prepare(
        after(own_mp, *[parts[tile] for tile in (1, 2, 3, 4)]), [others, others_one, others_two, others_three],
        layers, other_rows, rows, float(all_rows),
    )
    hidden, vectors, out_weight = prepared[:3]
    if single:
        targets = prepared[3]

    running, back, made_of = None, {}, {}
    for tiles in (NEAR, FAR_ONE, FAR_TWO):
        made = critic(
            own_dp, key_row, targets, state_part, hidden, vectors, out_weight,
            [parts[t] for t in tiles], tiles, running, tiles == FAR_TWO,
        )
        running = (made[-2], made[-1], made[len(tiles)])
        made_of.update(zip(tiles, made))
        if tiles == FAR_ONE:
            for tile in NEAR + FAR_ONE:
                back[tile] = across(after(made_of[tile], made_of[FAR_ONE[0]], *[parts[u] for u in FAR_TWO]), tile, dp_count)
    for tile in FAR_TWO:
        back[tile] = across(after(made_of[tile], *[back[u] for u in NEAR + FAR_ONE]), tile, dp_count)
    first, rest = made[-2], made[-1]

    state_made = state_weight_grad(core_bit, key_column, first, states, rest, single)

    early = NEAR + FAR_ONE
    if single:
        kept, sent = state_made[1:]
        sent = after(sent, *[back[t] for t in early])
        states_kept, sent = fold(kept, swap_bit(sent, CORE, dp_count, mp_count), (number >> Y) & 1)
        states_got = swap_bit(sent, Y, dp_count, mp_count)
        back[0] = after(back[0], states_kept)
    grad_goals, running_sum = goal_backward(
        own_tile, core_bit, [back[t] for t in early], goals, goal_weight, early, True, True
    )
    grad_states = state_grad(own_dp, after(state_made[0], running_sum), state_weight)
    running_sum = after(running_sum, grad_states)
    if single:
        states_got = after(states_got, grad_states, *[back[t] for t in FAR_TWO])
        block = call(
            round_kernel, "round", (1,), own_dp[None], [whole(states_kept.shape)] * 2, [whole(states_kept.shape)],
            [like(*states_kept.shape, BF)], [states_kept, states_got],
        )[0]
        running_sum = after(running_sum, block)
    goal_made = goal_backward(
        own_tile, core_bit, [back[t] for t in FAR_TWO], goals, goal_weight, FAR_TWO, False, True,
        running_sum, single,
    )
    grad_goals = goal_backward(
        own_tile, core_bit, [after(back[t], goal_made[0]) for t in FAR_TWO], goals, goal_weight, FAR_TWO, True, False,
        grad_goals,
    )[0]

    share = units // (dp_count * mp_count)
    if single:
        goals_kept, goals_sent = goal_made
        goals_got = swap_bit(goals_sent, CORE, dp_count, mp_count)
        goals_kept, goals_sent = fold(goals_kept, goals_got, (number >> Y) & 1)
        goals_got = swap_bit(goals_sent, Y, dp_count, mp_count)
        block = lax.all_to_all(block.reshape(dp_count, share, -1), "dp", 0, 0, tiled=True)
        arrived = [block.reshape(dp_count * share, -1)]
        blocks = call(
            functools.partial(spread_kernel, dp_count), "spread", (1,), own_dp[None],
            [whole(goals_kept.shape)] * 2,
            [whole((share, goal_width))] * dp_count,
            [like(share, goal_width, F32)] + [like(share, goal_width, BF)] * (dp_count - 1),
            [goals_kept, goals_got],
        )
        arrived += [blocks[0]] + [
            lax.ppermute(blocks[o], "dp", xor_pairs(dp_count, o)) for o in range(1, dp_count)
        ]
        shapes = [
            like(share, feat_width + goal_width, F32), like(layers - 1, share, units, F32),
            like(layers, share, F32), like(layers, share, F32), like(1, share, F32), like(1, 1, F32),
        ]
        first_share, hidden_share, gain_grad, shift_grad, out_grad, loss = call(
            functools.partial(finish_kernel, 0.5 / all_rows),
            "finish", (1,), core_bit[None],
            [whole(block.shape) for block in arrived],
            [whole(shape.shape) for shape in shapes],
            shapes,
            arrived,
        )
    else:
        total = sum_plain(state_made[1], dp_count)
        hidden_share = total[:, feat_width : feat_width + (layers - 1) * units]
        hidden_share = hidden_share.reshape(share, layers - 1, units).transpose(1, 0, 2)
        rest = total[:, feat_width + (layers - 1) * units :]
        first_share = jnp.concatenate([total[:, :feat_width], sum_plain(goal_made[0], dp_count)], axis=1)

        count = 2 * layers + 2
        rest = (rest[:, :count] + rest[:, count : 2 * count]).T
        gain_grad, shift_grad, out_grad = rest[:layers], rest[layers : 2 * layers], rest[2 * layers]
        loss = 0.5 * rest[count - 1, 0] / all_rows
    return (
        loss.reshape(()),
        grad_states,
        grad_goals,
        first_share.T,
        hidden_share.transpose(0, 2, 1),
        gain_grad,
        shift_grad,
        out_grad.reshape(share),
    )


def solution(mesh):
    placed = (
        P(("dp", "mp"), None),
        P(("dp", "mp"), None),
        P(("dp", "mp"), None),
        P(("dp", "mp")),
        P("mp", None),
        P(None, "mp", None),
        P(None, "mp"),
        P(None, "mp"),
        P("mp"),
    )
    return jax.shard_map(
        shards,
        mesh=mesh,
        in_specs=placed,
        out_specs=(
            P(),
            P(("dp", "mp"), None),
            P(("dp", "mp"), None),
            P(None, ("dp", "mp")),
            P(None, None, ("dp", "mp")),
            P(None, ("dp", "mp")),
            P(None, ("dp", "mp")),
            P(("dp", "mp")),
        ),
        check_vma=False,
    )
```

```python
import functools

import jax
import jax.numpy as jnp
from jax import lax
from jax.experimental import pallas as pl
from jax.experimental.pallas import tpu as pltpu
from jax.sharding import PartitionSpec as P

BF = jnp.bfloat16
F32 = jnp.float32
I32 = jnp.int32
TILES = 8
STEP = 64
VMEM = 63 * 1024 * 1024
NEAR, FAR_ONE, FAR_TWO = (0, 1, 2, 3), (4, 5), (6, 7)
BRIEF = pl.CostEstimate(flops=1, bytes_accessed=1, transcendentals=0)
LONG = pl.CostEstimate(flops=9_000_000_000, bytes_accessed=10_000_000, transcendentals=0)
CORE, Y, X, Z_LOW, Z_HIGH = range(5)
FIRST_ORDER = (CORE, Y, Z_HIGH, Z_LOW, X)


def dot(first, second, dims):
    return lax.dot_general(first, second, (dims, ((), ())), preferred_element_type=F32)


ROWS_BY_COLUMNS, BY_ROWS, OVER_ROWS = ((1,), (0,)), ((1,), (1,)), ((0,), (0,))


def after(value, *others):
    return lax.optimization_barrier((value, *others))[0]


def xor_pairs(count, bits):
    return [(i, i ^ bits) for i in range(count)]


def like(*shape_and_type):
    *shape, dtype = shape_and_type
    return jax.ShapeDtypeStruct(tuple(shape), dtype)


def whole(shape):
    return pl.BlockSpec(tuple(shape), lambda *_: (0,) * len(shape))


ANYWHERE = pl.BlockSpec(memory_space=pl.ANY)


def call(kernel, name, grid, scalars, in_specs, out_specs, out_shape, operands, scratch=(), aliases=None, cost=BRIEF):
    return pl.pallas_call(
        kernel,
        out_shape=out_shape,
        grid_spec=pltpu.PrefetchScalarGridSpec(
            num_scalar_prefetch=1,
            grid=grid,
            in_specs=in_specs,
            out_specs=out_specs,
            scratch_shapes=list(scratch),
        ),
        input_output_aliases=aliases or {},
        compiler_params=pltpu.CompilerParams(vmem_limit_bytes=VMEM),
        cost_estimate=cost,
        name=name,
    )(scalars, *operands)


def route_kernel(capacity, own_ref, dest_ref, returns_ref, row_ref, message_ref, wide, text):
    own = own_ref[0]
    tokens = dest_ref.shape[1]
    count = returns_ref.shape[0]
    blocks = tokens // 128
    offsets = dest_ref[...] ^ own
    marks = (lax.broadcasted_iota(I32, (count, tokens), 0) == offsets).astype(F32)
    stacked = jnp.concatenate([marks[:, 128 * b : 128 * b + 128] for b in range(blocks)], axis=0)
    upper = lax.broadcasted_iota(I32, (128, 128), 0) < lax.broadcasted_iota(I32, (128, 128), 1)
    within = dot(stacked.astype(BF), upper.astype(F32).astype(BF), ROWS_BY_COLUMNS)
    totals = jnp.sum(stacked, axis=1, keepdims=True)
    ahead = jnp.zeros((count, 1), F32)
    for b in range(blocks):
        part = slice(count * b, count * b + count)
        lanes = slice(128 * b, 128 * b + 128)
        rank = jnp.sum(stacked[part] * (within[part] + ahead), axis=0, keepdims=True)
        key = offsets[:, lanes].astype(F32) * capacity + rank
        row_ref[:, lanes] = key.astype(I32)
        ahead = ahead + totals[part]
    wide[...] = returns_ref[...].astype(F32)
    lane = lax.broadcasted_iota(I32, text.shape, 1) - (text.shape[1] - 128)
    high = jnp.floor(ahead * 0.0625)
    text[...] = jnp.where(lane == 0, high, jnp.where(lane == 1, ahead - 16.0 * high, 0.0))
    for offset in range(count):
        text[offset : offset + 1, 0:capacity] = wide[pl.ds(own ^ offset, 1), :]
    message_ref[...] = text[...].astype(BF)


def route(own, dest_row, returns, units):
    tokens, (count, capacity) = dest_row.shape[1], returns.shape
    return call(
        functools.partial(route_kernel, capacity),
        "route",
        (1,),
        own[None],
        [whole(dest_row.shape), whole(returns.shape)],
        [whole((1, tokens)), whole((count, units))],
        [like(1, tokens, I32), like(count, units, BF)],
        [dest_row, returns],
        [pltpu.VMEM(returns.shape, F32), pltpu.VMEM((count, units), F32)],
    )


def reverse(bits):
    return (bits % 2) * 4 + (bits // 2 % 2) * 2 + bits // 4


def prepare_kernel(layers, rows, capacity, total_rows, own_ref, *refs):
    pieces, refs = refs[:4], refs[4:]
    hidden_ref, vectors_ref, out_weight_ref = refs[:3]
    own = own_ref[0]
    width = hidden_ref.shape[2] // 4
    for shard in range(4):
        columns = slice(shard * width, (shard + 1) * width)
        for value in range(4):

            @pl.when(own == value)
            def _():
                piece = pieces[shard ^ value]
                for layer in range(layers - 1):
                    hidden_ref[layer, columns, :] = piece[layer * width : (layer + 1) * width, :]
                start = (layers - 1) * width
                small = piece[start : start + 16, :].astype(F32)
                for row in range(2 * layers + 1):
                    vectors_ref[row : row + 1, columns] = small[
                        row // 4 : row // 4 + 1, (row % 4) * width : (row % 4 + 1) * width
                    ]

    vectors_ref[2 * layers + 1 :, :] = jnp.zeros((16 - 2 * layers - 1, vectors_ref.shape[1]), F32)
    out_weight_ref[...] = jnp.concatenate(
        [vectors_ref[2 * layers : 2 * layers + 1, :], jnp.zeros((7, vectors_ref.shape[1]), F32)], axis=0
    ).astype(BF)
    if len(refs) == 3:
        return
    targets_ref = refs[3]
    targets_ref[...] = jnp.zeros_like(targets_ref)
    index = lax.broadcasted_iota(I32, (64, 64), 0)
    partner = (reverse(reverse(index // 8) ^ (index % 8))) * 8 + index % 8
    swap = (lax.broadcasted_iota(I32, (64, 64), 1) == partner).astype(F32).astype(BF)
    lane = lax.broadcasted_iota(I32, (64, 128 * 3), 1).astype(F32)
    total = jnp.zeros((1, 1), F32)
    for piece in pieces:
        message = piece[rows : rows + 64, :]
        counts = dot(swap, message[:, 384:512], ROWS_BY_COLUMNS)
        counts = counts[:, 0:1] * 16.0 + counts[:, 1:2]
        values = message[:, 0:384].astype(F32)
        squares = jnp.sum(jnp.where(lane < counts, values * values, 0.0), axis=1, keepdims=True)
        total = total + jnp.sum(squares, axis=0, keepdims=True)
    scale = jnp.sqrt(total / total_rows + 1e-06)
    message = pieces[0][rows : rows + 64, :].astype(F32)
    counts = message[0:8, 384:385] * 16.0 + message[0:8, 385:386]
    for tile in range(TILES):
        lanes = slice((tile % 2) * capacity, (tile % 2) * capacity + capacity)
        row = reverse(tile) * 8 + tile
        target = message[row : row + 1, 0:384] / scale
        filled = (lane[0:1] < counts[tile : tile + 1]).astype(F32)
        targets_ref[tile // 2, 0:1, lanes] = target[:, 0:capacity]
        targets_ref[tile // 2, 1:2, lanes] = filled[:, 0:capacity]
        targets_ref[tile // 2, 2:3, lanes] = jnp.full((1, capacity), 1.0 / total_rows, F32)


def prepare(own, pieces, layers, rows, capacity, total_rows):
    units = pieces[0].shape[1]
    shapes = [like(layers - 1, units, units, BF), like(16, units, F32), like(8, units, BF)]
    if pieces[0].shape[0] > rows:
        shapes.append(like(TILES // 2, 8, 2 * capacity, F32))
    return call(
        functools.partial(prepare_kernel, layers, rows, capacity, total_rows),
        "prepare",
        (1,),
        own[None],
        [whole(piece.shape) for piece in pieces],
        [whole(shape.shape) for shape in shapes],
        shapes,
        pieces,
    )


def fetch(own, parts, target_ref, sems, later=()):
    place = 0
    for number, (shard, candidates) in enumerate(parts):
        size = candidates[0].shape[0]
        there = target_ref.at[place : place + size]
        for value in range(4):

            @pl.when(own == value)
            def _():
                pltpu.make_async_copy(candidates[shard ^ value], there, sems.at[number]).start()

        place += size
    for copy in later:
        copy.start()
    place = 0
    for number, (shard, candidates) in enumerate(parts):
        size = candidates[0].shape[0]
        there = target_ref.at[place : place + size]
        pltpu.make_async_copy(candidates[0], there, sems.at[number]).wait()
        place += size


def first_weight_parts(pieces, cut, shards, first, last):
    parts = []
    for shard in shards:
        here = slice(cut if shard == first else 0, cut if shard == last else pieces[0].shape[0])
        parts.append((shard, [piece.at[here] for piece in pieces]))
    return parts


def goal_forward_kernel(cut, first_shard, scalars_ref, goals_ref, *refs):
    pieces, refs = refs[:4], refs[4:]
    out_refs, weight_ref, refs = refs[:TILES], refs[TILES], refs[TILES + 1 :]
    goals, made, sems, out_sems, fetch_sems = refs
    rows = goals_ref.shape[0] // TILES
    copies = []
    for place in range(TILES):
        there = goals_ref.at[pl.ds(pl.multiple_of((scalars_ref[0] ^ place) * rows, rows), rows)]
        copies.append(pltpu.make_async_copy(there, goals.at[place], sems.at[place]))
    order = [*NEAR[1:], *FAR_ONE, *FAR_TWO, 0]
    copies[order[0]].start()
    parts = first_weight_parts(pieces, cut, range(first_shard, 4), first_shard, None)
    fetch(scalars_ref[1], parts, weight_ref, fetch_sems, [copies[place] for place in order[1:]])
    sent = []
    for place in order:
        copies[place].wait()
        made[place] = dot(goals[place], weight_ref[...], ROWS_BY_COLUMNS).astype(BF)
        sent.append(pltpu.make_async_copy(made.at[place], out_refs[place], out_sems.at[place]))
        sent[-1].start()
    for copy in sent:
        copy.wait()


def goal_forward(own_tile, own_mp, goals, pieces, cut, first_shard):
    rows, width = goals.shape[0] // TILES, goals.shape[1]
    units = pieces[0].shape[1]
    return call(
        functools.partial(goal_forward_kernel, cut, first_shard),
        "goal_forward",
        (1,),
        jnp.stack([own_tile, own_mp]),
        [ANYWHERE] * 5,
        [ANYWHERE] * TILES + [whole((width, units))],
        [like(rows, units, BF)] * TILES + [like(width, units, BF)],
        [goals, *pieces],
        [
            pltpu.VMEM((TILES, rows, width), BF),
            pltpu.VMEM((TILES, rows, units), BF),
            pltpu.SemaphoreType.DMA((TILES,)),
            pltpu.SemaphoreType.DMA((TILES,)),
            pltpu.SemaphoreType.DMA((4,)),
        ],
    )


def state_forward_kernel(steps, cut, last_shard, own_ref, states_ref, *refs):
    pieces, (out_ref, weight_ref, states, sems, fetch_sems) = refs[:4], refs[4:]
    rows = states.shape[1]
    copies = [
        pltpu.make_async_copy(states_ref.at[step * rows : (step + 1) * rows], states.at[step], sems.at[step])
        for step in range(steps)
    ]
    copies[0].start()
    parts = first_weight_parts(pieces, cut, range(last_shard + 1), None, last_shard)
    fetch(own_ref[0], parts, weight_ref, fetch_sems, copies[1:])
    for step in range(steps):
        copies[step].wait()
        here = slice(step * rows, (step + 1) * rows)
        out_ref[here, :] = dot(states[step], weight_ref[...], ROWS_BY_COLUMNS).astype(BF)


def state_forward(own, states, pieces, cut, last_shard):
    tokens, width = states.shape
    units = pieces[0].shape[1]
    steps = 4
    return call(
        functools.partial(state_forward_kernel, steps, cut, last_shard),
        "state_forward",
        (1,),
        own[None],
        [ANYWHERE] * 5,
        [whole((tokens, units)), whole((width, units))],
        [like(tokens, units, BF), like(width, units, BF)],
        [states, *pieces],
        [
            pltpu.VMEM((steps, tokens // steps, width), BF),
            pltpu.SemaphoreType.DMA((steps,)),
            pltpu.SemaphoreType.DMA((4,)),
        ],
    )


def split_rows(total_ref, kept_ref, sent_ref, bit_value, order):
    parts = 1 << len(order)
    size = total_ref.shape[0] // parts
    for place in range(parts // 2):
        number = 0
        for depth, bit in enumerate(order[1:]):
            number += ((place >> (len(order) - 2 - depth)) & 1) << bit
        here = slice(place * size, (place + 1) * size)
        mine = pl.multiple_of((number + (bit_value << order[0])) * size, size)
        other = pl.multiple_of((number + ((1 - bit_value) << order[0])) * size, size)
        kept_ref[here, :] = total_ref[pl.ds(mine, size), :]
        sent_ref[here, :] = total_ref[pl.ds(other, size), :].astype(BF)


def critic_kernel(pairs, first_pair, layers, first_call, last_call, _, *refs):
    key_ref, target_ref, states_ref, hidden_ref, vectors_ref, out_weight_ref = refs[:6]
    refs = refs[6:]
    goal_refs, refs = refs[: 2 * pairs], refs[2 * pairs :]
    if not first_call:
        shares_before_hbm, sums_before_ref = refs[:2]
        refs = refs[3:]
    first_refs, refs = refs[: 2 * pairs], refs[2 * pairs :]
    all_first_ref, refs = refs[0], refs[1:]
    if last_call:
        total_ref, refs = refs[0], refs[1:]
    else:
        shares_ref, sums_ref = refs[:2]
        refs = refs[2:]
    work, nhat, slope, spread, acts, low_grad = refs[:6]
    if last_call:
        sums_ref = refs[6]
        share_at = lambda layer: total_ref.at[:, layer * work.shape[1] : (layer + 1) * work.shape[1]]
    else:
        share_at = lambda layer: shares_ref.at[layer]
    step = pl.program_id(0)
    rows, units = work.shape
    if not first_call:
        loads = [
            pltpu.make_async_copy(shares_before_hbm.at[layer], share_at(layer), refs[-1].at[layer])
            for layer in range(layers - 1)
        ]
        for load in loads:
            load.start()
    half = rows // 2
    tokens = key_ref.shape[1]
    steps = rows // STEP

    @pl.when(step == 0)
    def _():
        if first_call:
            for layer in range(layers - 1):
                share_at(layer)[...] = jnp.zeros((units, units), F32)
        sums_ref[...] = jnp.zeros_like(sums_ref) if first_call else sums_before_ref[...]

    for pair in range(pairs):

        @pl.when(step == pair)
        def _():
            low_grad[0:half, :] = goal_refs[2 * pair][...]
            low_grad[half:rows, :] = goal_refs[2 * pair + 1][...]

    base = (first_pair + step) * rows
    slot = base + lax.broadcasted_iota(I32, (rows, tokens), 0)
    pick = (slot == key_ref[...]).astype(F32).astype(BF)
    work[...] = dot(pick, states_ref[...], ROWS_BY_COLUMNS) + low_grad[...].astype(F32)

    for layer in range(layers):
        gain = vectors_ref[layer : layer + 1, :]
        shift = vectors_ref[layers + layer : layers + layer + 1, :]
        for i in range(steps):
            here = slice(i * STEP, (i + 1) * STEP)
            values = work[here, :]
            center = values - jnp.mean(values, axis=1, keepdims=True)
            inverse = lax.rsqrt(jnp.mean(center * center, axis=1, keepdims=True) + 1e-05)
            scaled = center * inverse
            shifted = scaled * gain + shift
            slopes = jnp.exp(jnp.minimum(shifted, 0.0))
            nhat[layer, here, :] = scaled
            slope[layer, here, :] = slopes
            spread[layer, here, :] = inverse
            acts[layer, here, :] = (jnp.maximum(shifted, 0.0) + (slopes - 1.0)).astype(BF)
        if layer < layers - 1:
            work[...] = dot(acts[layer], hidden_ref[layer], ROWS_BY_COLUMNS)

    out_weight = out_weight_ref[...]
    last = acts[layers - 1]
    value = dot(out_weight, last, BY_ROWS)
    target = target_ref[0]
    error = (value[0:1, :] - target[0:1, :]) * target[1:2, :]
    grad_value = (error * target[2:3, :]).astype(BF)
    grad_rows = jnp.concatenate([grad_value.astype(F32), jnp.zeros((7, rows), F32)], axis=0).astype(BF)
    sums_ref[2 * layers] += dot(grad_rows, last, ROWS_BY_COLUMNS)
    sums_ref[2 * layers + 1] += jnp.broadcast_to(jnp.sum(error * error, axis=1, keepdims=True), (8, units))
    work[...] = dot(grad_rows, out_weight, OVER_ROWS)

    if not first_call:
        for load in loads:
            load.wait()
    for layer in reversed(range(layers)):
        gain = vectors_ref[layer : layer + 1, :]
        for i in range(steps):
            here = slice(i * STEP, (i + 1) * STEP)
            scaled = nhat[layer, here, :]
            grad_norm = work[here, :] * slope[layer, here, :]
            by_scaled = grad_norm * scaled
            sums_ref[layer] += jnp.sum(by_scaled.reshape(STEP // 8, 8, units), axis=0)
            sums_ref[layers + layer] += jnp.sum(grad_norm.reshape(STEP // 8, 8, units), axis=0)
            grad_scaled = grad_norm * gain
            first_mean = jnp.mean(grad_scaled, axis=1, keepdims=True)
            second_mean = jnp.mean(by_scaled * gain, axis=1, keepdims=True)
            grad = spread[layer, here, :] * (grad_scaled - first_mean - scaled * second_mean)
            low_grad[here, :] = grad.astype(BF)
        if layer > 0:
            grads = low_grad[...]
            work[...] = dot(grads, hidden_ref[layer - 1], BY_ROWS)
            share_at(layer - 1)[...] += dot(grads, acts[layer - 1], OVER_ROWS)

    all_first_ref[...] = low_grad[...]
    for pair in range(pairs):

        @pl.when(step == pair)
        def _():
            first_refs[2 * pair][...] = low_grad[0:half, :]
            first_refs[2 * pair + 1][...] = low_grad[half:rows, :]

    if last_call:

        @pl.when(step == pairs - 1)
        def _():
            count = 2 * layers + 2
            sums = jnp.concatenate(
                [jnp.sum(sums_ref[row], axis=0, keepdims=True) for row in range(count - 1)]
                + [sums_ref[count - 1][0:1, :]],
                axis=0,
            )
            high = sums.astype(BF).astype(F32)
            columns = jnp.concatenate([high, sums - high, jnp.zeros((128 - 2 * count, units), F32)], axis=0)
            total_ref[:, (layers - 1) * units :] = columns.T


def critic(own, key_row, targets, state_part, hidden, vectors, out_weight, goal_parts, tiles, before, last_call):
    pairs, first_pair = len(tiles) // 2, tiles[0] // 2
    half, units = goal_parts[0].shape
    rows = 2 * half
    layers = hidden.shape[0] + 1
    width = (layers - 1) * units + 128
    sums_shape, shares_shape = (2 * layers + 2, 8, units), (layers - 1, units, units)
    operands = [key_row, targets, state_part, hidden, vectors, out_weight, *goal_parts]
    in_specs = [
        whole(key_row.shape),
        pl.BlockSpec((1,) + targets.shape[1:], lambda i, _: (first_pair + i, 0, 0)),
        whole(state_part.shape),
        whole(hidden.shape),
        whole(vectors.shape),
        whole(out_weight.shape),
    ] + [whole((half, units))] * (2 * pairs)
    aliases = {}
    if before is not None:
        in_specs += [ANYWHERE, whole(sums_shape), ANYWHERE]
        assert pairs == 1
        operands += list(before)
        aliases = {len(operands): 2 * pairs}
    out_shape = [like(half, units, BF)] * (2 * pairs) + [like(TILES * half, units, BF)]
    out_specs = [whole((half, units))] * (2 * pairs) + [
        pl.BlockSpec((rows, units), lambda i, _: (first_pair + i, 0))
    ]
    scratch = [
        pltpu.VMEM((rows, units), F32),
        pltpu.VMEM((layers, rows, units), F32),
        pltpu.VMEM((layers, rows, units), F32),
        pltpu.VMEM((layers, rows, 1), F32),
        pltpu.VMEM((layers, rows, units), BF),
        pltpu.VMEM((rows, units), BF),
    ]
    if last_call:
        shapes = [like(units, width, F32)]
        scratch += [pltpu.VMEM(sums_shape, F32)]
    else:
        shapes = [like(*shares_shape, F32), like(*sums_shape, F32)]
    if before is not None:
        scratch.append(pltpu.SemaphoreType.DMA((layers - 1,)))
    return call(
        functools.partial(critic_kernel, pairs, first_pair, layers, before is None, last_call),
        "critic",
        (pairs,),
        own[None],
        in_specs,
        out_specs + [whole(shape.shape) for shape in shapes],
        out_shape + shapes,
        operands,
        scratch,
        aliases,
    )


def state_weight_kernel(steps, split, core_ref, key_ref, first_hbm, states_hbm, rest_hbm, grad_hbm, *refs):
    outs, refs = refs[: 2 if split else 1], refs[2 if split else 1 :]
    first, states, rest, grad, total, first_sem, states_sems, rest_sem, grad_sems, out_sems = refs[:10]
    pieces = refs[10:]
    slots, units = first.shape
    tokens, width = states.shape
    rows, part = tokens // steps, width // steps
    load_first = pltpu.make_async_copy(first_hbm, first, first_sem)
    load_first.start()
    load_rest = pltpu.make_async_copy(rest_hbm, rest, rest_sem)
    load_rest.start()
    loads = [
        pltpu.make_async_copy(
            states_hbm.at[:, step * part : (step + 1) * part], states.at[:, step * part : (step + 1) * part],
            states_sems.at[step],
        )
        for step in range(steps)
    ]
    for load in loads:
        load.start()
    stores = []

    def give(source, start, number):
        there = slice(start, start + source.shape[1])
        if split:
            split_rows(source, pieces[0].at[:, there], pieces[1].at[:, there], core_ref[0], FIRST_ORDER)
            for which in range(2):
                copy = pltpu.make_async_copy(
                    pieces[which].at[:, there], outs[which].at[:, there], out_sems.at[which, number]
                )
                copy.start()
                stores.append(copy)
        else:
            outs[0][:, there] = source[...]

    load_first.wait()
    for step in range(steps):
        here = slice(step * rows, (step + 1) * rows)
        slot = lax.broadcasted_iota(I32, (slots, rows), 0)
        pick = (slot == key_ref[:, here]).astype(F32).astype(BF)
        grad[here, :] = dot(pick, first[...], OVER_ROWS).astype(BF)
    load_rest.wait()
    give(rest, width, steps)
    store_grad = pltpu.make_async_copy(grad, grad_hbm, grad_sems)
    store_grad.start()
    for step in range(steps):
        loads[step].wait()
        here = slice(step * part, (step + 1) * part)
        total[:, here] = dot(grad[...], states[:, here], OVER_ROWS)
        give(total.at[:, here], step * part, step)
    store_grad.wait()
    for store in stores:
        store.wait()


def state_weight_grad(core_bit, key_row, first, states, rest, split):
    tokens, width = states.shape
    slots, units = first.shape
    steps = 4
    columns = width + rest.shape[1]
    shapes = [like(units // 2, columns, F32), like(units // 2, columns, BF)] if split else [like(units, columns, F32)]
    dma = pltpu.SemaphoreType.DMA
    return call(
        functools.partial(state_weight_kernel, steps, split),
        "state_weight_grad",
        (1,),
        core_bit[None],
        [whole(key_row.shape), ANYWHERE, ANYWHERE, ANYWHERE],
        [ANYWHERE] * 3 if split else [ANYWHERE, whole(shapes[0].shape)],
        [like(tokens, units, BF)] + shapes,
        [key_row, first, states, rest],
        [
            pltpu.VMEM(first.shape, BF),
            pltpu.VMEM(states.shape, BF),
            pltpu.VMEM(rest.shape, F32),
            pltpu.VMEM((tokens, units), BF),
            pltpu.VMEM((units, width), F32),
            dma,
            dma((steps,)),
            dma,
            dma,
            dma((2, steps + 1)),
        ]
        + ([pltpu.VMEM(shape.shape, shape.dtype) for shape in shapes] if split else []),
    )


def state_grad_kernel(steps, _, grad_hbm, weight_hbm, out_hbm, grad, weight, out, grad_sem, weight_sem, sems):
    rows = out.shape[1]
    load_weight = pltpu.make_async_copy(weight_hbm, weight, weight_sem)
    load_weight.start()
    load_grad = pltpu.make_async_copy(grad_hbm, grad, grad_sem)
    load_grad.start()
    load_weight.wait()
    load_grad.wait()
    stores = []
    for step in range(steps):
        here = slice(step * rows, (step + 1) * rows)
        out[step] = dot(grad[here, :], weight[...], BY_ROWS).astype(BF)
        stores.append(pltpu.make_async_copy(out.at[step], out_hbm.at[here], sems.at[step]))
        stores[-1].start()
    for store in stores:
        store.wait()


def state_grad(own, grad, weight):
    tokens, units = grad.shape
    width = weight.shape[0]
    steps = 4
    dma = pltpu.SemaphoreType.DMA
    return call(
        functools.partial(state_grad_kernel, steps),
        "state_grad",
        (1,),
        own[None],
        [ANYWHERE] * 2,
        [ANYWHERE],
        [like(tokens, width, BF)],
        [grad, weight],
        [
            pltpu.VMEM(grad.shape, BF),
            pltpu.VMEM(weight.shape, BF),
            pltpu.VMEM((steps, tokens // steps, width), BF),
            dma,
            dma,
            dma((steps,)),
        ],
        cost=BRIEF,
    )[0]


def goal_backward_kernel(count, with_grad, with_sum, has_before, split, scalars_ref, *refs):
    grad_hbm, refs = refs[:count], refs[count:]
    goals_hbm, weight_hbm, refs = refs[0], refs[1], refs[2:]
    if has_before:
        before_hbm, refs = refs[0], refs[1:]
    if with_grad:
        out_hbm, refs = refs[0], refs[1:]
    if with_sum:
        sum_outs, refs = refs[: 2 if split else 1], refs[2 if split else 1 :]
    grads, goals, weight, out, total, grad_sems, goal_sems, weight_sem, before_sem, out_sems = refs
    rows, width = goals_hbm.shape[0] // TILES, goals_hbm.shape[1]
    at = [pl.ds(pl.multiple_of(scalars_ref[n] * rows, rows), rows) for n in range(count)]
    loads = []
    for n in range(count):
        here = slice(n * rows, (n + 1) * rows)
        load = [pltpu.make_async_copy(grad_hbm[n], grads.at[here], grad_sems.at[n])]
        if with_sum:
            load.append(pltpu.make_async_copy(goals_hbm.at[at[n]], goals.at[here], goal_sems.at[n]))
        loads.append(load)
    for load in loads:
        load[0].start()
    if with_grad:
        load_weight = pltpu.make_async_copy(weight_hbm, weight, weight_sem)
        load_weight.start()
    if with_sum:
        for load in loads:
            load[1].start()
        if has_before:
            load_before = pltpu.make_async_copy(before_hbm, total, before_sem)
            load_before.start()
    stores = []
    for load in loads:
        load[0].wait()
    if with_grad:
        load_weight.wait()
        for n in range(count):
            here = slice(n * rows, (n + 1) * rows)
            out[here, :] = dot(grads[here, :], weight[...], BY_ROWS).astype(BF)
            stores.append(pltpu.make_async_copy(out.at[here], out_hbm.at[at[n]], out_sems.at[n]))
            stores[-1].start()
    if with_sum:
        for load in loads:
            load[1].wait()
        share = dot(grads[...], goals[...], OVER_ROWS)
        if has_before:
            load_before.wait()
            total[...] += share
        else:
            total[...] = share
        if split:
            split_rows(total, sum_outs[0], sum_outs[1], scalars_ref[count], FIRST_ORDER)
        else:
            sum_outs[0][...] = total[...]
    for store in stores:
        store.wait()


def goal_backward(own_tile, core_bit, grads, goals, weight, tiles, with_grad, with_sum, before=None, split=False):
    rows, width, units = goals.shape[0] // TILES, goals.shape[1], weight.shape[1]
    scalars = jnp.concatenate([jnp.array(tiles, I32) ^ own_tile, core_bit[None]])
    count = len(tiles)
    operands = [*grads, goals, weight]
    out_specs, shapes, aliases = [], [], {}
    if with_grad:
        out_specs.append(ANYWHERE)
        shapes.append(like(*goals.shape, BF))
    if before is not None:
        operands.append(before)
        if not with_sum:
            aliases = {len(operands): 0}
    if with_sum and split:
        shapes += [like(units // 2, width, F32), like(units // 2, width, BF)]
        out_specs += [whole(shape.shape) for shape in shapes[-2:]]
    elif with_sum:
        shapes.append(like(units, width, F32))
        out_specs.append(whole((units, width)))
    dma = pltpu.SemaphoreType.DMA
    return call(
        functools.partial(goal_backward_kernel, count, with_grad, with_sum, before is not None, split),
        "goal_backward",
        (1,),
        scalars,
        [ANYWHERE] * len(operands),
        out_specs,
        shapes,
        operands,
        [
            pltpu.VMEM((count * rows, units), BF),
            pltpu.VMEM((count * rows, width), BF),
            pltpu.VMEM(weight.shape, BF),
            pltpu.VMEM((count * rows, width), BF),
            pltpu.VMEM((units, width), F32),
            dma((count,)),
            dma((count,)),
            dma,
            dma,
            dma((count,)),
        ],
        aliases,
        BRIEF if with_sum else LONG,
    )


def fold_kernel(_, kept_mine_ref, got_mine_ref, kept_other_ref, got_other_ref, kept_ref, sent_ref):
    kept_ref[...] = kept_mine_ref[...] + got_mine_ref[...].astype(F32)
    sent_ref[...] = (kept_other_ref[...] + got_other_ref[...].astype(F32)).astype(BF)


def fold(kept, got, bit_value):
    rows, width = kept.shape[0] // 2, kept.shape[1]
    block = min(rows, 64)
    steps = rows // block
    mine = pl.BlockSpec((block, width), lambda i, bit: (bit[0] * steps + i, 0))
    other = pl.BlockSpec((block, width), lambda i, bit: ((1 - bit[0]) * steps + i, 0))
    straight = pl.BlockSpec((block, width), lambda i, bit: (i, 0))
    return call(
        fold_kernel,
        "fold",
        (steps,),
        bit_value[None],
        [mine, mine, other, other],
        [straight, straight],
        [like(rows, width, F32), like(rows, width, BF)],
        [kept, got, kept, got],
    )


def spread_kernel(count, own_ref, kept_ref, got_ref, *out_refs):
    own = own_ref[0]
    size = kept_ref.shape[0] // count
    for offset in range(count):
        here = pl.ds(pl.multiple_of((own ^ offset) * size, size), size)
        total = kept_ref[here, :] + got_ref[here, :].astype(F32)
        out_refs[offset][...] = total.astype(out_refs[offset].dtype)


def round_kernel(_, kept_ref, got_ref, out_ref):
    out_ref[...] = (kept_ref[...] + got_ref[...].astype(F32)).astype(BF)


def finish_kernel(loss_factor, _, states_ref, *refs):
    goal_refs, refs = refs[:-6], refs[-6:]
    first_ref, hidden_ref, gain_ref, shift_ref, out_ref, loss_ref = refs
    layers, share, units = hidden_ref.shape
    total = sum(states_ref[n * share : (n + 1) * share, :].astype(F32) for n in range(states_ref.shape[0] // share))
    goal_total = sum(ref[...].astype(F32) for ref in goal_refs)
    feat_width = first_ref.shape[1] - goal_total.shape[1]
    first_ref[:, 0:feat_width] = total[:, 0:feat_width]
    first_ref[:, feat_width:] = goal_total
    for layer in range(layers):
        start = feat_width + layer * units
        hidden_ref[layer] = total[:, start : start + units]
    rest = total[:, feat_width + layers * units :].T
    parts = 2 * layers + 4
    rest = rest[:parts] + rest[parts : 2 * parts]
    gain_ref[...] = rest[: layers + 1]
    shift_ref[...] = rest[layers + 1 : 2 * layers + 2]
    out_ref[...] = rest[2 * layers + 2 : 2 * layers + 3]
    loss_ref[...] = rest[2 * layers + 3 :, 0:1] * loss_factor


def swap_bit(block, bit, dp_count, mp_count):
    if bit < 2:
        return lax.ppermute(block, "mp", xor_pairs(mp_count, 1 << bit))
    return lax.ppermute(block, "dp", xor_pairs(dp_count, 1 << (bit - 2)))


def sum_plain(partial, dp_count):
    return lax.psum_scatter(partial, ("dp", "mp"), scatter_dimension=0, tiled=True)


def across(block, tile, dp_count):
    per = dp_count // TILES
    moved = block if tile == 0 else lax.ppermute(block, "dp", xor_pairs(dp_count, tile * per))
    if per == 1:
        return moved
    groups = [[group * per + low for low in range(per)] for group in range(TILES)]
    parts = moved.reshape((per, block.shape[0] // per) + block.shape[1:])
    parts = lax.all_to_all(parts, "dp", 0, 0, axis_index_groups=groups, tiled=True)
    return parts.reshape(block.shape)


def shards(
    states, dest_device, goals, returns, weight_in, weight_hidden, norm_gain, norm_shift, weight_out
):
    dp_count, mp_count = lax.axis_size("dp"), lax.axis_size("mp")
    own_dp, own_mp = lax.axis_index("dp"), lax.axis_index("mp")
    number = own_dp * mp_count + own_mp
    core_bit = number & 1
    tokens, feat_width = states.shape
    all_rows = tokens * dp_count * mp_count
    slot_count, goal_width = goals.shape
    capacity = slot_count // dp_count
    shard_in, units = weight_in.shape
    layers = norm_gain.shape[0]
    shard_units = norm_gain.shape[1]
    per = dp_count // TILES
    rows = slot_count // TILES
    own_tile = own_dp // per
    single = per == 1
    swap, cross = xor_pairs(4, 1), xor_pairs(4, 2)

    small = jnp.concatenate([norm_gain, norm_shift, weight_out[None, :]], axis=0)
    small = jnp.pad(small.reshape(-1), (0, 16 * units - small.size)).reshape(16, units)
    others = jnp.concatenate([weight_hidden.reshape((layers - 1) * shard_units, units), small], axis=0)
    other_rows = others.shape[0]
    if single:
        key_row, message = route(
            own_dp, dest_device.reshape(1, tokens), returns.reshape(dp_count, capacity), units
        )
    else:
        dest = dest_device[:, 0]
        offset = ((dest // per) ^ own_tile) * per + dest % per
        blocks = tokens // 128
        marks = (offset[None, :] == jnp.arange(dp_count, dtype=I32)[:, None]).astype(F32)
        marks = marks.reshape(dp_count, blocks, 128)
        upper = jnp.arange(128)[:, None] < jnp.arange(128)[None, :]
        within = dot(marks.astype(BF), upper.astype(BF), ((2,), (0,)))
        block_sums = jnp.sum(marks, axis=2)
        earlier = jnp.arange(blocks)[None, :] < jnp.arange(blocks)[:, None]
        ahead = jnp.sum(jnp.where(earlier[None], block_sums[:, None, :], 0.0), axis=2)
        rank = jnp.sum(marks * (within + ahead[:, :, None]), axis=0).reshape(tokens)
        key = offset * capacity + rank.astype(I32)
        key_row = key[None, :]
        valid = jnp.arange(capacity, dtype=F32)[None, :] < jnp.sum(block_sums, axis=1)[:, None]
        tile_returns = returns.reshape(TILES, rows)
        got_returns = [
            across(lax.dynamic_index_in_dim(tile_returns, own_tile ^ t, 0, keepdims=False), t, dp_count)
            for t in range(TILES)
        ]
        got_returns = jnp.stack(got_returns).reshape(dp_count, capacity).astype(F32)
        square_total = lax.psum(jnp.sum(jnp.where(valid, got_returns * got_returns, 0.0)), ("dp", "mp"))
        scale_value = jnp.sqrt(square_total / all_rows + 1e-06)
        targets = jnp.stack(
            [got_returns / scale_value, valid.astype(F32), jnp.full(valid.shape, 1.0 / all_rows, F32)]
            + [jnp.zeros(valid.shape, F32)] * 5
        )
        targets = targets.reshape(8, TILES // 2, 2 * rows).transpose(1, 0, 2)

    cut = feat_width % shard_in
    first_goal_shard = feat_width // shard_in
    one = lax.ppermute(weight_in, "mp", swap)
    two = lax.ppermute(weight_in, "mp", cross)
    if single:
        messages = message
        for bit in (4, 2, 1):
            messages = jnp.concatenate([messages, lax.ppermute(messages, "dp", xor_pairs(dp_count, bit))], axis=0)
        two = after(two, messages)
    pieces = (weight_in, one, two, lax.ppermute(two, "mp", swap))

    *parts, goal_weight = goal_forward(own_tile, own_mp, goals, pieces, cut, first_goal_shard)
    if single:
        others = jnp.concatenate([others, after(messages, goal_weight)], axis=0)
    others_one = lax.ppermute(others, "mp", swap)
    others_two = lax.ppermute(others, "mp", cross)
    others_three = lax.ppermute(others_two, "mp", swap)

    state_part, state_weight = state_forward(after(own_mp, goal_weight), states, pieces, cut, first_goal_shard)
    parts = [across(after(part, state_part) if tile > 4 else part, tile, dp_count) for tile, part in enumerate(parts)]
    prepared = prepare(
        after(own_mp, *[parts[tile] for tile in (1, 2, 3, 4)]), [others, others_one, others_two, others_three],
        layers, other_rows, rows, float(all_rows),
    )
    hidden, vectors, out_weight = prepared[:3]
    if single:
        targets = prepared[3]

    running, back, made_of = None, {}, {}
    for tiles in (NEAR, FAR_ONE, FAR_TWO):
        made = critic(
            own_dp, key_row, targets, state_part, hidden, vectors, out_weight,
            [parts[t] for t in tiles], tiles, running, tiles == FAR_TWO,
        )
        running = (made[-2], made[-1], made[len(tiles)])
        made_of.update(zip(tiles, made))
        if tiles == FAR_ONE:
            for tile in NEAR + FAR_ONE:
                back[tile] = across(after(made_of[tile], made_of[FAR_ONE[0]], *[parts[u] for u in FAR_TWO]), tile, dp_count)
    for tile in FAR_TWO:
        back[tile] = across(after(made_of[tile], *[back[u] for u in NEAR + FAR_ONE]), tile, dp_count)
    first, rest = made[-2], made[-1]

    state_made = state_weight_grad(core_bit, key_row, first, states, rest, single)

    early = NEAR + FAR_ONE
    if single:
        kept, sent = state_made[1:]
        sent = after(sent, *[back[t] for t in early])
        states_kept, sent = fold(kept, swap_bit(sent, CORE, dp_count, mp_count), (number >> Y) & 1)
        states_got = swap_bit(sent, Y, dp_count, mp_count)
        back[0] = after(back[0], states_kept)
    grad_goals, running_sum = goal_backward(
        own_tile, core_bit, [back[t] for t in early], goals, goal_weight, early, True, True
    )
    if single:
        grad_states = state_grad(own_dp, after(state_made[0], running_sum), state_weight)
        states_got = after(states_got, grad_states)
        block = call(
            round_kernel, "round", (1,), own_dp[None], [whole(states_kept.shape)] * 2, [whole(states_kept.shape)],
            [like(*states_kept.shape, BF)], [states_kept, states_got],
        )[0]
        running_sum = after(running_sum, block)
    goal_made = goal_backward(
        own_tile, core_bit, [back[t] for t in FAR_TWO], goals, goal_weight, FAR_TWO, False, True,
        running_sum, single,
    )

    share = units // (dp_count * mp_count)
    if single:
        goals_kept, goals_sent = goal_made
        goals_got = swap_bit(goals_sent, CORE, dp_count, mp_count)
        goals_kept, goals_sent = fold(goals_kept, goals_got, (number >> Y) & 1)
        goals_got = swap_bit(goals_sent, Y, dp_count, mp_count)
        grad_goals = goal_backward(
            own_tile, core_bit, [after(back[t], goals_kept) for t in FAR_TWO], goals, goal_weight, FAR_TWO, True, False,
            grad_goals,
        )[0]
        block = lax.all_to_all(block.reshape(dp_count, share, -1), "dp", 0, 0, tiled=True)
        arrived = [block.reshape(dp_count * share, -1)]
        blocks = call(
            functools.partial(spread_kernel, dp_count), "spread", (1,), own_dp[None],
            [whole(goals_kept.shape)] * 2,
            [whole((share, goal_width))] * dp_count,
            [like(share, goal_width, F32)] + [like(share, goal_width, BF)] * (dp_count - 1),
            [after(goals_kept, grad_goals), goals_got],
        )
        arrived += [blocks[0]] + [
            lax.ppermute(blocks[o], "dp", xor_pairs(dp_count, o)) for o in range(1, dp_count)
        ]
        shapes = [
            like(share, feat_width + goal_width, F32), like(layers - 1, share, units, F32),
            like(layers, share, F32), like(layers, share, F32), like(1, share, F32), like(1, 1, F32),
        ]
        first_share, hidden_share, gain_grad, shift_grad, out_grad, loss = call(
            functools.partial(finish_kernel, 0.5 / all_rows),
            "finish", (1,), core_bit[None],
            [whole(block.shape) for block in arrived],
            [whole(shape.shape) for shape in shapes],
            shapes,
            arrived,
        )
    else:
        grad_goals = goal_backward(
            own_tile, core_bit, [after(back[t], goal_made[0]) for t in FAR_TWO], goals, goal_weight, FAR_TWO, True, False,
            grad_goals,
        )[0]
        grad_states = state_grad(own_dp, state_made[0], state_weight)
        total = sum_plain(state_made[1], dp_count)
        hidden_share = total[:, feat_width : feat_width + (layers - 1) * units]
        hidden_share = hidden_share.reshape(share, layers - 1, units).transpose(1, 0, 2)
        rest = total[:, feat_width + (layers - 1) * units :]
        first_share = jnp.concatenate([total[:, :feat_width], sum_plain(goal_made[0], dp_count)], axis=1)

        count = 2 * layers + 2
        rest = (rest[:, :count] + rest[:, count : 2 * count]).T
        gain_grad, shift_grad, out_grad = rest[:layers], rest[layers : 2 * layers], rest[2 * layers]
        loss = 0.5 * rest[count - 1, 0] / all_rows
    return (
        loss.reshape(()),
        grad_states,
        grad_goals,
        first_share.T,
        hidden_share.transpose(0, 2, 1),
        gain_grad,
        shift_grad,
        out_grad.reshape(share),
    )


def solution(mesh):
    placed = (
        P(("dp", "mp"), None),
        P(("dp", "mp"), None),
        P(("dp", "mp"), None),
        P(("dp", "mp")),
        P("mp", None),
        P(None, "mp", None),
        P(None, "mp"),
        P(None, "mp"),
        P("mp"),
    )
    return jax.shard_map(
        shards,
        mesh=mesh,
        in_specs=placed,
        out_specs=(
            P(),
            P(("dp", "mp"), None),
            P(("dp", "mp"), None),
            P(None, ("dp", "mp")),
            P(None, None, ("dp", "mp")),
            P(None, ("dp", "mp")),
            P(None, ("dp", "mp")),
            P(("dp", "mp")),
        ),
        check_vma=False,
    )
```

```python
import functools

import jax
import jax.numpy as jnp
from jax import lax
from jax.experimental import pallas as pl
from jax.experimental.pallas import tpu as pltpu
from jax.sharding import PartitionSpec as P

BF = jnp.bfloat16
F32 = jnp.float32
I32 = jnp.int32
TILES = 8
STEP = 64
VMEM = 63 * 1024 * 1024 + 512 * 1024
NEAR, FAR_ONE, FAR_TWO = (0, 1, 2, 3), (4, 5), (6, 7)
BRIEF = pl.CostEstimate(flops=1, bytes_accessed=1, transcendentals=0)
LONG = pl.CostEstimate(flops=9_000_000_000, bytes_accessed=10_000_000, transcendentals=0)
CORE, Y, X, Z_LOW, Z_HIGH = range(5)
FIRST_ORDER = (CORE, Y, Z_HIGH, Z_LOW, X)


def dot(first, second, dims):
    return lax.dot_general(first, second, (dims, ((), ())), preferred_element_type=F32)


ROWS_BY_COLUMNS, BY_ROWS, OVER_ROWS = ((1,), (0,)), ((1,), (1,)), ((0,), (0,))


def after(value, *others):
    return lax.optimization_barrier((value, *others))[0]


def xor_pairs(count, bits):
    return [(i, i ^ bits) for i in range(count)]


def like(*shape_and_type):
    *shape, dtype = shape_and_type
    return jax.ShapeDtypeStruct(tuple(shape), dtype)


def whole(shape):
    return pl.BlockSpec(tuple(shape), lambda *_: (0,) * len(shape))


ANYWHERE = pl.BlockSpec(memory_space=pl.ANY)


def call(kernel, name, grid, scalars, in_specs, out_specs, out_shape, operands, scratch=(), aliases=None, cost=BRIEF):
    return pl.pallas_call(
        kernel,
        out_shape=out_shape,
        grid_spec=pltpu.PrefetchScalarGridSpec(
            num_scalar_prefetch=1,
            grid=grid,
            in_specs=in_specs,
            out_specs=out_specs,
            scratch_shapes=list(scratch),
        ),
        input_output_aliases=aliases or {},
        compiler_params=pltpu.CompilerParams(vmem_limit_bytes=VMEM),
        cost_estimate=cost,
        name=name,
    )(scalars, *operands)


def route_kernel(capacity, own_ref, dest_ref, returns_ref, row_ref, message_ref, wide, text):
    own = own_ref[0]
    tokens = dest_ref.shape[1]
    count = returns_ref.shape[0]
    blocks = tokens // 128
    offsets = dest_ref[...] ^ own
    marks = (lax.broadcasted_iota(I32, (count, tokens), 0) == offsets).astype(F32)
    stacked = jnp.concatenate([marks[:, 128 * b : 128 * b + 128] for b in range(blocks)], axis=0)
    upper = lax.broadcasted_iota(I32, (128, 128), 0) < lax.broadcasted_iota(I32, (128, 128), 1)
    within = dot(stacked.astype(BF), upper.astype(F32).astype(BF), ROWS_BY_COLUMNS)
    totals = jnp.sum(stacked, axis=1, keepdims=True)
    ahead = jnp.zeros((count, 1), F32)
    for b in range(blocks):
        part = slice(count * b, count * b + count)
        lanes = slice(128 * b, 128 * b + 128)
        rank = jnp.sum(stacked[part] * (within[part] + ahead), axis=0, keepdims=True)
        key = offsets[:, lanes].astype(F32) * capacity + rank
        row_ref[:, lanes] = key.astype(I32)
        ahead = ahead + totals[part]
    wide[...] = returns_ref[...].astype(F32)
    lane = lax.broadcasted_iota(I32, text.shape, 1) - (text.shape[1] - 128)
    high = jnp.floor(ahead * 0.0625)
    text[...] = jnp.where(lane == 0, high, jnp.where(lane == 1, ahead - 16.0 * high, 0.0))
    for offset in range(count):
        text[offset : offset + 1, 0:capacity] = wide[pl.ds(own ^ offset, 1), :]
    message_ref[...] = text[...].astype(BF)


def route(own, dest_row, returns, units):
    tokens, (count, capacity) = dest_row.shape[1], returns.shape
    return call(
        functools.partial(route_kernel, capacity),
        "route",
        (1,),
        own[None],
        [whole(dest_row.shape), whole(returns.shape)],
        [whole((1, tokens)), whole((count, units))],
        [like(1, tokens, I32), like(count, units, BF)],
        [dest_row, returns],
        [pltpu.VMEM(returns.shape, F32), pltpu.VMEM((count, units), F32)],
    )


def reverse(bits):
    return (bits % 2) * 4 + (bits // 2 % 2) * 2 + bits // 4


def prepare_kernel(layers, rows, capacity, total_rows, own_ref, *refs):
    pieces, refs = refs[:4], refs[4:]
    hidden_ref, vectors_ref, out_weight_ref = refs[:3]
    own = own_ref[0]
    width = hidden_ref.shape[2] // 4
    for shard in range(4):
        columns = slice(shard * width, (shard + 1) * width)
        for value in range(4):

            @pl.when(own == value)
            def _():
                piece = pieces[shard ^ value]
                for layer in range(layers - 1):
                    hidden_ref[layer, columns, :] = piece[layer * width : (layer + 1) * width, :]
                start = (layers - 1) * width
                small = piece[start : start + 16, :].astype(F32)
                for row in range(2 * layers + 1):
                    vectors_ref[row : row + 1, columns] = small[
                        row // 4 : row // 4 + 1, (row % 4) * width : (row % 4 + 1) * width
                    ]

    vectors_ref[2 * layers + 1 :, :] = jnp.zeros((16 - 2 * layers - 1, vectors_ref.shape[1]), F32)
    out_weight_ref[...] = jnp.concatenate(
        [vectors_ref[2 * layers : 2 * layers + 1, :], jnp.zeros((7, vectors_ref.shape[1]), F32)], axis=0
    ).astype(BF)
    if len(refs) == 3:
        return
    targets_ref = refs[3]
    targets_ref[...] = jnp.zeros_like(targets_ref)
    index = lax.broadcasted_iota(I32, (64, 64), 0)
    partner = (reverse(reverse(index // 8) ^ (index % 8))) * 8 + index % 8
    swap = (lax.broadcasted_iota(I32, (64, 64), 1) == partner).astype(F32).astype(BF)
    lane = lax.broadcasted_iota(I32, (64, 128 * 3), 1).astype(F32)
    total = jnp.zeros((1, 1), F32)
    for piece in pieces:
        message = piece[rows : rows + 64, :]
        counts = dot(swap, message[:, 384:512], ROWS_BY_COLUMNS)
        counts = counts[:, 0:1] * 16.0 + counts[:, 1:2]
        values = message[:, 0:384].astype(F32)
        squares = jnp.sum(jnp.where(lane < counts, values * values, 0.0), axis=1, keepdims=True)
        total = total + jnp.sum(squares, axis=0, keepdims=True)
    scale = jnp.sqrt(total / total_rows + 1e-06)
    message = pieces[0][rows : rows + 64, :].astype(F32)
    counts = message[0:8, 384:385] * 16.0 + message[0:8, 385:386]
    for tile in range(TILES):
        lanes = slice((tile % 2) * capacity, (tile % 2) * capacity + capacity)
        row = reverse(tile) * 8 + tile
        target = message[row : row + 1, 0:384] / scale
        filled = (lane[0:1] < counts[tile : tile + 1]).astype(F32)
        targets_ref[tile // 2, 0:1, lanes] = target[:, 0:capacity]
        targets_ref[tile // 2, 1:2, lanes] = filled[:, 0:capacity]
        targets_ref[tile // 2, 2:3, lanes] = jnp.full((1, capacity), 1.0 / total_rows, F32)


def prepare(own, pieces, layers, rows, capacity, total_rows):
    units = pieces[0].shape[1]
    shapes = [like(layers - 1, units, units, BF), like(16, units, F32), like(8, units, BF)]
    if pieces[0].shape[0] > rows:
        shapes.append(like(TILES // 2, 8, 2 * capacity, F32))
    return call(
        functools.partial(prepare_kernel, layers, rows, capacity, total_rows),
        "prepare",
        (1,),
        own[None],
        [whole(piece.shape) for piece in pieces],
        [whole(shape.shape) for shape in shapes],
        shapes,
        pieces,
    )


def fetch(own, parts, target_ref, sems, later=()):
    place = 0
    for number, (shard, candidates) in enumerate(parts):
        size = candidates[0].shape[0]
        there = target_ref.at[place : place + size]
        for value in range(4):

            @pl.when(own == value)
            def _():
                pltpu.make_async_copy(candidates[shard ^ value], there, sems.at[number]).start()

        place += size
    for copy in later:
        copy.start()
    place = 0
    for number, (shard, candidates) in enumerate(parts):
        size = candidates[0].shape[0]
        there = target_ref.at[place : place + size]
        pltpu.make_async_copy(candidates[0], there, sems.at[number]).wait()
        place += size


def first_weight_parts(pieces, cut, shards, first, last):
    parts = []
    for shard in shards:
        here = slice(cut if shard == first else 0, cut if shard == last else pieces[0].shape[0])
        parts.append((shard, [piece.at[here] for piece in pieces]))
    return parts


def goal_forward_kernel(cut, first_shard, scalars_ref, goals_hbm, *refs):
    pieces, refs = refs[:4], refs[4:]
    out_refs, weight_out, refs = refs[:TILES], refs[TILES], refs[TILES + 1 :]
    goals, weight, made, sems, out_sems, fetch_sems, weight_sem = refs
    rows = goals_hbm.shape[0] // TILES
    order = [*NEAR[1:], *FAR_ONE, *FAR_TWO, 0]
    copies = []
    for place, tile in enumerate(order):
        there = goals_hbm.at[pl.ds(pl.multiple_of((scalars_ref[0] ^ tile) * rows, rows), rows)]
        here = goals.at[place * rows : (place + 1) * rows]
        copies.append(pltpu.make_async_copy(there, here, sems.at[place]))
    for copy in copies[:2]:
        copy.start()
    parts = first_weight_parts(pieces, cut, range(first_shard, 4), first_shard, None)
    fetch(scalars_ref[1], parts, weight, fetch_sems, copies[2:])
    sent = [pltpu.make_async_copy(weight, weight_out, weight_sem)]
    sent[0].start()
    for pair in range(TILES // 2):
        for copy in copies[2 * pair : 2 * pair + 2]:
            copy.wait()
        both = slice(2 * pair * rows, (2 * pair + 2) * rows)
        made[both, :] = dot(goals[both, :], weight[...], ROWS_BY_COLUMNS).astype(BF)
        for place in (2 * pair, 2 * pair + 1):
            here = made.at[place * rows : (place + 1) * rows]
            sent.append(pltpu.make_async_copy(here, out_refs[order[place]], out_sems.at[place]))
            sent[-1].start()
    for copy in sent:
        copy.wait()


def goal_forward(own_tile, own_mp, goals, pieces, cut, first_shard):
    width = goals.shape[1]
    rows, units = goals.shape[0] // TILES, pieces[0].shape[1]
    dma = pltpu.SemaphoreType.DMA
    return call(
        functools.partial(goal_forward_kernel, cut, first_shard),
        "goal_forward",
        (1,),
        jnp.stack([own_tile, own_mp]),
        [ANYWHERE] * 5,
        [ANYWHERE] * (TILES + 1),
        [like(rows, units, BF)] * TILES + [like(width, units, BF)],
        [goals, *pieces],
        [
            pltpu.VMEM(goals.shape, BF),
            pltpu.VMEM((width, units), BF),
            pltpu.VMEM((TILES * rows, units), BF),
            dma((TILES,)),
            dma((TILES,)),
            dma((4,)),
            dma,
        ],
    )


def state_forward_kernel(steps, cut, last_shard, own_ref, states_hbm, *refs):
    pieces, (out_hbm, weight_out), refs = refs[:4], refs[4:6], refs[6:]
    states, weight, made, sems, out_sems, fetch_sems, weight_sem = refs
    rows = states.shape[0] // steps
    copies = []
    for step in range(steps):
        here = slice(step * rows, (step + 1) * rows)
        copies.append(pltpu.make_async_copy(states_hbm.at[here], states.at[here], sems.at[step]))
    copies[0].start()
    parts = first_weight_parts(pieces, cut, range(last_shard + 1), None, last_shard)
    fetch(own_ref[0], parts, weight, fetch_sems, copies[1:])
    sent = [pltpu.make_async_copy(weight, weight_out, weight_sem)]
    sent[0].start()
    for step in range(steps):
        copies[step].wait()
        here = slice(step * rows, (step + 1) * rows)
        made[here, :] = dot(states[here, :], weight[...], ROWS_BY_COLUMNS).astype(BF)
        sent.append(pltpu.make_async_copy(made.at[here], out_hbm.at[here], out_sems.at[step]))
        sent[-1].start()
    for copy in sent:
        copy.wait()


def state_forward(own, states, pieces, cut, last_shard):
    tokens, width = states.shape
    units = pieces[0].shape[1]
    steps = 4
    dma = pltpu.SemaphoreType.DMA
    return call(
        functools.partial(state_forward_kernel, steps, cut, last_shard),
        "state_forward",
        (1,),
        own[None],
        [ANYWHERE] * 5,
        [ANYWHERE] * 2,
        [like(tokens, units, BF), like(width, units, BF)],
        [states, *pieces],
        [
            pltpu.VMEM(states.shape, BF),
            pltpu.VMEM((width, units), BF),
            pltpu.VMEM((tokens, units), BF),
            dma((steps,)),
            dma((steps,)),
            dma((4,)),
            dma,
        ],
    )


def split_rows(total_ref, kept_ref, sent_ref, bit_value, order):
    parts = 1 << len(order)
    size = total_ref.shape[0] // parts
    for place in range(parts // 2):
        number = 0
        for depth, bit in enumerate(order[1:]):
            number += ((place >> (len(order) - 2 - depth)) & 1) << bit
        here = slice(place * size, (place + 1) * size)
        mine = pl.multiple_of((number + (bit_value << order[0])) * size, size)
        other = pl.multiple_of((number + ((1 - bit_value) << order[0])) * size, size)
        kept_ref[here, :] = total_ref[pl.ds(mine, size), :]
        sent_ref[here, :] = total_ref[pl.ds(other, size), :].astype(BF)


def critic_kernel(pairs, first_pair, layers, first_call, last_call, _, *refs):
    key_ref, target_ref, states_ref, hidden_ref, vectors_ref, out_weight_ref = refs[:6]
    refs = refs[6:]
    goal_refs, refs = refs[: 2 * pairs], refs[2 * pairs :]
    if not first_call:
        shares_before_hbm, sums_before_ref = refs[:2]
        refs = refs[3:]
    first_refs, refs = refs[: 2 * pairs], refs[2 * pairs :]
    all_first_ref, refs = refs[0], refs[1:]
    if last_call:
        total_ref, refs = refs[0], refs[1:]
    else:
        shares_ref, sums_ref = refs[:2]
        refs = refs[2:]
    work, nhat, slope, spread, acts, low_grad = refs[:6]
    if last_call:
        sums_ref = refs[6]
        share_at = lambda layer: total_ref.at[:, layer * work.shape[1] : (layer + 1) * work.shape[1]]
    else:
        share_at = lambda layer: shares_ref.at[layer]
    step = pl.program_id(0)
    rows, units = work.shape
    if not first_call:
        loads = [
            pltpu.make_async_copy(shares_before_hbm.at[layer], share_at(layer), refs[-1].at[layer])
            for layer in range(layers - 1)
        ]
        for load in loads:
            load.start()
    half = rows // 2
    tokens = key_ref.shape[1]
    steps = rows // STEP

    @pl.when(step == 0)
    def _():
        if first_call:
            for layer in range(layers - 1):
                share_at(layer)[...] = jnp.zeros((units, units), F32)
        sums_ref[...] = jnp.zeros_like(sums_ref) if first_call else sums_before_ref[...]

    for pair in range(pairs):

        @pl.when(step == pair)
        def _():
            low_grad[0:half, :] = goal_refs[2 * pair][...]
            low_grad[half:rows, :] = goal_refs[2 * pair + 1][...]

    base = (first_pair + step) * rows
    slot = base + lax.broadcasted_iota(I32, (rows, tokens), 0)
    pick = (slot == key_ref[...]).astype(F32).astype(BF)
    work[...] = dot(pick, states_ref[...], ROWS_BY_COLUMNS) + low_grad[...].astype(F32)

    for layer in range(layers):
        gain = vectors_ref[layer : layer + 1, :]
        shift = vectors_ref[layers + layer : layers + layer + 1, :]
        for i in range(steps):
            here = slice(i * STEP, (i + 1) * STEP)
            values = work[here, :]
            center = values - jnp.mean(values, axis=1, keepdims=True)
            inverse = lax.rsqrt(jnp.mean(center * center, axis=1, keepdims=True) + 1e-05)
            scaled = center * inverse
            shifted = scaled * gain + shift
            slopes = jnp.exp(jnp.minimum(shifted, 0.0))
            nhat[layer, here, :] = scaled
            slope[layer, here, :] = slopes
            spread[layer, here, :] = inverse
            acts[layer, here, :] = (jnp.maximum(shifted, 0.0) + (slopes - 1.0)).astype(BF)
        if layer < layers - 1:
            work[...] = dot(acts[layer], hidden_ref[layer], ROWS_BY_COLUMNS)

    out_weight = out_weight_ref[...]
    last = acts[layers - 1]
    value = dot(out_weight, last, BY_ROWS)
    target = target_ref[0]
    error = (value[0:1, :] - target[0:1, :]) * target[1:2, :]
    grad_value = (error * target[2:3, :]).astype(BF)
    grad_rows = jnp.concatenate([grad_value.astype(F32), jnp.zeros((7, rows), F32)], axis=0).astype(BF)
    sums_ref[2 * layers] += dot(grad_rows, last, ROWS_BY_COLUMNS)
    sums_ref[2 * layers + 1] += jnp.broadcast_to(jnp.sum(error * error, axis=1, keepdims=True), (8, units))
    work[...] = dot(grad_rows, out_weight, OVER_ROWS)

    if not first_call:
        for load in loads:
            load.wait()
    for layer in reversed(range(layers)):
        gain = vectors_ref[layer : layer + 1, :]
        for i in range(steps):
            here = slice(i * STEP, (i + 1) * STEP)
            scaled = nhat[layer, here, :]
            grad_norm = work[here, :] * slope[layer, here, :]
            by_scaled = grad_norm * scaled
            sums_ref[layer] += jnp.sum(by_scaled.reshape(STEP // 8, 8, units), axis=0)
            sums_ref[layers + layer] += jnp.sum(grad_norm.reshape(STEP // 8, 8, units), axis=0)
            grad_scaled = grad_norm * gain
            first_mean = jnp.mean(grad_scaled, axis=1, keepdims=True)
            second_mean = jnp.mean(by_scaled * gain, axis=1, keepdims=True)
            grad = spread[layer, here, :] * (grad_scaled - first_mean - scaled * second_mean)
            low_grad[here, :] = grad.astype(BF)
        if layer > 0:
            grads = low_grad[...]
            work[...] = dot(grads, hidden_ref[layer - 1], BY_ROWS)
            share_at(layer - 1)[...] += dot(grads, acts[layer - 1], OVER_ROWS)

    all_first_ref[...] = low_grad[...]
    for pair in range(pairs):

        @pl.when(step == pair)
        def _():
            first_refs[2 * pair][...] = low_grad[0:half, :]
            first_refs[2 * pair + 1][...] = low_grad[half:rows, :]

    if last_call:

        @pl.when(step == pairs - 1)
        def _():
            count = 2 * layers + 2
            sums = jnp.concatenate(
                [jnp.sum(sums_ref[row], axis=0, keepdims=True) for row in range(count - 1)]
                + [sums_ref[count - 1][0:1, :]],
                axis=0,
            )
            high = sums.astype(BF).astype(F32)
            columns = jnp.concatenate([high, sums - high, jnp.zeros((128 - 2 * count, units), F32)], axis=0)
            total_ref[:, (layers - 1) * units :] = columns.T


def critic(own, key_row, targets, state_part, hidden, vectors, out_weight, goal_parts, tiles, before, last_call):
    pairs, first_pair = len(tiles) // 2, tiles[0] // 2
    half, units = goal_parts[0].shape
    rows = 2 * half
    layers = hidden.shape[0] + 1
    width = (layers - 1) * units + 128
    sums_shape, shares_shape = (2 * layers + 2, 8, units), (layers - 1, units, units)
    operands = [key_row, targets, state_part, hidden, vectors, out_weight, *goal_parts]
    in_specs = [
        whole(key_row.shape),
        pl.BlockSpec((1,) + targets.shape[1:], lambda i, _: (first_pair + i, 0, 0)),
        whole(state_part.shape),
        whole(hidden.shape),
        whole(vectors.shape),
        whole(out_weight.shape),
    ] + [whole((half, units))] * (2 * pairs)
    aliases = {}
    if before is not None:
        in_specs += [ANYWHERE, whole(sums_shape), ANYWHERE]
        assert pairs == 1
        operands += list(before)
        aliases = {len(operands): 2 * pairs}
    out_shape = [like(half, units, BF)] * (2 * pairs) + [like(TILES * half, units, BF)]
    out_specs = [whole((half, units))] * (2 * pairs) + [
        pl.BlockSpec((rows, units), lambda i, _: (first_pair + i, 0))
    ]
    scratch = [
        pltpu.VMEM((rows, units), F32),
        pltpu.VMEM((layers, rows, units), F32),
        pltpu.VMEM((layers, rows, units), F32),
        pltpu.VMEM((layers, rows, 1), F32),
        pltpu.VMEM((layers, rows, units), BF),
        pltpu.VMEM((rows, units), BF),
    ]
    if last_call:
        shapes = [like(units, width, F32)]
        scratch += [pltpu.VMEM(sums_shape, F32)]
    else:
        shapes = [like(*shares_shape, F32), like(*sums_shape, F32)]
    if before is not None:
        scratch.append(pltpu.SemaphoreType.DMA((layers - 1,)))
    return call(
        functools.partial(critic_kernel, pairs, first_pair, layers, before is None, last_call),
        "critic",
        (pairs,),
        own[None],
        in_specs,
        out_specs + [whole(shape.shape) for shape in shapes],
        out_shape + shapes,
        operands,
        scratch,
        aliases,
    )


def state_weight_kernel(steps, split, core_ref, key_ref, first_hbm, states_hbm, rest_hbm, grad_hbm, *refs):
    outs, refs = refs[: 2 if split else 1], refs[2 if split else 1 :]
    first, states, rest, grad, total, first_sem, states_sems, rest_sem, grad_sems, out_sems = refs[:10]
    pieces = refs[10:]
    slots, units = first.shape
    tokens, width = states.shape
    rows, part = tokens // steps, width // steps
    load_first = pltpu.make_async_copy(first_hbm, first, first_sem)
    load_first.start()
    load_rest = pltpu.make_async_copy(rest_hbm, rest, rest_sem)
    load_rest.start()
    loads = [
        pltpu.make_async_copy(
            states_hbm.at[:, step * part : (step + 1) * part], states.at[:, step * part : (step + 1) * part],
            states_sems.at[step],
        )
        for step in range(steps)
    ]
    for load in loads:
        load.start()
    stores = []

    def give(source, start, number):
        there = slice(start, start + source.shape[1])
        if split:
            split_rows(source, pieces[0].at[:, there], pieces[1].at[:, there], core_ref[0], FIRST_ORDER)
            for which in range(2):
                copy = pltpu.make_async_copy(
                    pieces[which].at[:, there], outs[which].at[:, there], out_sems.at[which, number]
                )
                copy.start()
                stores.append(copy)
        else:
            outs[0][:, there] = source[...]

    load_first.wait()
    for step in range(steps):
        here = slice(step * rows, (step + 1) * rows)
        slot = lax.broadcasted_iota(I32, (slots, rows), 0)
        pick = (slot == key_ref[:, here]).astype(F32).astype(BF)
        grad[here, :] = dot(pick, first[...], OVER_ROWS).astype(BF)
    load_rest.wait()
    give(rest, width, steps)
    store_grad = pltpu.make_async_copy(grad, grad_hbm, grad_sems)
    store_grad.start()
    for step in range(steps):
        loads[step].wait()
        here = slice(step * part, (step + 1) * part)
        total[:, here] = dot(grad[...], states[:, here], OVER_ROWS)
        give(total.at[:, here], step * part, step)
    store_grad.wait()
    for store in stores:
        store.wait()


def state_weight_grad(core_bit, key_row, first, states, rest, split):
    tokens, width = states.shape
    slots, units = first.shape
    steps = 4
    columns = width + rest.shape[1]
    shapes = [like(units // 2, columns, F32), like(units // 2, columns, BF)] if split else [like(units, columns, F32)]
    dma = pltpu.SemaphoreType.DMA
    return call(
        functools.partial(state_weight_kernel, steps, split),
        "state_weight_grad",
        (1,),
        core_bit[None],
        [whole(key_row.shape), ANYWHERE, ANYWHERE, ANYWHERE],
        [ANYWHERE] * 3 if split else [ANYWHERE, whole(shapes[0].shape)],
        [like(tokens, units, BF)] + shapes,
        [key_row, first, states, rest],
        [
            pltpu.VMEM(first.shape, BF),
            pltpu.VMEM(states.shape, BF),
            pltpu.VMEM(rest.shape, F32),
            pltpu.VMEM((tokens, units), BF),
            pltpu.VMEM((units, width), F32),
            dma,
            dma((steps,)),
            dma,
            dma,
            dma((2, steps + 1)),
        ]
        + ([pltpu.VMEM(shape.shape, shape.dtype) for shape in shapes] if split else []),
    )


def state_grad_kernel(steps, _, grad_hbm, weight_hbm, out_hbm, grad, weight, out, grad_sem, weight_sem, sems):
    rows = out.shape[1]
    load_weight = pltpu.make_async_copy(weight_hbm, weight, weight_sem)
    load_weight.start()
    load_grad = pltpu.make_async_copy(grad_hbm, grad, grad_sem)
    load_grad.start()
    load_weight.wait()
    load_grad.wait()
    stores = []
    for step in range(steps):
        here = slice(step * rows, (step + 1) * rows)
        out[step] = dot(grad[here, :], weight[...], BY_ROWS).astype(BF)
        stores.append(pltpu.make_async_copy(out.at[step], out_hbm.at[here], sems.at[step]))
        stores[-1].start()
    for store in stores:
        store.wait()


def state_grad(own, grad, weight):
    tokens, units = grad.shape
    width = weight.shape[0]
    steps = 4
    dma = pltpu.SemaphoreType.DMA
    return call(
        functools.partial(state_grad_kernel, steps),
        "state_grad",
        (1,),
        own[None],
        [ANYWHERE] * 2,
        [ANYWHERE],
        [like(tokens, width, BF)],
        [grad, weight],
        [
            pltpu.VMEM(grad.shape, BF),
            pltpu.VMEM(weight.shape, BF),
            pltpu.VMEM((steps, tokens // steps, width), BF),
            dma,
            dma,
            dma((steps,)),
        ],
        cost=BRIEF,
    )[0]


def goal_backward_kernel(count, with_grad, with_sum, has_before, split, scalars_ref, *refs):
    grad_hbm, refs = refs[:count], refs[count:]
    goals_hbm, weight_hbm, refs = refs[0], refs[1], refs[2:]
    if has_before:
        before_hbm, refs = refs[0], refs[1:]
    if with_grad:
        out_hbm, refs = refs[0], refs[1:]
    if with_sum:
        sum_outs, refs = refs[: 2 if split else 1], refs[2 if split else 1 :]
    grads, goals, weight, out, total, grad_sems, goal_sems, weight_sem, before_sem, out_sems = refs
    rows, width = goals_hbm.shape[0] // TILES, goals_hbm.shape[1]
    at = [pl.ds(pl.multiple_of(scalars_ref[n] * rows, rows), rows) for n in range(count)]
    loads = []
    for n in range(count):
        here = slice(n * rows, (n + 1) * rows)
        load = [pltpu.make_async_copy(grad_hbm[n], grads.at[here], grad_sems.at[n])]
        if with_sum:
            load.append(pltpu.make_async_copy(goals_hbm.at[at[n]], goals.at[here], goal_sems.at[n]))
        loads.append(load)
    for load in loads:
        load[0].start()
    if with_sum:
        for load in loads:
            load[1].start()
        if has_before:
            load_before = pltpu.make_async_copy(before_hbm, total, before_sem)
            load_before.start()
    if with_grad:
        load_weight = pltpu.make_async_copy(weight_hbm, weight, weight_sem)
        load_weight.start()
    stores = []
    for load in loads:
        load[0].wait()
    if with_sum:
        for load in loads:
            load[1].wait()
        share = dot(grads[...], goals[...], OVER_ROWS)
        if has_before:
            load_before.wait()
            total[...] += share
        else:
            total[...] = share
        if split:
            split_rows(total, sum_outs[0], sum_outs[1], scalars_ref[count], FIRST_ORDER)
        else:
            stores.append(pltpu.make_async_copy(total, sum_outs[0], before_sem))
            stores[-1].start()
    if with_grad:
        load_weight.wait()
        for n in range(count):
            here = slice(n * rows, (n + 1) * rows)
            out[here, :] = dot(grads[here, :], weight[...], BY_ROWS).astype(BF)
            stores.append(pltpu.make_async_copy(out.at[here], out_hbm.at[at[n]], out_sems.at[n]))
            stores[-1].start()
    for store in stores:
        store.wait()


def goal_backward(own_tile, core_bit, grads, goals, weight, tiles, with_grad, with_sum, before=None, split=False):
    rows, width, units = goals.shape[0] // TILES, goals.shape[1], weight.shape[1]
    scalars = jnp.concatenate([jnp.array(tiles, I32) ^ own_tile, core_bit[None]])
    count = len(tiles)
    operands = [*grads, goals, weight]
    out_specs, shapes, aliases = [], [], {}
    if with_grad:
        out_specs.append(ANYWHERE)
        shapes.append(like(*goals.shape, BF))
    if before is not None:
        operands.append(before)
        if not with_sum:
            aliases = {len(operands): 0}
    if with_sum and split:
        shapes += [like(units // 2, width, F32), like(units // 2, width, BF)]
        out_specs += [whole(shape.shape) for shape in shapes[-2:]]
    elif with_sum:
        shapes.append(like(units, width, F32))
        out_specs.append(ANYWHERE)
    dma = pltpu.SemaphoreType.DMA
    return call(
        functools.partial(goal_backward_kernel, count, with_grad, with_sum, before is not None, split),
        "goal_backward",
        (1,),
        scalars,
        [ANYWHERE] * len(operands),
        out_specs,
        shapes,
        operands,
        [
            pltpu.VMEM((count * rows, units), BF),
            pltpu.VMEM((count * rows, width), BF),
            pltpu.VMEM(weight.shape, BF),
            pltpu.VMEM((count * rows, width), BF),
            pltpu.VMEM((units, width), F32),
            dma((count,)),
            dma((count,)),
            dma,
            dma,
            dma((count,)),
        ],
        aliases,
        BRIEF if with_sum else LONG,
    )


def fold_kernel(_, kept_mine_ref, got_mine_ref, kept_other_ref, got_other_ref, kept_ref, sent_ref):
    kept_ref[...] = kept_mine_ref[...] + got_mine_ref[...].astype(F32)
    sent_ref[...] = (kept_other_ref[...] + got_other_ref[...].astype(F32)).astype(BF)


def fold(kept, got, bit_value):
    rows, width = kept.shape[0] // 2, kept.shape[1]
    block = min(rows, 64)
    steps = rows // block
    mine = pl.BlockSpec((block, width), lambda i, bit: (bit[0] * steps + i, 0))
    other = pl.BlockSpec((block, width), lambda i, bit: ((1 - bit[0]) * steps + i, 0))
    straight = pl.BlockSpec((block, width), lambda i, bit: (i, 0))
    return call(
        fold_kernel,
        "fold",
        (steps,),
        bit_value[None],
        [mine, mine, other, other],
        [straight, straight],
        [like(rows, width, F32), like(rows, width, BF)],
        [kept, got, kept, got],
    )


def spread_kernel(count, own_ref, kept_ref, got_ref, *out_refs):
    own = own_ref[0]
    size = kept_ref.shape[0] // count
    for offset in range(count):
        here = pl.ds(pl.multiple_of((own ^ offset) * size, size), size)
        total = kept_ref[here, :] + got_ref[here, :].astype(F32)
        out_refs[offset][...] = total.astype(out_refs[offset].dtype)


def round_kernel(_, kept_ref, got_ref, out_ref):
    out_ref[...] = (kept_ref[...] + got_ref[...].astype(F32)).astype(BF)


def finish_kernel(loss_factor, _, states_ref, *refs):
    goal_refs, refs = refs[:-6], refs[-6:]
    first_ref, hidden_ref, gain_ref, shift_ref, out_ref, loss_ref = refs
    layers, share, units = hidden_ref.shape
    total = sum(states_ref[n * share : (n + 1) * share, :].astype(F32) for n in range(states_ref.shape[0] // share))
    goal_total = sum(ref[...].astype(F32) for ref in goal_refs)
    feat_width = first_ref.shape[1] - goal_total.shape[1]
    first_ref[:, 0:feat_width] = total[:, 0:feat_width]
    first_ref[:, feat_width:] = goal_total
    for layer in range(layers):
        start = feat_width + layer * units
        hidden_ref[layer] = total[:, start : start + units]
    rest = total[:, feat_width + layers * units :].T
    parts = 2 * layers + 4
    rest = rest[:parts] + rest[parts : 2 * parts]
    gain_ref[...] = rest[: layers + 1]
    shift_ref[...] = rest[layers + 1 : 2 * layers + 2]
    out_ref[...] = rest[2 * layers + 2 : 2 * layers + 3]
    loss_ref[...] = rest[2 * layers + 3 :, 0:1] * loss_factor


def swap_bit(block, bit, dp_count, mp_count):
    if bit < 2:
        return lax.ppermute(block, "mp", xor_pairs(mp_count, 1 << bit))
    return lax.ppermute(block, "dp", xor_pairs(dp_count, 1 << (bit - 2)))


def sum_plain(partial, dp_count):
    return lax.psum_scatter(partial, ("dp", "mp"), scatter_dimension=0, tiled=True)


def across(block, tile, dp_count):
    per = dp_count // TILES
    moved = block if tile == 0 else lax.ppermute(block, "dp", xor_pairs(dp_count, tile * per))
    if per == 1:
        return moved
    groups = [[group * per + low for low in range(per)] for group in range(TILES)]
    parts = moved.reshape((per, block.shape[0] // per) + block.shape[1:])
    parts = lax.all_to_all(parts, "dp", 0, 0, axis_index_groups=groups, tiled=True)
    return parts.reshape(block.shape)


def shards(
    states, dest_device, goals, returns, weight_in, weight_hidden, norm_gain, norm_shift, weight_out
):
    dp_count, mp_count = lax.axis_size("dp"), lax.axis_size("mp")
    own_dp, own_mp = lax.axis_index("dp"), lax.axis_index("mp")
    number = own_dp * mp_count + own_mp
    core_bit = number & 1
    tokens, feat_width = states.shape
    all_rows = tokens * dp_count * mp_count
    slot_count, goal_width = goals.shape
    capacity = slot_count // dp_count
    shard_in, units = weight_in.shape
    layers = norm_gain.shape[0]
    shard_units = norm_gain.shape[1]
    per = dp_count // TILES
    rows = slot_count // TILES
    own_tile = own_dp // per
    single = per == 1
    swap, cross = xor_pairs(4, 1), xor_pairs(4, 2)

    small = jnp.concatenate([norm_gain, norm_shift, weight_out[None, :]], axis=0)
    small = jnp.pad(small.reshape(-1), (0, 16 * units - small.size)).reshape(16, units)
    others = jnp.concatenate([weight_hidden.reshape((layers - 1) * shard_units, units), small], axis=0)
    other_rows = others.shape[0]
    if single:
        key_row, message = route(
            own_dp, dest_device.reshape(1, tokens), returns.reshape(dp_count, capacity), units
        )
    else:
        dest = dest_device[:, 0]
        offset = ((dest // per) ^ own_tile) * per + dest % per
        blocks = tokens // 128
        marks = (offset[None, :] == jnp.arange(dp_count, dtype=I32)[:, None]).astype(F32)
        marks = marks.reshape(dp_count, blocks, 128)
        upper = jnp.arange(128)[:, None] < jnp.arange(128)[None, :]
        within = dot(marks.astype(BF), upper.astype(BF), ((2,), (0,)))
        block_sums = jnp.sum(marks, axis=2)
        earlier = jnp.arange(blocks)[None, :] < jnp.arange(blocks)[:, None]
        ahead = jnp.sum(jnp.where(earlier[None], block_sums[:, None, :], 0.0), axis=2)
        rank = jnp.sum(marks * (within + ahead[:, :, None]), axis=0).reshape(tokens)
        key = offset * capacity + rank.astype(I32)
        key_row = key[None, :]
        valid = jnp.arange(capacity, dtype=F32)[None, :] < jnp.sum(block_sums, axis=1)[:, None]
        tile_returns = returns.reshape(TILES, rows)
        got_returns = [
            across(lax.dynamic_index_in_dim(tile_returns, own_tile ^ t, 0, keepdims=False), t, dp_count)
            for t in range(TILES)
        ]
        got_returns = jnp.stack(got_returns).reshape(dp_count, capacity).astype(F32)
        square_total = lax.psum(jnp.sum(jnp.where(valid, got_returns * got_returns, 0.0)), ("dp", "mp"))
        scale_value = jnp.sqrt(square_total / all_rows + 1e-06)
        targets = jnp.stack(
            [got_returns / scale_value, valid.astype(F32), jnp.full(valid.shape, 1.0 / all_rows, F32)]
            + [jnp.zeros(valid.shape, F32)] * 5
        )
        targets = targets.reshape(8, TILES // 2, 2 * rows).transpose(1, 0, 2)

    cut = feat_width % shard_in
    first_goal_shard = feat_width // shard_in
    one = lax.ppermute(weight_in, "mp", swap)
    two = lax.ppermute(weight_in, "mp", cross)
    if single:
        messages = message
        for bit in (4, 2, 1):
            messages = jnp.concatenate([messages, lax.ppermute(messages, "dp", xor_pairs(dp_count, bit))], axis=0)
        two = after(two, messages)
    pieces = (weight_in, one, two, lax.ppermute(two, "mp", swap))

    *parts, goal_weight = goal_forward(own_tile, own_mp, goals, pieces, cut, first_goal_shard)
    if single:
        others = jnp.concatenate([others, after(messages, goal_weight)], axis=0)
    others_two = lax.ppermute(others, "mp", cross)

    state_part, state_weight = state_forward(after(own_mp, goal_weight), states, pieces, cut, first_goal_shard)
    others_one = lax.ppermute(after(others, state_part), "mp", swap)
    others_three = lax.ppermute(after(others_two, state_part), "mp", swap)
    parts = [across(after(part, state_part) if tile > 4 else part, tile, dp_count) for tile, part in enumerate(parts)]
    prepared = prepare(
        after(own_mp, *[parts[tile] for tile in (1, 2, 3, 4)]), [others, others_one, others_two, others_three],
        layers, other_rows, rows, float(all_rows),
    )
    hidden, vectors, out_weight = prepared[:3]
    if single:
        targets = prepared[3]

    running, back, made_of = None, {}, {}
    for tiles in (NEAR, FAR_ONE, FAR_TWO):
        made = critic(
            own_dp, key_row, targets, state_part, hidden, vectors, out_weight,
            [parts[t] for t in tiles], tiles, running, tiles == FAR_TWO,
        )
        running = (made[-2], made[-1], made[len(tiles)])
        made_of.update(zip(tiles, made))
        if tiles == FAR_ONE:
            for tile in NEAR + FAR_ONE:
                back[tile] = across(after(made_of[tile], made_of[FAR_ONE[0]], *[parts[u] for u in FAR_TWO]), tile, dp_count)
    for tile in FAR_TWO:
        back[tile] = across(after(made_of[tile], *[back[u] for u in NEAR + FAR_ONE]), tile, dp_count)
    first, rest = made[-2], made[-1]

    state_made = state_weight_grad(core_bit, key_row, first, states, rest, single)

    early = NEAR + FAR_ONE
    if single:
        kept, sent = state_made[1:]
        sent = after(sent, *[back[t] for t in early])
        states_kept, sent = fold(kept, swap_bit(sent, CORE, dp_count, mp_count), (number >> Y) & 1)
        states_got = swap_bit(sent, Y, dp_count, mp_count)
        back[0] = after(back[0], states_kept)
    grad_goals, running_sum = goal_backward(
        own_tile, core_bit, [back[t] for t in early], goals, goal_weight, early, True, True
    )
    if single:
        grad_states = state_grad(own_dp, after(state_made[0], running_sum), state_weight)
        states_got = after(states_got, grad_states)
        block = call(
            round_kernel, "round", (1,), own_dp[None], [whole(states_kept.shape)] * 2, [whole(states_kept.shape)],
            [like(*states_kept.shape, BF)], [states_kept, states_got],
        )[0]
        running_sum = after(running_sum, block)
    goal_made = goal_backward(
        own_tile, core_bit, [back[t] for t in FAR_TWO], goals, goal_weight, FAR_TWO, False, True,
        running_sum, single,
    )

    share = units // (dp_count * mp_count)
    if single:
        goals_kept, goals_sent = goal_made
        goals_got = swap_bit(goals_sent, CORE, dp_count, mp_count)
        goals_kept, goals_sent = fold(goals_kept, goals_got, (number >> Y) & 1)
        goals_got = swap_bit(goals_sent, Y, dp_count, mp_count)
        grad_goals = goal_backward(
            own_tile, core_bit, [after(back[t], goals_kept) for t in FAR_TWO], goals, goal_weight, FAR_TWO, True, False,
            grad_goals,
        )[0]
        block = lax.all_to_all(block.reshape(dp_count, share, -1), "dp", 0, 0, tiled=True)
        arrived = [block.reshape(dp_count * share, -1)]
        blocks = call(
            functools.partial(spread_kernel, dp_count), "spread", (1,), own_dp[None],
            [whole(goals_kept.shape)] * 2,
            [whole((share, goal_width))] * dp_count,
            [like(share, goal_width, F32)] + [like(share, goal_width, BF)] * (dp_count - 1),
            [after(goals_kept, grad_goals), goals_got],
        )
        arrived += [blocks[0]] + [
            lax.ppermute(blocks[o], "dp", xor_pairs(dp_count, o)) for o in range(1, dp_count)
        ]
        shapes = [
            like(share, feat_width + goal_width, F32), like(layers - 1, share, units, F32),
            like(layers, share, F32), like(layers, share, F32), like(1, share, F32), like(1, 1, F32),
        ]
        first_share, hidden_share, gain_grad, shift_grad, out_grad, loss = call(
            functools.partial(finish_kernel, 0.5 / all_rows),
            "finish", (1,), core_bit[None],
            [whole(block.shape) for block in arrived],
            [whole(shape.shape) for shape in shapes],
            shapes,
            arrived,
        )
    else:
        grad_goals = goal_backward(
            own_tile, core_bit, [after(back[t], goal_made[0]) for t in FAR_TWO], goals, goal_weight, FAR_TWO, True, False,
            grad_goals,
        )[0]
        grad_states = state_grad(own_dp, state_made[0], state_weight)
        total = sum_plain(state_made[1], dp_count)
        hidden_share = total[:, feat_width : feat_width + (layers - 1) * units]
        hidden_share = hidden_share.reshape(share, layers - 1, units).transpose(1, 0, 2)
        rest = total[:, feat_width + (layers - 1) * units :]
        first_share = jnp.concatenate([total[:, :feat_width], sum_plain(goal_made[0], dp_count)], axis=1)

        count = 2 * layers + 2
        rest = (rest[:, :count] + rest[:, count : 2 * count]).T
        gain_grad, shift_grad, out_grad = rest[:layers], rest[layers : 2 * layers], rest[2 * layers]
        loss = 0.5 * rest[count - 1, 0] / all_rows
    return (
        loss.reshape(()),
        grad_states,
        grad_goals,
        first_share.T,
        hidden_share.transpose(0, 2, 1),
        gain_grad,
        shift_grad,
        out_grad.reshape(share),
    )


def solution(mesh):
    placed = (
        P(("dp", "mp"), None),
        P(("dp", "mp"), None),
        P(("dp", "mp"), None),
        P(("dp", "mp")),
        P("mp", None),
        P(None, "mp", None),
        P(None, "mp"),
        P(None, "mp"),
        P("mp"),
    )
    return jax.shard_map(
        shards,
        mesh=mesh,
        in_specs=placed,
        out_specs=(
            P(),
            P(("dp", "mp"), None),
            P(("dp", "mp"), None),
            P(None, ("dp", "mp")),
            P(None, None, ("dp", "mp")),
            P(None, ("dp", "mp")),
            P(None, ("dp", "mp")),
            P(("dp", "mp")),
        ),
        check_vma=False,
    )
```

```python
import functools

import jax
import jax.numpy as jnp
from jax import lax
from jax.experimental import pallas as pl
from jax.experimental.pallas import tpu as pltpu
from jax.sharding import PartitionSpec as P

BF = jnp.bfloat16
F32 = jnp.float32
I32 = jnp.int32
TILES = 8
STEP = 64
VMEM = 63 * 1024 * 1024 + 512 * 1024
NEAR, FAR_ONE, FAR_TWO = (0, 1, 2, 3), (4, 5), (6, 7)
BRIEF = pl.CostEstimate(flops=1, bytes_accessed=1, transcendentals=0)
LONG = pl.CostEstimate(flops=9_000_000_000, bytes_accessed=10_000_000, transcendentals=0)
CORE, Y, X, Z_LOW, Z_HIGH = range(5)
FIRST_ORDER = (CORE, Y, Z_HIGH, Z_LOW, X)


def dot(first, second, dims):
    return lax.dot_general(first, second, (dims, ((), ())), preferred_element_type=F32)


ROWS_BY_COLUMNS, BY_ROWS, OVER_ROWS = ((1,), (0,)), ((1,), (1,)), ((0,), (0,))


def after(value, *others):
    return lax.optimization_barrier((value, *others))[0]


def xor_pairs(count, bits):
    return [(i, i ^ bits) for i in range(count)]


def like(*shape_and_type):
    *shape, dtype = shape_and_type
    return jax.ShapeDtypeStruct(tuple(shape), dtype)


def whole(shape):
    return pl.BlockSpec(tuple(shape), lambda *_: (0,) * len(shape))


ANYWHERE = pl.BlockSpec(memory_space=pl.ANY)


def call(kernel, name, grid, scalars, in_specs, out_specs, out_shape, operands, scratch=(), aliases=None, cost=BRIEF):
    return pl.pallas_call(
        kernel,
        out_shape=out_shape,
        grid_spec=pltpu.PrefetchScalarGridSpec(
            num_scalar_prefetch=1,
            grid=grid,
            in_specs=in_specs,
            out_specs=out_specs,
            scratch_shapes=list(scratch),
        ),
        input_output_aliases=aliases or {},
        compiler_params=pltpu.CompilerParams(vmem_limit_bytes=VMEM),
        cost_estimate=cost,
        name=name,
    )(scalars, *operands)


def route_kernel(capacity, own_ref, dest_ref, returns_ref, row_ref, message_ref, wide, text):
    own = own_ref[0]
    tokens = dest_ref.shape[1]
    count = returns_ref.shape[0]
    blocks = tokens // 128
    offsets = dest_ref[...] ^ own
    marks = (lax.broadcasted_iota(I32, (count, tokens), 0) == offsets).astype(F32)
    stacked = jnp.concatenate([marks[:, 128 * b : 128 * b + 128] for b in range(blocks)], axis=0)
    upper = lax.broadcasted_iota(I32, (128, 128), 0) < lax.broadcasted_iota(I32, (128, 128), 1)
    within = dot(stacked.astype(BF), upper.astype(F32).astype(BF), ROWS_BY_COLUMNS)
    totals = jnp.sum(stacked, axis=1, keepdims=True)
    ahead = jnp.zeros((count, 1), F32)
    for b in range(blocks):
        part = slice(count * b, count * b + count)
        lanes = slice(128 * b, 128 * b + 128)
        rank = jnp.sum(stacked[part] * (within[part] + ahead), axis=0, keepdims=True)
        key = offsets[:, lanes].astype(F32) * capacity + rank
        row_ref[:, lanes] = key.astype(I32)
        ahead = ahead + totals[part]
    wide[...] = returns_ref[...].astype(F32)
    lane = lax.broadcasted_iota(I32, text.shape, 1) - (text.shape[1] - 128)
    high = jnp.floor(ahead * 0.0625)
    text[...] = jnp.where(lane == 0, high, jnp.where(lane == 1, ahead - 16.0 * high, 0.0))
    for offset in range(count):
        text[offset : offset + 1, 0:capacity] = wide[pl.ds(own ^ offset, 1), :]
    message_ref[...] = text[...].astype(BF)


def route(own, dest_row, returns, units):
    tokens, (count, capacity) = dest_row.shape[1], returns.shape
    return call(
        functools.partial(route_kernel, capacity),
        "route",
        (1,),
        own[None],
        [whole(dest_row.shape), whole(returns.shape)],
        [whole((1, tokens)), whole((count, units))],
        [like(1, tokens, I32), like(count, units, BF)],
        [dest_row, returns],
        [pltpu.VMEM(returns.shape, F32), pltpu.VMEM((count, units), F32)],
    )


def reverse(bits):
    return (bits % 2) * 4 + (bits // 2 % 2) * 2 + bits // 4


def prepare_kernel(layers, rows, capacity, total_rows, own_ref, *refs):
    pieces, refs = refs[:4], refs[4:]
    hidden_ref, vectors_ref, out_weight_ref = refs[:3]
    own = own_ref[0]
    width = hidden_ref.shape[2] // 4
    for shard in range(4):
        columns = slice(shard * width, (shard + 1) * width)
        for value in range(4):

            @pl.when(own == value)
            def _():
                piece = pieces[shard ^ value]
                for layer in range(layers - 1):
                    hidden_ref[layer, columns, :] = piece[layer * width : (layer + 1) * width, :]
                start = (layers - 1) * width
                small = piece[start : start + 16, :].astype(F32)
                for row in range(2 * layers + 1):
                    vectors_ref[row : row + 1, columns] = small[
                        row // 4 : row // 4 + 1, (row % 4) * width : (row % 4 + 1) * width
                    ]

    vectors_ref[2 * layers + 1 :, :] = jnp.zeros((16 - 2 * layers - 1, vectors_ref.shape[1]), F32)
    out_weight_ref[...] = jnp.concatenate(
        [vectors_ref[2 * layers : 2 * layers + 1, :], jnp.zeros((7, vectors_ref.shape[1]), F32)], axis=0
    ).astype(BF)
    if len(refs) == 3:
        return
    targets_ref = refs[3]
    targets_ref[...] = jnp.zeros_like(targets_ref)
    index = lax.broadcasted_iota(I32, (64, 64), 0)
    partner = (reverse(reverse(index // 8) ^ (index % 8))) * 8 + index % 8
    swap = (lax.broadcasted_iota(I32, (64, 64), 1) == partner).astype(F32).astype(BF)
    lane = lax.broadcasted_iota(I32, (64, 128 * 3), 1).astype(F32)
    total = jnp.zeros((1, 1), F32)
    for piece in pieces:
        message = piece[rows : rows + 64, :]
        counts = dot(swap, message[:, 384:512], ROWS_BY_COLUMNS)
        counts = counts[:, 0:1] * 16.0 + counts[:, 1:2]
        values = message[:, 0:384].astype(F32)
        squares = jnp.sum(jnp.where(lane < counts, values * values, 0.0), axis=1, keepdims=True)
        total = total + jnp.sum(squares, axis=0, keepdims=True)
    scale = jnp.sqrt(total / total_rows + 1e-06)
    message = pieces[0][rows : rows + 64, :].astype(F32)
    counts = message[0:8, 384:385] * 16.0 + message[0:8, 385:386]
    for tile in range(TILES):
        lanes = slice((tile % 2) * capacity, (tile % 2) * capacity + capacity)
        row = reverse(tile) * 8 + tile
        target = message[row : row + 1, 0:384] / scale
        filled = (lane[0:1] < counts[tile : tile + 1]).astype(F32)
        targets_ref[tile // 2, 0:1, lanes] = target[:, 0:capacity]
        targets_ref[tile // 2, 1:2, lanes] = filled[:, 0:capacity]
        targets_ref[tile // 2, 2:3, lanes] = jnp.full((1, capacity), 1.0 / total_rows, F32)


def prepare(own, pieces, layers, rows, capacity, total_rows):
    units = pieces[0].shape[1]
    shapes = [like(layers - 1, units, units, BF), like(16, units, F32), like(8, units, BF)]
    if pieces[0].shape[0] > rows:
        shapes.append(like(TILES // 2, 8, 2 * capacity, F32))
    return call(
        functools.partial(prepare_kernel, layers, rows, capacity, total_rows),
        "prepare",
        (1,),
        own[None],
        [whole(piece.shape) for piece in pieces],
        [whole(shape.shape) for shape in shapes],
        shapes,
        pieces,
    )


def fetch(own, parts, target_ref, sems, later=()):
    place = 0
    for number, (shard, candidates) in enumerate(parts):
        size = candidates[0].shape[0]
        there = target_ref.at[place : place + size]
        for value in range(4):

            @pl.when(own == value)
            def _():
                pltpu.make_async_copy(candidates[shard ^ value], there, sems.at[number]).start()

        place += size
    for copy in later:
        copy.start()
    place = 0
    for number, (shard, candidates) in enumerate(parts):
        size = candidates[0].shape[0]
        there = target_ref.at[place : place + size]
        pltpu.make_async_copy(candidates[0], there, sems.at[number]).wait()
        place += size


def first_weight_parts(pieces, cut, shards, first, last):
    parts = []
    for shard in shards:
        here = slice(cut if shard == first else 0, cut if shard == last else pieces[0].shape[0])
        parts.append((shard, [piece.at[here] for piece in pieces]))
    return parts


def goal_forward_kernel(cut, first_shard, scalars_ref, goals_hbm, *refs):
    pieces, refs = refs[:4], refs[4:]
    out_refs, weight_out, refs = refs[:TILES], refs[TILES], refs[TILES + 1 :]
    goals, weight, made, sems, out_sems, fetch_sems, weight_sem = refs
    rows = goals_hbm.shape[0] // TILES
    order = [*NEAR[1:], *FAR_ONE, *FAR_TWO, 0]
    copies = []
    for place, tile in enumerate(order):
        there = goals_hbm.at[pl.ds(pl.multiple_of((scalars_ref[0] ^ tile) * rows, rows), rows)]
        here = goals.at[place * rows : (place + 1) * rows]
        copies.append(pltpu.make_async_copy(there, here, sems.at[place]))
    for copy in copies[:2]:
        copy.start()
    parts = first_weight_parts(pieces, cut, range(first_shard, 4), first_shard, None)
    fetch(scalars_ref[1], parts, weight, fetch_sems, copies[2:])
    sent = [pltpu.make_async_copy(weight, weight_out, weight_sem)]
    sent[0].start()
    for pair in range(TILES // 2):
        for copy in copies[2 * pair : 2 * pair + 2]:
            copy.wait()
        both = slice(2 * pair * rows, (2 * pair + 2) * rows)
        made[both, :] = dot(goals[both, :], weight[...], ROWS_BY_COLUMNS).astype(BF)
        for place in (2 * pair, 2 * pair + 1):
            here = made.at[place * rows : (place + 1) * rows]
            sent.append(pltpu.make_async_copy(here, out_refs[order[place]], out_sems.at[place]))
            sent[-1].start()
    for copy in sent:
        copy.wait()


def goal_forward(own_tile, own_mp, goals, pieces, cut, first_shard):
    width = goals.shape[1]
    rows, units = goals.shape[0] // TILES, pieces[0].shape[1]
    dma = pltpu.SemaphoreType.DMA
    return call(
        functools.partial(goal_forward_kernel, cut, first_shard),
        "goal_forward",
        (1,),
        jnp.stack([own_tile, own_mp]),
        [ANYWHERE] * 5,
        [ANYWHERE] * (TILES + 1),
        [like(rows, units, BF)] * TILES + [like(width, units, BF)],
        [goals, *pieces],
        [
            pltpu.VMEM(goals.shape, BF),
            pltpu.VMEM((width, units), BF),
            pltpu.VMEM((TILES * rows, units), BF),
            dma((TILES,)),
            dma((TILES,)),
            dma((4,)),
            dma,
        ],
    )


def state_forward_kernel(steps, cut, last_shard, own_ref, states_hbm, *refs):
    pieces, (out_hbm, weight_out), refs = refs[:4], refs[4:6], refs[6:]
    states, weight, made, sems, out_sems, fetch_sems, weight_sem = refs
    rows = states.shape[0] // steps
    copies = []
    for step in range(steps):
        here = slice(step * rows, (step + 1) * rows)
        copies.append(pltpu.make_async_copy(states_hbm.at[here], states.at[here], sems.at[step]))
    copies[0].start()
    parts = first_weight_parts(pieces, cut, range(last_shard + 1), None, last_shard)
    fetch(own_ref[0], parts, weight, fetch_sems, copies[1:])
    sent = [pltpu.make_async_copy(weight, weight_out, weight_sem)]
    sent[0].start()
    for step in range(steps):
        copies[step].wait()
        here = slice(step * rows, (step + 1) * rows)
        made[here, :] = dot(states[here, :], weight[...], ROWS_BY_COLUMNS).astype(BF)
        sent.append(pltpu.make_async_copy(made.at[here], out_hbm.at[here], out_sems.at[step]))
        sent[-1].start()
    for copy in sent:
        copy.wait()


def state_forward(own, states, pieces, cut, last_shard):
    tokens, width = states.shape
    units = pieces[0].shape[1]
    steps = 4
    dma = pltpu.SemaphoreType.DMA
    return call(
        functools.partial(state_forward_kernel, steps, cut, last_shard),
        "state_forward",
        (1,),
        own[None],
        [ANYWHERE] * 5,
        [ANYWHERE] * 2,
        [like(tokens, units, BF), like(width, units, BF)],
        [states, *pieces],
        [
            pltpu.VMEM(states.shape, BF),
            pltpu.VMEM((width, units), BF),
            pltpu.VMEM((tokens, units), BF),
            dma((steps,)),
            dma((steps,)),
            dma((4,)),
            dma,
        ],
    )


def split_rows(total_ref, kept_ref, sent_ref, bit_value, order):
    parts = 1 << len(order)
    size = total_ref.shape[0] // parts
    for place in range(parts // 2):
        number = 0
        for depth, bit in enumerate(order[1:]):
            number += ((place >> (len(order) - 2 - depth)) & 1) << bit
        here = slice(place * size, (place + 1) * size)
        mine = pl.multiple_of((number + (bit_value << order[0])) * size, size)
        other = pl.multiple_of((number + ((1 - bit_value) << order[0])) * size, size)
        kept_ref[here, :] = total_ref[pl.ds(mine, size), :]
        sent_ref[here, :] = total_ref[pl.ds(other, size), :].astype(BF)


def critic_kernel(pairs, first_pair, layers, first_call, last_call, _, *refs):
    key_ref, target_ref, states_ref, hidden_ref, vectors_ref, out_weight_ref = refs[:6]
    refs = refs[6:]
    goal_refs, refs = refs[: 2 * pairs], refs[2 * pairs :]
    if not first_call:
        shares_before_hbm, sums_before_ref = refs[:2]
        refs = refs[3:]
    first_refs, refs = refs[: 2 * pairs], refs[2 * pairs :]
    all_first_ref, refs = refs[0], refs[1:]
    if last_call:
        total_ref, refs = refs[0], refs[1:]
    else:
        shares_ref, sums_ref = refs[:2]
        refs = refs[2:]
    work, nhat, slope, spread, acts, low_grad = refs[:6]
    if last_call:
        sums_ref = refs[6]
        share_at = lambda layer: total_ref.at[:, layer * work.shape[1] : (layer + 1) * work.shape[1]]
    else:
        share_at = lambda layer: shares_ref.at[layer]
    step = pl.program_id(0)
    rows, units = work.shape
    if not first_call:
        loads = [
            pltpu.make_async_copy(shares_before_hbm.at[layer], share_at(layer), refs[-1].at[layer])
            for layer in range(layers - 1)
        ]
        for load in loads:
            load.start()
    half = rows // 2
    tokens = key_ref.shape[1]
    steps = rows // STEP

    @pl.when(step == 0)
    def _():
        if first_call:
            for layer in range(layers - 1):
                share_at(layer)[...] = jnp.zeros((units, units), F32)
        sums_ref[...] = jnp.zeros_like(sums_ref) if first_call else sums_before_ref[...]

    for pair in range(pairs):

        @pl.when(step == pair)
        def _():
            low_grad[0:half, :] = goal_refs[2 * pair][...]
            low_grad[half:rows, :] = goal_refs[2 * pair + 1][...]

    base = (first_pair + step) * rows
    slot = base + lax.broadcasted_iota(I32, (rows, tokens), 0)
    pick = (slot == key_ref[...]).astype(F32).astype(BF)
    work[...] = dot(pick, states_ref[...], ROWS_BY_COLUMNS) + low_grad[...].astype(F32)

    for layer in range(layers):
        gain = vectors_ref[layer : layer + 1, :]
        shift = vectors_ref[layers + layer : layers + layer + 1, :]
        for i in range(steps):
            here = slice(i * STEP, (i + 1) * STEP)
            values = work[here, :]
            center = values - jnp.mean(values, axis=1, keepdims=True)
            inverse = lax.rsqrt(jnp.mean(center * center, axis=1, keepdims=True) + 1e-05)
            scaled = center * inverse
            shifted = scaled * gain + shift
            slopes = jnp.exp(jnp.minimum(shifted, 0.0))
            nhat[layer, here, :] = scaled
            slope[layer, here, :] = slopes
            spread[layer, here, :] = inverse
            acts[layer, here, :] = (jnp.maximum(shifted, 0.0) + (slopes - 1.0)).astype(BF)
        if layer < layers - 1:
            work[...] = dot(acts[layer], hidden_ref[layer], ROWS_BY_COLUMNS)

    out_weight = out_weight_ref[...]
    last = acts[layers - 1]
    value = dot(out_weight, last, BY_ROWS)
    target = target_ref[0]
    error = (value[0:1, :] - target[0:1, :]) * target[1:2, :]
    grad_value = (error * target[2:3, :]).astype(BF)
    grad_rows = jnp.concatenate([grad_value.astype(F32), jnp.zeros((7, rows), F32)], axis=0).astype(BF)
    sums_ref[2 * layers] += dot(grad_rows, last, ROWS_BY_COLUMNS)
    sums_ref[2 * layers + 1] += jnp.broadcast_to(jnp.sum(error * error, axis=1, keepdims=True), (8, units))
    work[...] = dot(grad_rows, out_weight, OVER_ROWS)

    if not first_call:
        for load in loads:
            load.wait()
    for layer in reversed(range(layers)):
        gain = vectors_ref[layer : layer + 1, :]
        for i in range(steps):
            here = slice(i * STEP, (i + 1) * STEP)
            scaled = nhat[layer, here, :]
            grad_norm = work[here, :] * slope[layer, here, :]
            by_scaled = grad_norm * scaled
            sums_ref[layer] += jnp.sum(by_scaled.reshape(STEP // 8, 8, units), axis=0)
            sums_ref[layers + layer] += jnp.sum(grad_norm.reshape(STEP // 8, 8, units), axis=0)
            grad_scaled = grad_norm * gain
            first_mean = jnp.mean(grad_scaled, axis=1, keepdims=True)
            second_mean = jnp.mean(by_scaled * gain, axis=1, keepdims=True)
            grad = spread[layer, here, :] * (grad_scaled - first_mean - scaled * second_mean)
            low_grad[here, :] = grad.astype(BF)
        if layer > 0:
            grads = low_grad[...]
            work[...] = dot(grads, hidden_ref[layer - 1], BY_ROWS)
            share_at(layer - 1)[...] += dot(grads, acts[layer - 1], OVER_ROWS)

    all_first_ref[...] = low_grad[...]
    for pair in range(pairs):

        @pl.when(step == pair)
        def _():
            first_refs[2 * pair][...] = low_grad[0:half, :]
            first_refs[2 * pair + 1][...] = low_grad[half:rows, :]

    if last_call:

        @pl.when(step == pairs - 1)
        def _():
            count = 2 * layers + 2
            sums = jnp.concatenate(
                [jnp.sum(sums_ref[row], axis=0, keepdims=True) for row in range(count - 1)]
                + [sums_ref[count - 1][0:1, :]],
                axis=0,
            )
            high = sums.astype(BF).astype(F32)
            columns = jnp.concatenate([high, sums - high, jnp.zeros((128 - 2 * count, units), F32)], axis=0)
            total_ref[:, (layers - 1) * units :] = columns.T


def critic(own, key_row, targets, state_part, hidden, vectors, out_weight, goal_parts, tiles, before, last_call):
    pairs, first_pair = len(tiles) // 2, tiles[0] // 2
    half, units = goal_parts[0].shape
    rows = 2 * half
    layers = hidden.shape[0] + 1
    width = (layers - 1) * units + 128
    sums_shape, shares_shape = (2 * layers + 2, 8, units), (layers - 1, units, units)
    operands = [key_row, targets, state_part, hidden, vectors, out_weight, *goal_parts]
    in_specs = [
        whole(key_row.shape),
        pl.BlockSpec((1,) + targets.shape[1:], lambda i, _: (first_pair + i, 0, 0)),
        whole(state_part.shape),
        whole(hidden.shape),
        whole(vectors.shape),
        whole(out_weight.shape),
    ] + [whole((half, units))] * (2 * pairs)
    aliases = {}
    if before is not None:
        in_specs += [ANYWHERE, whole(sums_shape), ANYWHERE]
        assert pairs == 1
        operands += list(before)
        aliases = {len(operands): 2 * pairs}
    out_shape = [like(half, units, BF)] * (2 * pairs) + [like(TILES * half, units, BF)]
    out_specs = [whole((half, units))] * (2 * pairs) + [
        pl.BlockSpec((rows, units), lambda i, _: (first_pair + i, 0))
    ]
    scratch = [
        pltpu.VMEM((rows, units), F32),
        pltpu.VMEM((layers, rows, units), F32),
        pltpu.VMEM((layers, rows, units), F32),
        pltpu.VMEM((layers, rows, 1), F32),
        pltpu.VMEM((layers, rows, units), BF),
        pltpu.VMEM((rows, units), BF),
    ]
    if last_call:
        shapes = [like(units, width, F32)]
        scratch += [pltpu.VMEM(sums_shape, F32)]
    else:
        shapes = [like(*shares_shape, F32), like(*sums_shape, F32)]
    if before is not None:
        scratch.append(pltpu.SemaphoreType.DMA((layers - 1,)))
    return call(
        functools.partial(critic_kernel, pairs, first_pair, layers, before is None, last_call),
        "critic",
        (pairs,),
        own[None],
        in_specs,
        out_specs + [whole(shape.shape) for shape in shapes],
        out_shape + shapes,
        operands,
        scratch,
        aliases,
    )


def state_weight_kernel(steps, split, core_ref, key_ref, first_hbm, states_hbm, rest_hbm, grad_hbm, *refs):
    outs, refs = refs[: 2 if split else 1], refs[2 if split else 1 :]
    first, states, rest, grad, total, first_sem, states_sems, rest_sem, grad_sems, out_sems = refs[:10]
    pieces = refs[10:]
    slots, units = first.shape
    tokens, width = states.shape
    rows, part = tokens // steps, width // steps
    load_first = pltpu.make_async_copy(first_hbm, first, first_sem)
    load_first.start()
    load_rest = pltpu.make_async_copy(rest_hbm, rest, rest_sem)
    load_rest.start()
    loads = [
        pltpu.make_async_copy(
            states_hbm.at[:, step * part : (step + 1) * part], states.at[:, step * part : (step + 1) * part],
            states_sems.at[step],
        )
        for step in range(steps)
    ]
    for load in loads:
        load.start()
    stores = []

    def give(source, start, number):
        there = slice(start, start + source.shape[1])
        if split:
            split_rows(source, pieces[0].at[:, there], pieces[1].at[:, there], core_ref[0], FIRST_ORDER)
            for which in range(2):
                copy = pltpu.make_async_copy(
                    pieces[which].at[:, there], outs[which].at[:, there], out_sems.at[which, number]
                )
                copy.start()
                stores.append(copy)
        else:
            outs[0][:, there] = source[...]

    load_first.wait()
    for step in range(steps):
        here = slice(step * rows, (step + 1) * rows)
        slot = lax.broadcasted_iota(I32, (slots, rows), 0)
        pick = (slot == key_ref[:, here]).astype(F32).astype(BF)
        grad[here, :] = dot(pick, first[...], OVER_ROWS).astype(BF)
    load_rest.wait()
    give(rest, width, steps)
    store_grad = pltpu.make_async_copy(grad, grad_hbm, grad_sems)
    store_grad.start()
    for step in range(steps):
        loads[step].wait()
        here = slice(step * part, (step + 1) * part)
        total[:, here] = dot(grad[...], states[:, here], OVER_ROWS)
        give(total.at[:, here], step * part, step)
    store_grad.wait()
    for store in stores:
        store.wait()


def state_weight_grad(core_bit, key_row, first, states, rest, split):
    tokens, width = states.shape
    slots, units = first.shape
    steps = 4
    columns = width + rest.shape[1]
    shapes = [like(units // 2, columns, F32), like(units // 2, columns, BF)] if split else [like(units, columns, F32)]
    dma = pltpu.SemaphoreType.DMA
    return call(
        functools.partial(state_weight_kernel, steps, split),
        "state_weight_grad",
        (1,),
        core_bit[None],
        [whole(key_row.shape), ANYWHERE, ANYWHERE, ANYWHERE],
        [ANYWHERE] * 3 if split else [ANYWHERE, whole(shapes[0].shape)],
        [like(tokens, units, BF)] + shapes,
        [key_row, first, states, rest],
        [
            pltpu.VMEM(first.shape, BF),
            pltpu.VMEM(states.shape, BF),
            pltpu.VMEM(rest.shape, F32),
            pltpu.VMEM((tokens, units), BF),
            pltpu.VMEM((units, width), F32),
            dma,
            dma((steps,)),
            dma,
            dma,
            dma((2, steps + 1)),
        ]
        + ([pltpu.VMEM(shape.shape, shape.dtype) for shape in shapes] if split else []),
    )


def state_grad_kernel(steps, _, grad_hbm, weight_hbm, out_hbm, grad, weight, out, grad_sem, weight_sem, sems):
    rows = out.shape[1]
    load_weight = pltpu.make_async_copy(weight_hbm, weight, weight_sem)
    load_weight.start()
    load_grad = pltpu.make_async_copy(grad_hbm, grad, grad_sem)
    load_grad.start()
    load_weight.wait()
    load_grad.wait()
    stores = []
    for step in range(steps):
        here = slice(step * rows, (step + 1) * rows)
        out[step] = dot(grad[here, :], weight[...], BY_ROWS).astype(BF)
        stores.append(pltpu.make_async_copy(out.at[step], out_hbm.at[here], sems.at[step]))
        stores[-1].start()
    for store in stores:
        store.wait()


def state_grad(own, grad, weight):
    tokens, units = grad.shape
    width = weight.shape[0]
    steps = 4
    dma = pltpu.SemaphoreType.DMA
    return call(
        functools.partial(state_grad_kernel, steps),
        "state_grad",
        (1,),
        own[None],
        [ANYWHERE] * 2,
        [ANYWHERE],
        [like(tokens, width, BF)],
        [grad, weight],
        [
            pltpu.VMEM(grad.shape, BF),
            pltpu.VMEM(weight.shape, BF),
            pltpu.VMEM((steps, tokens // steps, width), BF),
            dma,
            dma,
            dma((steps,)),
        ],
        cost=BRIEF,
    )[0]


def goal_backward_kernel(count, with_grad, with_sum, has_before, split, scalars_ref, *refs):
    grad_hbm, refs = refs[:count], refs[count:]
    goals_hbm, weight_hbm, refs = refs[0], refs[1], refs[2:]
    if has_before:
        before_hbm, refs = refs[0], refs[1:]
    if with_grad:
        out_hbm, refs = refs[0], refs[1:]
    if with_sum:
        sum_outs, refs = refs[: 2 if split else 1], refs[2 if split else 1 :]
    grads, goals, weight, out, total, grad_sems, goal_sems, weight_sem, before_sem, out_sems = refs
    rows, width = goals_hbm.shape[0] // TILES, goals_hbm.shape[1]
    at = [pl.ds(pl.multiple_of(scalars_ref[n] * rows, rows), rows) for n in range(count)]
    loads = []
    for n in range(count):
        here = slice(n * rows, (n + 1) * rows)
        load = [pltpu.make_async_copy(grad_hbm[n], grads.at[here], grad_sems.at[n])]
        if with_sum:
            load.append(pltpu.make_async_copy(goals_hbm.at[at[n]], goals.at[here], goal_sems.at[n]))
        loads.append(load)
    for load in loads:
        load[0].start()
    if with_sum:
        for load in loads:
            load[1].start()
        if has_before:
            load_before = pltpu.make_async_copy(before_hbm, total, before_sem)
            load_before.start()
    if with_grad:
        load_weight = pltpu.make_async_copy(weight_hbm, weight, weight_sem)
        load_weight.start()
    stores = []
    for load in loads:
        load[0].wait()
    if with_sum:
        for load in loads:
            load[1].wait()
        share = dot(grads[...], goals[...], OVER_ROWS)
        if has_before:
            load_before.wait()
            total[...] += share
        else:
            total[...] = share
        if split:
            split_rows(total, sum_outs[0], sum_outs[1], scalars_ref[count], FIRST_ORDER)
        else:
            stores.append(pltpu.make_async_copy(total, sum_outs[0], before_sem))
            stores[-1].start()
    if with_grad:
        load_weight.wait()
        for n in range(count):
            here = slice(n * rows, (n + 1) * rows)
            out[here, :] = dot(grads[here, :], weight[...], BY_ROWS).astype(BF)
            stores.append(pltpu.make_async_copy(out.at[here], out_hbm.at[at[n]], out_sems.at[n]))
            stores[-1].start()
    for store in stores:
        store.wait()


def goal_backward(own_tile, core_bit, grads, goals, weight, tiles, with_grad, with_sum, before=None, split=False):
    rows, width, units = goals.shape[0] // TILES, goals.shape[1], weight.shape[1]
    scalars = jnp.concatenate([jnp.array(tiles, I32) ^ own_tile, core_bit[None]])
    count = len(tiles)
    operands = [*grads, goals, weight]
    out_specs, shapes, aliases = [], [], {}
    if with_grad:
        out_specs.append(ANYWHERE)
        shapes.append(like(*goals.shape, BF))
    if before is not None:
        operands.append(before)
        if not with_sum:
            aliases = {len(operands): 0}
    if with_sum and split:
        shapes += [like(units // 2, width, F32), like(units // 2, width, BF)]
        out_specs += [whole(shape.shape) for shape in shapes[-2:]]
    elif with_sum:
        shapes.append(like(units, width, F32))
        out_specs.append(ANYWHERE)
    dma = pltpu.SemaphoreType.DMA
    return call(
        functools.partial(goal_backward_kernel, count, with_grad, with_sum, before is not None, split),
        "goal_backward",
        (1,),
        scalars,
        [ANYWHERE] * len(operands),
        out_specs,
        shapes,
        operands,
        [
            pltpu.VMEM((count * rows, units), BF),
            pltpu.VMEM((count * rows, width), BF),
            pltpu.VMEM(weight.shape, BF),
            pltpu.VMEM((count * rows, width), BF),
            pltpu.VMEM((units, width), F32),
            dma((count,)),
            dma((count,)),
            dma,
            dma,
            dma((count,)),
        ],
        aliases,
        BRIEF if split else LONG,
    )


def fold_kernel(_, kept_mine_ref, got_mine_ref, kept_other_ref, got_other_ref, kept_ref, sent_ref):
    kept_ref[...] = kept_mine_ref[...] + got_mine_ref[...].astype(F32)
    sent_ref[...] = (kept_other_ref[...] + got_other_ref[...].astype(F32)).astype(BF)


def fold(kept, got, bit_value):
    rows, width = kept.shape[0] // 2, kept.shape[1]
    block = min(rows, 64)
    steps = rows // block
    mine = pl.BlockSpec((block, width), lambda i, bit: (bit[0] * steps + i, 0))
    other = pl.BlockSpec((block, width), lambda i, bit: ((1 - bit[0]) * steps + i, 0))
    straight = pl.BlockSpec((block, width), lambda i, bit: (i, 0))
    return call(
        fold_kernel,
        "fold",
        (steps,),
        bit_value[None],
        [mine, mine, other, other],
        [straight, straight],
        [like(rows, width, F32), like(rows, width, BF)],
        [kept, got, kept, got],
    )


def spread_kernel(count, own_ref, kept_ref, got_ref, *out_refs):
    own = own_ref[0]
    size = kept_ref.shape[0] // count
    for offset in range(count):
        here = pl.ds(pl.multiple_of((own ^ offset) * size, size), size)
        total = kept_ref[here, :] + got_ref[here, :].astype(F32)
        out_refs[offset][...] = total.astype(out_refs[offset].dtype)


def round_kernel(_, kept_ref, got_ref, out_ref):
    out_ref[...] = (kept_ref[...] + got_ref[...].astype(F32)).astype(BF)


def finish_kernel(loss_factor, _, states_ref, *refs):
    goal_refs, refs = refs[:-6], refs[-6:]
    first_ref, hidden_ref, gain_ref, shift_ref, out_ref, loss_ref = refs
    layers, share, units = hidden_ref.shape
    total = sum(states_ref[n * share : (n + 1) * share, :].astype(F32) for n in range(states_ref.shape[0] // share))
    goal_total = sum(ref[...].astype(F32) for ref in goal_refs)
    feat_width = first_ref.shape[1] - goal_total.shape[1]
    first_ref[:, 0:feat_width] = total[:, 0:feat_width]
    first_ref[:, feat_width:] = goal_total
    for layer in range(layers):
        start = feat_width + layer * units
        hidden_ref[layer] = total[:, start : start + units]
    rest = total[:, feat_width + layers * units :].T
    parts = 2 * layers + 4
    rest = rest[:parts] + rest[parts : 2 * parts]
    gain_ref[...] = rest[: layers + 1]
    shift_ref[...] = rest[layers + 1 : 2 * layers + 2]
    out_ref[...] = rest[2 * layers + 2 : 2 * layers + 3]
    loss_ref[...] = rest[2 * layers + 3 :, 0:1] * loss_factor


def swap_bit(block, bit, dp_count, mp_count):
    if bit < 2:
        return lax.ppermute(block, "mp", xor_pairs(mp_count, 1 << bit))
    return lax.ppermute(block, "dp", xor_pairs(dp_count, 1 << (bit - 2)))


def sum_plain(partial, dp_count):
    return lax.psum_scatter(partial, ("dp", "mp"), scatter_dimension=0, tiled=True)


def across(block, tile, dp_count):
    per = dp_count // TILES
    moved = block if tile == 0 else lax.ppermute(block, "dp", xor_pairs(dp_count, tile * per))
    if per == 1:
        return moved
    groups = [[group * per + low for low in range(per)] for group in range(TILES)]
    parts = moved.reshape((per, block.shape[0] // per) + block.shape[1:])
    parts = lax.all_to_all(parts, "dp", 0, 0, axis_index_groups=groups, tiled=True)
    return parts.reshape(block.shape)


def shards(
    states, dest_device, goals, returns, weight_in, weight_hidden, norm_gain, norm_shift, weight_out
):
    dp_count, mp_count = lax.axis_size("dp"), lax.axis_size("mp")
    own_dp, own_mp = lax.axis_index("dp"), lax.axis_index("mp")
    number = own_dp * mp_count + own_mp
    core_bit = number & 1
    tokens, feat_width = states.shape
    all_rows = tokens * dp_count * mp_count
    slot_count, goal_width = goals.shape
    capacity = slot_count // dp_count
    shard_in, units = weight_in.shape
    layers = norm_gain.shape[0]
    shard_units = norm_gain.shape[1]
    per = dp_count // TILES
    rows = slot_count // TILES
    own_tile = own_dp // per
    single = per == 1
    swap, cross = xor_pairs(4, 1), xor_pairs(4, 2)

    small = jnp.concatenate([norm_gain, norm_shift, weight_out[None, :]], axis=0)
    small = jnp.pad(small.reshape(-1), (0, 16 * units - small.size)).reshape(16, units)
    others = jnp.concatenate([weight_hidden.reshape((layers - 1) * shard_units, units), small], axis=0)
    other_rows = others.shape[0]
    if single:
        key_row, message = route(
            own_dp, dest_device.reshape(1, tokens), returns.reshape(dp_count, capacity), units
        )
    else:
        dest = dest_device[:, 0]
        offset = ((dest // per) ^ own_tile) * per + dest % per
        blocks = tokens // 128
        marks = (offset[None, :] == jnp.arange(dp_count, dtype=I32)[:, None]).astype(F32)
        marks = marks.reshape(dp_count, blocks, 128)
        upper = jnp.arange(128)[:, None] < jnp.arange(128)[None, :]
        within = dot(marks.astype(BF), upper.astype(BF), ((2,), (0,)))
        block_sums = jnp.sum(marks, axis=2)
        earlier = jnp.arange(blocks)[None, :] < jnp.arange(blocks)[:, None]
        ahead = jnp.sum(jnp.where(earlier[None], block_sums[:, None, :], 0.0), axis=2)
        rank = jnp.sum(marks * (within + ahead[:, :, None]), axis=0).reshape(tokens)
        key = offset * capacity + rank.astype(I32)
        key_row = key[None, :]
        valid = jnp.arange(capacity, dtype=F32)[None, :] < jnp.sum(block_sums, axis=1)[:, None]
        tile_returns = returns.reshape(TILES, rows)
        got_returns = [
            across(lax.dynamic_index_in_dim(tile_returns, own_tile ^ t, 0, keepdims=False), t, dp_count)
            for t in range(TILES)
        ]
        got_returns = jnp.stack(got_returns).reshape(dp_count, capacity).astype(F32)
        square_total = lax.psum(jnp.sum(jnp.where(valid, got_returns * got_returns, 0.0)), ("dp", "mp"))
        scale_value = jnp.sqrt(square_total / all_rows + 1e-06)
        targets = jnp.stack(
            [got_returns / scale_value, valid.astype(F32), jnp.full(valid.shape, 1.0 / all_rows, F32)]
            + [jnp.zeros(valid.shape, F32)] * 5
        )
        targets = targets.reshape(8, TILES // 2, 2 * rows).transpose(1, 0, 2)

    cut = feat_width % shard_in
    first_goal_shard = feat_width // shard_in
    one = lax.ppermute(weight_in, "mp", swap)
    two = lax.ppermute(weight_in, "mp", cross)
    if single:
        messages = message
        for bit in (4, 2, 1):
            messages = jnp.concatenate([messages, lax.ppermute(messages, "dp", xor_pairs(dp_count, bit))], axis=0)
        two = after(two, messages)
    pieces = (weight_in, one, two, lax.ppermute(two, "mp", swap))

    *parts, goal_weight = goal_forward(own_tile, own_mp, goals, pieces, cut, first_goal_shard)
    if single:
        others = jnp.concatenate([others, after(messages, goal_weight)], axis=0)
    others_two = lax.ppermute(others, "mp", cross)

    state_part, state_weight = state_forward(after(own_mp, goal_weight), states, pieces, cut, first_goal_shard)
    others_one = lax.ppermute(after(others, state_part), "mp", swap)
    others_three = lax.ppermute(after(others_two, state_part), "mp", swap)
    parts = [across(after(part, state_part) if tile > 4 else part, tile, dp_count) for tile, part in enumerate(parts)]
    prepared = prepare(
        after(own_mp, *[parts[tile] for tile in (1, 2, 3, 4)]), [others, others_one, others_two, others_three],
        layers, other_rows, rows, float(all_rows),
    )
    hidden, vectors, out_weight = prepared[:3]
    if single:
        targets = prepared[3]

    running, back, made_of = None, {}, {}
    for tiles in (NEAR, FAR_ONE, FAR_TWO):
        made = critic(
            own_dp, key_row, targets, state_part, hidden, vectors, out_weight,
            [parts[t] for t in tiles], tiles, running, tiles == FAR_TWO,
        )
        running = (made[-2], made[-1], made[len(tiles)])
        made_of.update(zip(tiles, made))
        if tiles == FAR_ONE:
            for tile in FAR_ONE:
                back[tile] = across(after(made_of[tile], made_of[FAR_ONE[0]], *[parts[u] for u in FAR_TWO]), tile, dp_count)
    for tile in FAR_TWO:
        back[tile] = across(after(made_of[tile], *[back[u] for u in FAR_ONE]), tile, dp_count)
    first, rest = made[-2], made[-1]

    state_made = state_weight_grad(core_bit, key_row, first, states, rest, single)

    for tile in NEAR:
        back[tile] = across(after(made_of[tile], state_made[0]), tile, dp_count)

    early = NEAR + FAR_ONE
    if single:
        kept, sent = state_made[1:]
        sent = after(sent, *[back[t] for t in FAR_ONE])
        states_kept, sent = fold(kept, swap_bit(sent, CORE, dp_count, mp_count), (number >> Y) & 1)
        states_got = swap_bit(sent, Y, dp_count, mp_count)
        grad_states = state_grad(own_dp, after(state_made[0], states_kept), state_weight)
        back[0] = after(back[0], grad_states)
    grad_goals, running_sum = goal_backward(
        own_tile, core_bit, [back[t] for t in early], goals, goal_weight, early, True, True
    )
    if single:
        states_got = after(states_got, running_sum)
        block = call(
            round_kernel, "round", (1,), own_dp[None], [whole(states_kept.shape)] * 2, [whole(states_kept.shape)],
            [like(*states_kept.shape, BF)], [states_kept, states_got],
        )[0]
        running_sum = after(running_sum, block)
    goal_made = goal_backward(
        own_tile, core_bit, [back[t] for t in FAR_TWO], goals, goal_weight, FAR_TWO, False, True,
        running_sum, single,
    )

    share = units // (dp_count * mp_count)
    if single:
        goals_kept, goals_sent = goal_made
        goals_got = swap_bit(goals_sent, CORE, dp_count, mp_count)
        goals_kept, goals_sent = fold(goals_kept, goals_got, (number >> Y) & 1)
        goals_got = swap_bit(goals_sent, Y, dp_count, mp_count)
        grad_goals = goal_backward(
            own_tile, core_bit, [after(back[t], goals_kept) for t in FAR_TWO], goals, goal_weight, FAR_TWO, True, False,
            grad_goals,
        )[0]
        block = lax.all_to_all(block.reshape(dp_count, share, -1), "dp", 0, 0, tiled=True)
        arrived = [block.reshape(dp_count * share, -1)]
        blocks = call(
            functools.partial(spread_kernel, dp_count), "spread", (1,), own_dp[None],
            [whole(goals_kept.shape)] * 2,
            [whole((share, goal_width))] * dp_count,
            [like(share, goal_width, F32)] + [like(share, goal_width, BF)] * (dp_count - 1),
            [after(goals_kept, grad_goals), goals_got],
        )
        arrived += [blocks[0]] + [
            lax.ppermute(blocks[o], "dp", xor_pairs(dp_count, o)) for o in range(1, dp_count)
        ]
        shapes = [
            like(share, feat_width + goal_width, F32), like(layers - 1, share, units, F32),
            like(layers, share, F32), like(layers, share, F32), like(1, share, F32), like(1, 1, F32),
        ]
        first_share, hidden_share, gain_grad, shift_grad, out_grad, loss = call(
            functools.partial(finish_kernel, 0.5 / all_rows),
            "finish", (1,), core_bit[None],
            [whole(block.shape) for block in arrived],
            [whole(shape.shape) for shape in shapes],
            shapes,
            arrived,
        )
    else:
        grad_goals = goal_backward(
            own_tile, core_bit, [after(back[t], goal_made[0]) for t in FAR_TWO], goals, goal_weight, FAR_TWO, True, False,
            grad_goals,
        )[0]
        grad_states = state_grad(own_dp, state_made[0], state_weight)
        total = sum_plain(state_made[1], dp_count)
        hidden_share = total[:, feat_width : feat_width + (layers - 1) * units]
        hidden_share = hidden_share.reshape(share, layers - 1, units).transpose(1, 0, 2)
        rest = total[:, feat_width + (layers - 1) * units :]
        first_share = jnp.concatenate([total[:, :feat_width], sum_plain(goal_made[0], dp_count)], axis=1)

        count = 2 * layers + 2
        rest = (rest[:, :count] + rest[:, count : 2 * count]).T
        gain_grad, shift_grad, out_grad = rest[:layers], rest[layers : 2 * layers], rest[2 * layers]
        loss = 0.5 * rest[count - 1, 0] / all_rows
    return (
        loss.reshape(()),
        grad_states,
        grad_goals,
        first_share.T,
        hidden_share.transpose(0, 2, 1),
        gain_grad,
        shift_grad,
        out_grad.reshape(share),
    )


def solution(mesh):
    placed = (
        P(("dp", "mp"), None),
        P(("dp", "mp"), None),
        P(("dp", "mp"), None),
        P(("dp", "mp")),
        P("mp", None),
        P(None, "mp", None),
        P(None, "mp"),
        P(None, "mp"),
        P("mp"),
    )
    return jax.shard_map(
        shards,
        mesh=mesh,
        in_specs=placed,
        out_specs=(
            P(),
            P(("dp", "mp"), None),
            P(("dp", "mp"), None),
            P(None, ("dp", "mp")),
            P(None, None, ("dp", "mp")),
            P(None, ("dp", "mp")),
            P(None, ("dp", "mp")),
            P(("dp", "mp")),
        ),
        check_vma=False,
    )
```
